32 devices in a mesh: pitch: 8 (over y, x, core), span: 4 (over z).
Axes of the slice: x: 2, y: 2, z: 4, core: 2. Of those that a mesh axis runs over, the one named last changes fastest.
Arguments:
- state: float32 [5, 5, 5, 5, 16, 4, 128], P(None, None, None, None, 'pitch', 'span'), may hold values from -6 to 6
- wake_planes: float32 [5, 5, 5, 16, 4], P(None, None, None, 'pitch', 'span'), may hold values from -6 to 6
- bar_offsets: int32 [3], replicated, may hold values from 0 to 1, as said below
Outputs:
- advanced: float32 [5, 5, 5, 5, 16, 4, 128], P(None, None, None, None, 'pitch', 'span')
The draws below stay inside these ranges and needn't reach their ends.
Inputs may be any that keep to these rules, and one draw needn't show every extreme that they name: `bar_offsets`: some section has offset 1 and some section offset 0.
All inputs are finite; a program needn't handle non-finite values.
Results may differ from the reference program's by a relative error of at most 0.0001.
Values sent between devices are 32-bit elements; how exact they have to be, the bound alone decides.
No kernel may reach another device: no remote copies, remote signals or barrier semaphores. Data moves between devices by JAX's collectives and lax.ppermute only.
A program may use at most 64 MiB of HBM per device.

```python
import jax
import jax.numpy as jnp
import numpy as np
from jax import lax

VARS = 5
NODES = 5
SECTIONS = 3
EP = 2
EA = 128
EPT = 16
EST = 4


def draw_bar_offsets(key, part):
    first_key, second_key = jax.random.split(key)
    values = jax.random.randint(first_key, (SECTIONS,), 0, EP)
    which = jax.random.randint(second_key, (), 0, SECTIONS)
    values = values.at[which].set(EP - 1)
    values = values.at[(which + 1) % SECTIONS].set(0)
    return values.astype(jnp.int32)


def level_of(key, dims, shards, least, top_value):
    factor_of = 1.0
    for dim, shards_of in shards:
        heights = jax.random.uniform(jax.random.fold_in(jax.random.fold_in(key, 6), dim), (shards_of,), jnp.float32, least / len(shards), top_value / len(shards))
        factor_of = factor_of * jnp.repeat(jnp.exp(heights), dims[dim] // shards_of).reshape((-1,) + (1,) * (len(dims) - 1 - dim))
    return factor_of


def gaussian(own_key, shape, width, limit, shards=(), kind=jnp.bfloat16):
    entries = jax.random.normal(own_key, shape, jnp.float32) * width
    if len(shards) > 0:
        entries = level_of(own_key, shape, shards, -0.22, 0.18) * entries
    return jnp.clip(entries, min=-limit, max=limit).astype(kind)


def setup_inputs(seed: int = 0) -> dict:
    seeds = jax.random.split(jax.random.key(seed), 4)
    state = gaussian(seeds[0], (VARS, NODES, NODES, NODES, EPT, EST, EA), 1.0, 6.0, ((4, 8), (5, 4)), jnp.float32)
    wake_planes = gaussian(seeds[1], (VARS, NODES, NODES, EPT, EST), 1.0, 6.0, ((3, 8), (4, 4)), jnp.float32)
    bar_offsets = draw_bar_offsets(jax.random.fold_in(seeds[3], 71), 0)
    return dict(state=state, wake_planes=wake_planes, bar_offsets=bar_offsets)


MEAN_FLOW = (0.5, 0.3, 0.0)
WAVE_SPEED = (1.5, 1.3, 1.0)
ELEM_SIZE = (1.0, 0.8, 1.2)
END_WEIGHT = 0.1
TIME_STEP = 0.01
FORMS = ('ij,vjbcxyz->vibcxyz', 'ij,vajcxyz->vaicxyz', 'ij,vabjxyz->vabixyz')

def derivative_matrix():
    points = np.array([-1.0, -np.sqrt(3.0 / 7.0), 0.0, np.sqrt(3.0 / 7.0), 1.0])
    products = np.array([np.prod([points[j] - points[k] for k in range(5) if k != j]) for j in range(5)])
    matrix = np.zeros((5, 5))
    for i in range(5):
        for j in range(5):
            if i != j:
                matrix[i, j] = products[i] / (products[j] * (points[i] - points[j]))
        matrix[i, i] = sum((1.0 / (points[i] - points[k]) for k in range(5) if k != i))
    return jnp.asarray(matrix, dtype=jnp.float32)

def physical_flux(values, direction):
    mean_speed = MEAN_FLOW[direction]
    pieces = [mean_speed * values[v] for v in range(5)]
    normal_vel = values[1 + direction]
    pieces[0] = pieces[0] + normal_vel
    pieces[4] = pieces[4] + normal_vel
    pieces[1 + direction] = pieces[1 + direction] + values[4]
    return jnp.stack(pieces)

def interface_flux(left_state, right_state, direction):
    both_sides = physical_flux(left_state, direction) + physical_flux(right_state, direction)
    return 0.5 * both_sides - 0.5 * WAVE_SPEED[direction] * (right_state - left_state)

def volume_term(state, matrix):
    tendency = None
    for direction in range(3):
        derived = jnp.einsum(FORMS[direction], matrix, physical_flux(state, direction), precision=lax.Precision.HIGHEST)
        term = -(2.0 / ELEM_SIZE[direction]) * derived
        tendency = term if direction == 0 else tendency + term
    return tendency

def face_traces(state, direction):
    upper_trace = lax.index_in_dim(state, 4, 1 + direction, keepdims=False)
    lower_trace = lax.index_in_dim(state, 0, 1 + direction, keepdims=False)
    return (upper_trace, lower_trace)

def add_faces(tendency, upper_trace, lower_trace, upper_flux, lower_flux, direction):
    factor = 2.0 / (ELEM_SIZE[direction] * END_WEIGHT)
    lift_upper = factor * (physical_flux(upper_trace, direction) - upper_flux)
    lift_lower = factor * (lower_flux - physical_flux(lower_trace, direction))
    leading = (slice(None),) * (1 + direction)
    tendency = tendency.at[leading + (4,)].add(lift_upper)
    return tendency.at[leading + (0,)].add(lift_lower)

def tendency_of(state, matrix, inlet):
    tendency = volume_term(state, matrix)
    upper_trace, lower_trace = face_traces(state, 0)
    count = upper_trace.shape[5]
    next_trace = jnp.concatenate([lax.slice_in_dim(lower_trace, 1, count, axis=5), lax.slice_in_dim(upper_trace, count - 1, count, axis=5)], axis=5)
    prev_trace = jnp.concatenate([inlet[..., None], lax.slice_in_dim(upper_trace, 0, count - 1, axis=5)], axis=5)
    tendency = add_faces(tendency, upper_trace, lower_trace, interface_flux(upper_trace, next_trace, 0), interface_flux(prev_trace, lower_trace, 0), 0)
    upper_trace, lower_trace = face_traces(state, 1)
    next_trace = jnp.roll(lower_trace, -1, axis=3)
    prev_trace = jnp.roll(upper_trace, 1, axis=3)
    tendency = add_faces(tendency, upper_trace, lower_trace, interface_flux(upper_trace, next_trace, 1), interface_flux(prev_trace, lower_trace, 1), 1)
    upper_trace, lower_trace = face_traces(state, 2)
    count = upper_trace.shape[4]
    empty = jnp.zeros_like(lax.slice_in_dim(lower_trace, 0, 1, axis=4))
    next_trace = jnp.concatenate([lax.slice_in_dim(lower_trace, 1, count, axis=4), empty], axis=4)
    prev_trace = jnp.concatenate([empty, lax.slice_in_dim(upper_trace, 0, count - 1, axis=4)], axis=4)
    tendency = add_faces(tendency, upper_trace, lower_trace, interface_flux(upper_trace, next_trace, 2), interface_flux(prev_trace, lower_trace, 2), 2)
    return tendency

def reference(state, wake_planes, bar_offsets):
    matrix = derivative_matrix()
    blocks = EPT // EP
    heads = wake_planes.shape[:3]

    def inlet_for(section_idx):
        grouped = wake_planes.reshape(heads + (blocks, EP, EST))
        grouped = jnp.roll(grouped, section_idx + 1, axis=3)
        grouped = jnp.roll(grouped, bar_offsets[section_idx], axis=4)
        return grouped.reshape(heads + (EPT, EST))
    first = state + TIME_STEP * tendency_of(state, matrix, inlet_for(0))
    second = 0.75 * state + 0.25 * (first + TIME_STEP * tendency_of(first, matrix, inlet_for(1)))
    return 1.0 / 3.0 * state + 2.0 / 3.0 * (second + TIME_STEP * tendency_of(second, matrix, inlet_for(2)))
```

```python
import functools

import jax
import jax.numpy as jnp
import ml_dtypes
import numpy as np
from jax import lax
from jax.experimental import pallas as pl
from jax.experimental.pallas import tpu as pltpu
from jax.sharding import PartitionSpec as P

MEAN_FLOW = (0.5, 0.3, 0.0)
WAVE_SPEED = (1.5, 1.3, 1.0)
ELEM_SIZE = (1.0, 0.8, 1.2)
END_WEIGHT = 0.1
TIME_STEP = 0.01
KEEP = (0.0, 0.75, 1.0 / 3.0)
GAIN = (1.0, 0.25, 2.0 / 3.0)

PLANE = 32
PER_VAR = 144
ROWS = 5 * PER_VAR
BLOCK = 128
SPAN_ROWS = 104
TRACES = 4 * BLOCK
HALO = 5 * BLOCK
WAKE_ROW = 125
LANES = 128
VMEM_LIMIT = 24 * 1024 * 1024


def derivative_table():
    points = np.array([-1.0, -np.sqrt(3.0 / 7.0), 0.0, np.sqrt(3.0 / 7.0), 1.0])
    products = np.array(
        [np.prod([points[j] - points[k] for k in range(5) if k != j]) for j in range(5)]
    )
    matrix = np.zeros((5, 5))
    for i in range(5):
        for j in range(5):
            if i != j:
                matrix[i, j] = products[i] / (products[j] * (points[i] - points[j]))
        matrix[i, i] = sum((1.0 / (points[i] - points[k]) for k in range(5) if k != i))
    return matrix


def flux_matrix(direction):
    flux = MEAN_FLOW[direction] * np.eye(5)
    flux[0, 1 + direction] += 1.0
    flux[4, 1 + direction] += 1.0
    flux[1 + direction, 4] += 1.0
    return flux


def half_flux(direction, sign):
    return 0.5 * (flux_matrix(direction) + sign * WAVE_SPEED[direction] * np.eye(5))


def lift_factor(direction):
    return TIME_STEP * 2.0 / (ELEM_SIZE[direction] * END_WEIGHT)


def node_row(v, a, p, s):
    start = {0: 0, 4: PLANE}.get(a, 2 * PLANE + (a - 1) * 25)
    return v * PER_VAR + start + p * 5 + s


def operator_tables():
    deriv = derivative_table()
    volume = np.zeros((ROWS, ROWS))
    lift = np.zeros((ROWS, HALO))
    trace = np.zeros((TRACES, ROWS))
    fluxes = [flux_matrix(d) for d in range(3)]
    plus = [half_flux(d, 1.0) for d in range(3)]
    minus = [half_flux(d, -1.0) for d in range(3)]
    plus_sent, minus_sent = (plus[2][:4], minus[2][:4])
    back_plus = np.vstack([np.eye(4), [[0.0, 0.0, 0.0, 1.0]]])
    back_minus = np.vstack([np.eye(4), [[0.0, 0.0, 0.0, -1.0]]])
    assert np.allclose(back_plus @ plus_sent, plus[2])
    assert np.allclose(back_minus @ minus_sent, minus[2])
    for a in range(5):
        for p in range(5):
            for s in range(5):
                here = [node_row(v, a, p, s) for v in range(5)]
                place = (a, p, s)
                for d in range(3):
                    for j in range(5):
                        there = list(place)
                        there[d] = j
                        cols = [node_row(v, *there) for v in range(5)]
                        coeff = -TIME_STEP * (2.0 / ELEM_SIZE[d]) * deriv[place[d], j]
                        volume[np.ix_(here, cols)] += coeff * fluxes[d]
                for d in (1, 2):
                    if place[d] == 4:
                        volume[np.ix_(here, here)] += lift_factor(d) * minus[d]
                    if place[d] == 0:
                        volume[np.ix_(here, here)] -= lift_factor(d) * plus[d]
                if p == 0:
                    cols = [v * 25 + a * 5 + s for v in range(5)]
                    lift[np.ix_(here, cols)] += lift_factor(1) * plus[1]
                    for v in range(5):
                        trace[BLOCK + v * 25 + a * 5 + s, here[v]] = 1.0
                if p == 4:
                    cols = [BLOCK + v * 25 + a * 5 + s for v in range(5)]
                    lift[np.ix_(here, cols)] -= lift_factor(1) * minus[1]
                    for v in range(5):
                        trace[v * 25 + a * 5 + s, here[v]] = 1.0
                if s == 0:
                    cols = [2 * BLOCK + c * 25 + a * 5 + p for c in range(4)]
                    lift[np.ix_(here, cols)] += lift_factor(2) * back_plus
                    rows = [3 * BLOCK + c * 25 + a * 5 + p for c in range(4)]
                    trace[np.ix_(rows, here)] += minus_sent
                if s == 4:
                    cols = [3 * BLOCK + c * 25 + a * 5 + p for c in range(4)]
                    lift[np.ix_(here, cols)] -= lift_factor(2) * back_minus
                    rows = [2 * BLOCK + c * 25 + a * 5 + p for c in range(4)]
                    trace[np.ix_(rows, here)] += plus_sent
                if a == 0:
                    cols = [4 * BLOCK + v * 25 + p * 5 + s for v in range(5)]
                    lift[np.ix_(here, cols)] += lift_factor(0) * plus[0]
    return volume, lift, trace, trace @ lift


def split_table(table):
    high = table.astype(ml_dtypes.bfloat16)
    low = (table - high.astype(np.float64)).astype(ml_dtypes.bfloat16)
    return high, low


def split(values):
    high = values.astype(jnp.bfloat16)
    low = (values - high.astype(jnp.float32)).astype(jnp.bfloat16)
    return high, low


def product(high, low, values_high, values_low):
    dot = functools.partial(jnp.dot, preferred_element_type=jnp.float32)
    total = dot(high, values_high) + dot(high, values_low)
    return total if low is None else total + dot(low, values_high)


def emit_faces(traces, wake, pitch_odd, span_odd, outs):
    pitch_a, pitch_b, span_a, span_b, inner = outs
    upper, lower = traces[0:BLOCK], traces[BLOCK : 2 * BLOCK]
    rows = lax.broadcasted_iota(jnp.int32, (BLOCK, LANES), 0)
    up = upper[:, LANES:]
    for k in range(2):
        up = jnp.where(rows == WAKE_ROW + k, wake[k : k + 1], up)
    down = lower[:, :LANES]
    pitch_a[...] = jnp.where(pitch_odd, down, up)
    pitch_b[...] = jnp.where(pitch_odd, up, down)
    inner[0:BLOCK] = upper[:, :LANES]
    inner[BLOCK:] = lower[:, LANES:]
    above = traces[2 * BLOCK : 2 * BLOCK + SPAN_ROWS]
    below = traces[3 * BLOCK : 3 * BLOCK + SPAN_ROWS]
    span_a[...] = jnp.where(span_odd, below, above)
    span_b[...] = jnp.where(span_odd, above, below)


def parities():
    return lax.axis_index("pitch") % 2 == 1, lax.axis_index("span") % 2 == 1


def begin_kernel(x, wake, trace, state, pitch_a, pitch_b, span_a, span_b, inner):
    for e in range(2):
        lanes = slice(e * LANES, (e + 1) * LANES)
        for v in range(5):
            base = v * PER_VAR
            first = v * 250 + e
            for start, count, room, at in (
                (first, 25, PLANE, base),
                (first + 200, 25, PLANE, base + PLANE),
                (first + 50, 75, 80, base + 2 * PLANE),
            ):
                state[at + room - 8 : at + room, lanes] = jnp.zeros((8, LANES), jnp.float32)
                state[at : at + count, lanes] = x[pl.ds(start, count, stride=2), :]
    planes = wake[...]
    rows = lax.broadcasted_iota(jnp.int32, (50, LANES), 0)
    cols = lax.broadcasted_iota(jnp.int32, (50, LANES), 1)
    spread = jnp.zeros((50, LANES), jnp.float32)
    for s in range(5):
        mine = (cols - s) == 5 * (rows // 2)
        spread = jnp.where(mine, planes[:, s : s + 1], spread)
    own = [
        jnp.sum(jnp.where(rows % 2 == k, spread, 0.0), axis=0, keepdims=True) for k in range(2)
    ]
    traces = product(trace[...], None, *split(state[...]))
    pitch_odd, span_odd = parities()
    emit_faces(
        traces,
        jnp.concatenate(own, axis=0),
        pitch_odd,
        span_odd,
        (pitch_a, pitch_b, span_a, span_b, inner),
    )


def axial_terms(state):
    lanes = lax.broadcasted_iota(jnp.int32, (PLANE, LANES), 1)
    upper_parts, lower_parts = ([], [])
    for e in range(2):
        own = slice(e * LANES, (e + 1) * LANES)
        upper_gap, lower_gap = ([], [])
        for v in range(5):
            base = v * PER_VAR
            lower = state[base : base + PLANE, own]
            upper = state[base + PLANE : base + 2 * PLANE, own]
            after = jnp.where(lanes == LANES - 1, upper, pltpu.roll(lower, LANES - 1, 1))
            before = jnp.where(lanes == 0, 0.0, pltpu.roll(upper, 1, 1))
            upper_gap.append(upper - after)
            lower_gap.append(before - lower)
        mixed = []
        for gap, sign in ((upper_gap, -1.0), (lower_gap, 1.0)):
            table = lift_factor(0) * half_flux(0, sign)
            mixed.append(
                [
                    sum(float(table[i, j]) * gap[j] for j in range(5) if table[i, j] != 0.0)
                    for i in range(5)
                ]
            )
        upper_parts.append(mixed[0])
        lower_parts.append(mixed[1])
    return upper_parts, lower_parts


def advance_body(section, base, state, volume_high, volume_low, trace, partial, faces):
    rate = product(volume_high[...], volume_low[...], *split(state[...]))
    gain, keep = GAIN[section], KEEP[section]
    if keep == 0.0:
        partial[...] = state[...] + rate
    else:
        partial[...] = keep * base[...] + gain * (state[...] + rate)
    upper_parts, lower_parts = axial_terms(state)
    for e in range(2):
        lanes = slice(e * LANES, (e + 1) * LANES)
        for v in range(5):
            at = v * PER_VAR
            partial[at : at + PLANE, lanes] += gain * lower_parts[e][v]
            partial[at + PLANE : at + 2 * PLANE, lanes] += gain * upper_parts[e][v]
    faces[...] = product(trace[...], None, *split(partial[...]))


def first_kernel(state, volume_high, volume_low, trace, partial, faces):
    advance_body(0, None, state, volume_high, volume_low, trace, partial, faces)


def later_kernel(
    section, base, before, halo_high, halo_low, lift_high, lift_low, volume_high, volume_low,
    trace, partial, faces, state,
):
    lifted = product(lift_high[...], lift_low[...], halo_high[...], halo_low[...])
    state[...] = before[...] + GAIN[section - 1] * lifted
    advance_body(section, base, state, volume_high, volume_low, trace, partial, faces)


def gather_halo(section, offsets, pitch_a, pitch_b, span_a, span_b, inner, halo):
    pitch_odd, span_odd = parities()
    after = jnp.where(pitch_odd, pitch_b[...], pitch_a[...])
    before = jnp.where(pitch_odd, pitch_a[...], pitch_b[...])
    halo[0:BLOCK, :LANES] = before
    halo[0:BLOCK, LANES:] = inner[0:BLOCK]
    halo[BLOCK : 2 * BLOCK, :LANES] = inner[BLOCK:]
    halo[BLOCK : 2 * BLOCK, LANES:] = after
    above = jnp.where(span_odd, span_b[...], span_a[...])
    below = jnp.where(span_odd, span_a[...], span_b[...])
    rest = jnp.zeros((BLOCK - SPAN_ROWS, 2 * LANES), jnp.float32)
    halo[2 * BLOCK : 2 * BLOCK + SPAN_ROWS] = below
    halo[2 * BLOCK + SPAN_ROWS : 3 * BLOCK] = rest
    halo[3 * BLOCK : 3 * BLOCK + SPAN_ROWS] = above
    halo[3 * BLOCK + SPAN_ROWS : 4 * BLOCK] = rest
    wake = before[WAKE_ROW : WAKE_ROW + 2]
    moved = offsets[section] % 2 == 1
    rows = lax.broadcasted_iota(jnp.int32, (BLOCK, LANES), 0)
    cols = lax.broadcasted_iota(jnp.int32, (BLOCK, LANES), 1)
    for e in range(2):
        row = jnp.where(moved, wake[1 - e : 2 - e], wake[e : e + 1])
        column = jnp.sum(jnp.where(rows == cols, row, 0.0), axis=1, keepdims=True)
        halo[4 * BLOCK :, e * LANES : (e + 1) * LANES] = jnp.where(cols == 0, column, 0.0)
    return wake


def exchange_kernel(
    section, offsets, pitch_a, pitch_b, span_a, span_b, inner, faces, link_high, link_low,
    next_pitch_a, next_pitch_b, next_span_a, next_span_b, next_inner, halo_high, halo_low, halo,
):
    wake = gather_halo(section, offsets, pitch_a, pitch_b, span_a, span_b, inner, halo)
    high, low = split(halo[...])
    halo_high[...] = high
    halo_low[...] = low
    traces = faces[...] + GAIN[section] * product(link_high[...], link_low[...], high, low)
    pitch_odd, span_odd = parities()
    emit_faces(
        traces,
        wake,
        pitch_odd,
        span_odd,
        (next_pitch_a, next_pitch_b, next_span_a, next_span_b, next_inner),
    )


def final_kernel(
    offsets, pitch_a, pitch_b, span_a, span_b, inner, before, lift_high, lift_low, out, halo
):
    gather_halo(2, offsets, pitch_a, pitch_b, span_a, span_b, inner, halo)
    high, low = split(halo[...])
    lifted = product(lift_high[...], lift_low[...], high, low)
    result = before[...] + GAIN[2] * lifted
    for e in range(2):
        lanes = slice(e * LANES, (e + 1) * LANES)
        for v in range(5):
            base = v * PER_VAR
            first = v * 250 + e
            out[pl.ds(first, 25, stride=2), :] = result[base : base + 25, lanes]
            out[pl.ds(first + 200, 25, stride=2), :] = result[base + PLANE : base + PLANE + 25, lanes]
            at = base + 2 * PLANE
            out[pl.ds(first + 50, 75, stride=2), :] = result[at : at + 75, lanes]


IN_VMEM = pl.BlockSpec(memory_space=pltpu.VMEM)
IN_SMEM = pl.BlockSpec(memory_space=pltpu.SMEM)


def call(kernel, name, outs, args, scalars=0, scratch=(), flops=0):
    return pl.pallas_call(
        kernel,
        name=name,
        out_shape=[jax.ShapeDtypeStruct(shape, dtype) for shape, dtype in outs],
        in_specs=[IN_SMEM] * scalars + [IN_VMEM] * (len(args) - scalars),
        out_specs=[IN_VMEM] * len(outs),
        scratch_shapes=list(scratch),
        compiler_params=pltpu.CompilerParams(vmem_limit_bytes=VMEM_LIMIT),
        cost_estimate=pl.CostEstimate(flops=flops, bytes_accessed=2**20, transcendentals=0),
    )(*args)


def swapped(value, axis, odd, wrap):
    size = lax.axis_size(axis)
    pairs = []
    for i in range(odd, size if wrap else size - 1, 2):
        j = (i + 1) % size
        pairs += [(i, j), (j, i)]
    return lax.ppermute(value, axis, pairs)


def exchanged(faces):
    pitch_a, pitch_b, span_a, span_b, inner = faces
    return (
        swapped(pitch_a, "pitch", 0, True),
        swapped(pitch_b, "pitch", 1, True),
        swapped(span_a, "span", 0, False),
        swapped(span_b, "span", 1, False),
        inner,
    )


F32 = jnp.float32
FACE_OUTS = [
    ((BLOCK, LANES), F32),
    ((BLOCK, LANES), F32),
    ((SPAN_ROWS, 2 * LANES), F32),
    ((SPAN_ROWS, 2 * LANES), F32),
    ((2 * BLOCK, LANES), F32),
]
HALO_OUTS = [((HALO, 2 * LANES), jnp.bfloat16)] * 2
PARTIAL_OUTS = [((ROWS, 2 * LANES), F32), ((TRACES, 2 * LANES), F32)]


def shards(tables, state, wake_planes, bar_offsets):
    volume, lift, trace, link = tables
    x = state.reshape(-1, LANES)
    wake = wake_planes.transpose(0, 1, 3, 4, 2).reshape(50, 5)
    base, *faces = call(
        begin_kernel, "begin", [((ROWS, 2 * LANES), F32)] + FACE_OUTS, [x, wake, trace], flops=10**8
    )
    arrived = exchanged(faces)
    partial, traces = call(
        first_kernel, "first", PARTIAL_OUTS, [base, *volume, trace], flops=2 * 10**9
    )
    for section in range(2):
        *faces, high, low = call(
            functools.partial(exchange_kernel, section),
            "exchange",
            FACE_OUTS + HALO_OUTS,
            [bar_offsets, *arrived, traces, *link],
            scalars=1,
            scratch=[pltpu.VMEM((HALO, 2 * LANES), F32)],
            flops=10**8,
        )
        arrived = exchanged(faces)
        partial, traces = call(
            functools.partial(later_kernel, section + 1),
            "later",
            PARTIAL_OUTS,
            [base, partial, high, low, *lift, *volume, trace],
            scratch=[pltpu.VMEM((ROWS, 2 * LANES), F32)],
            flops=3 * 10**9,
        )
    (out,) = call(
        final_kernel,
        "final",
        [(x.shape, F32)],
        [bar_offsets, *arrived, partial, *lift],
        scalars=1,
        scratch=[pltpu.VMEM((HALO, 2 * LANES), F32)],
        flops=10**8,
    )
    return out.reshape(state.shape)


def solution(mesh):
    volume, lift, trace, link = operator_tables()
    tables = (
        split_table(volume),
        split_table(lift),
        trace.astype(ml_dtypes.bfloat16),
        split_table(link),
    )
    tables = jax.tree.map(jnp.asarray, tables)
    in_specs = (
        P(None, None, None, None, "pitch", "span", None),
        P(None, None, None, "pitch", "span"),
        P(),
    )
    out_specs = P(None, None, None, None, "pitch", "span", None)
    return jax.shard_map(
        functools.partial(shards, tables),
        mesh=mesh,
        in_specs=in_specs,
        out_specs=out_specs,
        check_vma=False,
    )
```

```python
import functools

import jax
import jax.numpy as jnp
import ml_dtypes
import numpy as np
from jax import lax
from jax.experimental import pallas as pl
from jax.experimental.pallas import tpu as pltpu
from jax.sharding import PartitionSpec as P

MEAN_FLOW = (0.5, 0.3, 0.0)
WAVE_SPEED = (1.5, 1.3, 1.0)
ELEM_SIZE = (1.0, 0.8, 1.2)
END_WEIGHT = 0.1
TIME_STEP = 0.01
KEEP = (0.0, 0.75, 1.0 / 3.0)
GAIN = (1.0, 0.25, 2.0 / 3.0)

ORDER = (1, 4, 2, 3, 0)
MAIN = 24
TAIL = 5 * MAIN
PER_VAR = 128
ROWS = 5 * PER_VAR
TILES = ((0, 0, 2), (1, 2, 4), (4, 4, 5))
BLOCK = 128
SPAN_ROWS = 104
TRACES = 4 * BLOCK
HALO = 5 * BLOCK
WAKE_ROW = 125
LANES = 128
VMEM_LIMIT = 24 * 1024 * 1024


def derivative_table():
    points = np.array([-1.0, -np.sqrt(3.0 / 7.0), 0.0, np.sqrt(3.0 / 7.0), 1.0])
    products = np.array(
        [np.prod([points[j] - points[k] for k in range(5) if k != j]) for j in range(5)]
    )
    matrix = np.zeros((5, 5))
    for i in range(5):
        for j in range(5):
            if i != j:
                matrix[i, j] = products[i] / (products[j] * (points[i] - points[j]))
        matrix[i, i] = sum((1.0 / (points[i] - points[k]) for k in range(5) if k != i))
    return matrix


def flux_matrix(direction):
    flux = MEAN_FLOW[direction] * np.eye(5)
    flux[0, 1 + direction] += 1.0
    flux[4, 1 + direction] += 1.0
    flux[1 + direction, 4] += 1.0
    return flux


def half_flux(direction, sign):
    return 0.5 * (flux_matrix(direction) + sign * WAVE_SPEED[direction] * np.eye(5))


def lift_factor(direction):
    return TIME_STEP * 2.0 / (ELEM_SIZE[direction] * END_WEIGHT)


def half_scales():
    return (lift_factor(1) / 10.0, lift_factor(1), lift_factor(2), lift_factor(2), lift_factor(0))


def var_start(v):
    return ORDER.index(v) * PER_VAR


def node_row(v, a, p, s):
    node = p * 5 + s
    return var_start(v) + (a * MAIN + node if node < MAIN else TAIL + a)


def operator_tables():
    deriv = derivative_table()
    volume = np.zeros((ROWS, ROWS))
    lift = np.zeros((ROWS, HALO))
    trace = np.zeros((TRACES, ROWS))
    fluxes = [flux_matrix(d) for d in range(3)]
    plus = [half_flux(d, 1.0) for d in range(3)]
    minus = [half_flux(d, -1.0) for d in range(3)]
    plus_sent, minus_sent = (plus[2][:4], minus[2][:4])
    back_plus = np.vstack([np.eye(4), [[0.0, 0.0, 0.0, 1.0]]])
    back_minus = np.vstack([np.eye(4), [[0.0, 0.0, 0.0, -1.0]]])
    assert np.allclose(back_plus @ plus_sent, plus[2])
    assert np.allclose(back_minus @ minus_sent, minus[2])
    for a in range(5):
        for p in range(5):
            for s in range(5):
                here = [node_row(v, a, p, s) for v in range(5)]
                place = (a, p, s)
                for d in range(3):
                    for j in range(5):
                        there = list(place)
                        there[d] = j
                        cols = [node_row(v, *there) for v in range(5)]
                        coeff = -TIME_STEP * (2.0 / ELEM_SIZE[d]) * deriv[place[d], j]
                        volume[np.ix_(here, cols)] += coeff * fluxes[d]
                for d in (1, 2):
                    if place[d] == 4:
                        volume[np.ix_(here, here)] += lift_factor(d) * minus[d]
                    if place[d] == 0:
                        volume[np.ix_(here, here)] -= lift_factor(d) * plus[d]
                if p == 0:
                    cols = [v * 25 + a * 5 + s for v in range(5)]
                    lift[np.ix_(here, cols)] += lift_factor(1) * plus[1]
                    for v in range(5):
                        trace[BLOCK + v * 25 + a * 5 + s, here[v]] = 1.0
                if p == 4:
                    cols = [BLOCK + v * 25 + a * 5 + s for v in range(5)]
                    lift[np.ix_(here, cols)] -= lift_factor(1) * minus[1]
                    for v in range(5):
                        trace[v * 25 + a * 5 + s, here[v]] = 1.0
                if s == 0:
                    cols = [2 * BLOCK + c * 25 + a * 5 + p for c in range(4)]
                    lift[np.ix_(here, cols)] += lift_factor(2) * back_plus
                    rows = [3 * BLOCK + c * 25 + a * 5 + p for c in range(4)]
                    trace[np.ix_(rows, here)] += minus_sent
                if s == 4:
                    cols = [3 * BLOCK + c * 25 + a * 5 + p for c in range(4)]
                    lift[np.ix_(here, cols)] -= lift_factor(2) * back_minus
                    rows = [2 * BLOCK + c * 25 + a * 5 + p for c in range(4)]
                    trace[np.ix_(rows, here)] += plus_sent
                if a == 0:
                    cols = [4 * BLOCK + v * 25 + p * 5 + s for v in range(5)]
                    lift[np.ix_(here, cols)] += lift_factor(0) * plus[0]
    lift = lift / np.repeat(half_scales(), BLOCK)
    return volume, lift, trace, trace @ lift


def exact_table(table):
    exact = table.astype(ml_dtypes.bfloat16)
    assert np.allclose(exact.astype(np.float64), table, rtol=1e-12, atol=1e-12)
    return exact


def split_table(table):
    high = table.astype(ml_dtypes.bfloat16)
    low = (table - high.astype(np.float64)).astype(ml_dtypes.bfloat16)
    return high, low


def split(values):
    high = values.astype(jnp.bfloat16)
    low = (values - high.astype(jnp.float32)).astype(jnp.bfloat16)
    return high, low


def dot(left, right):
    return jnp.dot(left, right, preferred_element_type=jnp.float32)


def product(table, high, low):
    return dot(table, high) + dot(table, low)


def emit_faces(traces, wake, pitch_odd, span_odd, outs):
    pitch_a, pitch_b, span_a, span_b, inner = outs
    upper, lower = traces[0:BLOCK], traces[BLOCK : 2 * BLOCK]
    rows = lax.broadcasted_iota(jnp.int32, (BLOCK, LANES), 0)
    up = upper[:, LANES:]
    for k in range(2):
        up = jnp.where(rows == WAKE_ROW + k, wake[k : k + 1], up)
    down = lower[:, :LANES]
    pitch_a[...] = jnp.where(pitch_odd, down, up)
    pitch_b[...] = jnp.where(pitch_odd, up, down)
    inner[0:BLOCK] = upper[:, :LANES]
    inner[BLOCK:] = lower[:, LANES:]
    above = traces[2 * BLOCK : 2 * BLOCK + SPAN_ROWS]
    below = traces[3 * BLOCK : 3 * BLOCK + SPAN_ROWS]
    span_a[...] = jnp.where(span_odd, below, above)
    span_b[...] = jnp.where(span_odd, above, below)


def parities():
    return lax.axis_index("pitch") % 2 == 1, lax.axis_index("span") % 2 == 1


def begin_kernel(x, wake, trace, state, pitch_a, pitch_b, span_a, span_b, inner):
    flat = x.reshape(x.shape[0], LANES)
    for e in range(2):
        lanes = slice(e * LANES, (e + 1) * LANES)
        for v in range(5):
            base = var_start(v)
            first = v * 250 + e
            for a in range(5):
                at = base + a * MAIN
                state[at : at + MAIN, lanes] = flat[pl.ds(first + a * 50, MAIN, stride=2), :]
            tail = base + TAIL
            state[tail : tail + 8, lanes] = jnp.zeros((8, LANES), jnp.float32)
            state[tail : tail + 5, lanes] = flat[pl.ds(first + 2 * MAIN, 5, stride=50), :]
    planes = wake[...]
    rows = lax.broadcasted_iota(jnp.int32, (50, LANES), 0)
    cols = lax.broadcasted_iota(jnp.int32, (50, LANES), 1)
    spread = jnp.zeros((50, LANES), jnp.float32)
    for s in range(5):
        mine = (cols - s) == 5 * (rows // 2)
        spread = jnp.where(mine, planes[:, s : s + 1], spread)
    own = [
        jnp.sum(jnp.where(rows % 2 == k, spread, 0.0), axis=0, keepdims=True) for k in range(2)
    ]
    traces = product(trace[...], *split(state[...]))
    pitch_odd, span_odd = parities()
    emit_faces(
        traces,
        jnp.concatenate(own, axis=0),
        pitch_odd,
        span_odd,
        (pitch_a, pitch_b, span_a, span_b, inner),
    )


def add_axial_terms(gain, state, partial):
    lanes = lax.broadcasted_iota(jnp.int32, (MAIN + 8, LANES), 1)
    rows = lax.broadcasted_iota(jnp.int32, (8, LANES), 0)
    for e in range(2):
        own = slice(e * LANES, (e + 1) * LANES)
        upper_gap, lower_gap = ([], [])
        for v in range(5):
            base = var_start(v)
            lower = state[base : base + MAIN, own]
            upper = state[base + 4 * MAIN : base + TAIL, own]
            tail = state[base + TAIL : base + PER_VAR, own]
            turned = pltpu.roll(tail, 4, 0)
            join = lambda main, end: jnp.concatenate([main, end], axis=0)
            after = pltpu.roll(join(lower, turned), LANES - 1, 1)
            before = pltpu.roll(join(upper, turned), 1, 1)
            upper = join(upper, tail)
            upper_gap.append(jnp.where(lanes == LANES - 1, 0.0, upper - after))
            lower_gap.append(jnp.where(lanes == 0, 0.0, before) - join(lower, tail))
        mixed = []
        for gap, sign in ((upper_gap, -1.0), (lower_gap, 1.0)):
            table = gain * lift_factor(0) * half_flux(0, sign)
            mixed.append(
                [
                    sum(float(table[i, j]) * gap[j] for j in range(5) if table[i, j] != 0.0)
                    for i in range(5)
                ]
            )
        for v in range(5):
            base = var_start(v)
            upper, lower = (mixed[0][v], mixed[1][v])
            partial[base : base + MAIN, own] += lower[:MAIN]
            partial[base + 4 * MAIN : base + TAIL, own] += upper[:MAIN]
            ends = jnp.where(rows == 0, lower[MAIN:], jnp.where(rows == 4, upper[MAIN:], 0.0))
            partial[base + TAIL : base + PER_VAR, own] += ends


def volume_rate(tables, high, low):
    rate = [None] * 5
    for (first, start, stop), table_high, table_low in zip(TILES, tables[:3], tables[3:]):
        part = slice(start * PER_VAR, stop * PER_VAR)
        term = product(table_high[...], high[part], low[part]) + dot(table_low[...], high[part])
        for v in range(first, 5):
            block = term[(v - first) * PER_VAR : (v - first + 1) * PER_VAR]
            rate[v] = block if rate[v] is None else rate[v] + block
    return jnp.concatenate(rate, axis=0)


def advance_body(section, base, state, volume, partial):
    rate = volume_rate(volume, *split(state[...]))
    gain, keep = GAIN[section], KEEP[section]
    if keep == 0.0:
        partial[...] = state[...] + rate
    else:
        partial[...] = keep * base[...] + gain * (state[...] + rate)
    add_axial_terms(gain, state, partial)


def first_kernel(state, trace, *refs):
    *volume, partial, faces = refs
    advance_body(0, None, state, volume, partial)
    faces[...] = product(trace[...], *split(partial[...]))


def later_kernel(section, base, before, halo_high, halo_low, lift, trace, *refs):
    *volume, partial, faces, state = refs
    state[...] = before[...] + GAIN[section - 1] * product(lift[...], halo_high[...], halo_low[...])
    advance_body(section, base, state, volume, partial)
    faces[...] = product(trace[...], *split(partial[...]))


def last_kernel(section, base, before, halo_high, halo_low, lift, *refs):
    *volume, partial, state = refs
    state[...] = before[...] + GAIN[section - 1] * product(lift[...], halo_high[...], halo_low[...])
    advance_body(section, base, state, volume, partial)


def gather_halo(section, offsets, pitch_a, pitch_b, span_a, span_b, inner, halo):
    pitch_odd, span_odd = parities()
    after = jnp.where(pitch_odd, pitch_b[...], pitch_a[...])
    before = jnp.where(pitch_odd, pitch_a[...], pitch_b[...])
    scales = half_scales()
    halo[0:BLOCK, :LANES] = scales[0] * before
    halo[0:BLOCK, LANES:] = scales[0] * inner[0:BLOCK]
    halo[BLOCK : 2 * BLOCK, :LANES] = scales[1] * inner[BLOCK:]
    halo[BLOCK : 2 * BLOCK, LANES:] = scales[1] * after
    above = jnp.where(span_odd, span_b[...], span_a[...])
    below = jnp.where(span_odd, span_a[...], span_b[...])
    rest = jnp.zeros((BLOCK - SPAN_ROWS, 2 * LANES), jnp.float32)
    halo[2 * BLOCK : 2 * BLOCK + SPAN_ROWS] = scales[2] * below
    halo[2 * BLOCK + SPAN_ROWS : 3 * BLOCK] = rest
    halo[3 * BLOCK : 3 * BLOCK + SPAN_ROWS] = scales[3] * above
    halo[3 * BLOCK + SPAN_ROWS : 4 * BLOCK] = rest
    wake = before[WAKE_ROW : WAKE_ROW + 2]
    moved = offsets[section] % 2 == 1
    rows = lax.broadcasted_iota(jnp.int32, (BLOCK, LANES), 0)
    cols = lax.broadcasted_iota(jnp.int32, (BLOCK, LANES), 1)
    for e in range(2):
        row = jnp.where(moved, wake[1 - e : 2 - e], wake[e : e + 1])
        column = jnp.sum(jnp.where(rows == cols, row, 0.0), axis=1, keepdims=True)
        halo[4 * BLOCK :, e * LANES : (e + 1) * LANES] = jnp.where(
            cols == 0, scales[4] * column, 0.0
        )
    return wake


def exchange_kernel(
    section, offsets, pitch_a, pitch_b, span_a, span_b, inner, faces, link,
    next_pitch_a, next_pitch_b, next_span_a, next_span_b, next_inner, halo_high, halo_low, halo,
):
    wake = gather_halo(section, offsets, pitch_a, pitch_b, span_a, span_b, inner, halo)
    high, low = split(halo[...])
    halo_high[...] = high
    halo_low[...] = low
    traces = faces[...] + GAIN[section] * product(link[...], high, low)
    pitch_odd, span_odd = parities()
    emit_faces(
        traces,
        wake,
        pitch_odd,
        span_odd,
        (next_pitch_a, next_pitch_b, next_span_a, next_span_b, next_inner),
    )


def final_kernel(
    offsets, pitch_a, pitch_b, span_a, span_b, inner, before, lift, out, halo
):
    gather_halo(2, offsets, pitch_a, pitch_b, span_a, span_b, inner, halo)
    high, low = split(halo[...])
    result = before[...] + GAIN[2] * product(lift[...], high, low)
    flat = out.reshape(out.shape[0], LANES)
    for e in range(2):
        lanes = slice(e * LANES, (e + 1) * LANES)
        for v in range(5):
            base = var_start(v)
            first = v * 250 + e
            for a in range(5):
                at = base + a * MAIN
                flat[pl.ds(first + a * 50, MAIN, stride=2), :] = result[at : at + MAIN, lanes]
            tail = base + TAIL
            flat[pl.ds(first + 2 * MAIN, 5, stride=50), :] = result[tail : tail + 5, lanes]


IN_VMEM = pl.BlockSpec(memory_space=pltpu.VMEM)
IN_SMEM = pl.BlockSpec(memory_space=pltpu.SMEM)


def call(kernel, name, outs, args, scalars=0, scratch=(), flops=0):
    return pl.pallas_call(
        kernel,
        name=name,
        out_shape=[jax.ShapeDtypeStruct(shape, dtype) for shape, dtype in outs],
        in_specs=[IN_SMEM] * scalars + [IN_VMEM] * (len(args) - scalars),
        out_specs=[IN_VMEM] * len(outs),
        scratch_shapes=list(scratch),
        compiler_params=pltpu.CompilerParams(vmem_limit_bytes=VMEM_LIMIT),
        cost_estimate=pl.CostEstimate(flops=flops, bytes_accessed=2**20, transcendentals=0),
    )(*args)


def swapped(value, axis, odd, wrap):
    size = lax.axis_size(axis)
    pairs = []
    for i in range(odd, size if wrap else size - 1, 2):
        j = (i + 1) % size
        pairs += [(i, j), (j, i)]
    return lax.ppermute(value, axis, pairs)


def exchanged(faces):
    pitch_a, pitch_b, span_a, span_b, inner = faces
    return (
        swapped(pitch_a, "pitch", 0, True),
        swapped(pitch_b, "pitch", 1, True),
        swapped(span_a, "span", 0, False),
        swapped(span_b, "span", 1, False),
        inner,
    )


F32 = jnp.float32
FACE_OUTS = [
    ((BLOCK, LANES), F32),
    ((BLOCK, LANES), F32),
    ((SPAN_ROWS, 2 * LANES), F32),
    ((SPAN_ROWS, 2 * LANES), F32),
    ((2 * BLOCK, LANES), F32),
]
HALO_OUTS = [((HALO, 2 * LANES), jnp.bfloat16)] * 2
PARTIAL_OUTS = [((ROWS, 2 * LANES), F32), ((TRACES, 2 * LANES), F32)]


def shards(tables, state, wake_planes, bar_offsets):
    volume, lift, trace, link = tables
    x = state.reshape(-1, 1, LANES)
    wake = wake_planes.transpose(0, 1, 3, 4, 2).reshape(50, 5)
    base, *faces = call(
        begin_kernel, "begin", [((ROWS, 2 * LANES), F32)] + FACE_OUTS, [x, wake, trace], flops=10**8
    )
    arrived = exchanged(faces)
    partial, traces = call(
        first_kernel, "first", PARTIAL_OUTS, [base, trace, *volume], flops=2 * 10**9
    )
    for section in range(2):
        *faces, high, low = call(
            functools.partial(exchange_kernel, section),
            "exchange",
            FACE_OUTS + HALO_OUTS,
            [bar_offsets, *arrived, traces, link],
            scalars=1,
            scratch=[pltpu.VMEM((HALO, 2 * LANES), F32)],
            flops=10**8,
        )
        arrived = exchanged(faces)
        last = section == 1
        partial, *traces = call(
            functools.partial(last_kernel if last else later_kernel, section + 1),
            "last" if last else "later",
            PARTIAL_OUTS[:1] if last else PARTIAL_OUTS,
            [base, partial, high, low, lift] + ([] if last else [trace]) + [*volume],
            scratch=[pltpu.VMEM((ROWS, 2 * LANES), F32)],
            flops=2 * 10**9,
        )
        traces = None if last else traces[0]
    (out,) = call(
        final_kernel,
        "final",
        [(x.shape, F32)],
        [bar_offsets, *arrived, partial, lift],
        scalars=1,
        scratch=[pltpu.VMEM((HALO, 2 * LANES), F32)],
        flops=10**8,
    )
    return out.reshape(state.shape)


def solution(mesh):
    volume, lift, trace, link = operator_tables()
    blocks = []
    for first, start, stop in TILES:
        blocks.append(volume[first * PER_VAR :, start * PER_VAR : stop * PER_VAR].copy())
        volume[first * PER_VAR :, start * PER_VAR : stop * PER_VAR] = 0.0
    assert not volume.any()
    halves = [split_table(block) for block in blocks]
    tables = (
        [high for high, _ in halves] + [low for _, low in halves],
        exact_table(lift),
        exact_table(trace),
        exact_table(link),
    )
    tables = jax.tree.map(jnp.asarray, tables)
    in_specs = (
        P(None, None, None, None, "pitch", "span", None),
        P(None, None, None, "pitch", "span"),
        P(),
    )
    out_specs = P(None, None, None, None, "pitch", "span", None)
    return jax.shard_map(
        functools.partial(shards, tables),
        mesh=mesh,
        in_specs=in_specs,
        out_specs=out_specs,
        check_vma=False,
    )
```

```python
import functools

import jax
import jax.numpy as jnp
import ml_dtypes
import numpy as np
from jax import lax
from jax.experimental import pallas as pl
from jax.experimental.pallas import tpu as pltpu
from jax.sharding import PartitionSpec as P

MEAN_FLOW = (0.5, 0.3, 0.0)
WAVE_SPEED = (1.5, 1.3, 1.0)
ELEM_SIZE = (1.0, 0.8, 1.2)
END_WEIGHT = 0.1
TIME_STEP = 0.01
KEEP = (0.0, 0.75, 1.0 / 3.0)
GAIN = (1.0, 0.25, 2.0 / 3.0)

ORDER = (1, 4, 2, 3, 0)
MAIN = 24
TAIL = 5 * MAIN
PER_VAR = 128
ROWS = 5 * PER_VAR
TILES = ((0, 0, 2), (1, 2, 4), (4, 4, 5))
BLOCK = 128
SPAN_ROWS = 104
TRACES = 4 * BLOCK
HALO = 5 * BLOCK
WAKE_ROW = 125
TRACE_AT, LINK_AT, LIFT_AT = (0, TRACES, 2 * TRACES)
HIGH_AT = LIFT_AT + ROWS
LOW_AT = HIGH_AT + ROWS
TABLE_ROWS = LOW_AT + ROWS
LANES = 128
VMEM_LIMIT = 24 * 1024 * 1024


def derivative_table():
    points = np.array([-1.0, -np.sqrt(3.0 / 7.0), 0.0, np.sqrt(3.0 / 7.0), 1.0])
    products = np.array(
        [np.prod([points[j] - points[k] for k in range(5) if k != j]) for j in range(5)]
    )
    matrix = np.zeros((5, 5))
    for i in range(5):
        for j in range(5):
            if i != j:
                matrix[i, j] = products[i] / (products[j] * (points[i] - points[j]))
        matrix[i, i] = sum((1.0 / (points[i] - points[k]) for k in range(5) if k != i))
    return matrix


def flux_matrix(direction):
    flux = MEAN_FLOW[direction] * np.eye(5)
    flux[0, 1 + direction] += 1.0
    flux[4, 1 + direction] += 1.0
    flux[1 + direction, 4] += 1.0
    return flux


def half_flux(direction, sign):
    return 0.5 * (flux_matrix(direction) + sign * WAVE_SPEED[direction] * np.eye(5))


def lift_factor(direction):
    return TIME_STEP * 2.0 / (ELEM_SIZE[direction] * END_WEIGHT)


def half_scales():
    return (lift_factor(1) / 10.0, lift_factor(1), lift_factor(2), lift_factor(2), lift_factor(0))


def var_start(v):
    return ORDER.index(v) * PER_VAR


def node_row(v, a, p, s):
    node = p * 5 + s
    return var_start(v) + (a * MAIN + node if node < MAIN else TAIL + a)


def operator_tables():
    deriv = derivative_table()
    volume = np.zeros((ROWS, ROWS))
    lift = np.zeros((ROWS, HALO))
    trace = np.zeros((TRACES, ROWS))
    fluxes = [flux_matrix(d) for d in range(3)]
    plus = [half_flux(d, 1.0) for d in range(3)]
    minus = [half_flux(d, -1.0) for d in range(3)]
    plus_sent, minus_sent = (plus[2][:4], minus[2][:4])
    back_plus = np.vstack([np.eye(4), [[0.0, 0.0, 0.0, 1.0]]])
    back_minus = np.vstack([np.eye(4), [[0.0, 0.0, 0.0, -1.0]]])
    assert np.allclose(back_plus @ plus_sent, plus[2])
    assert np.allclose(back_minus @ minus_sent, minus[2])
    for a in range(5):
        for p in range(5):
            for s in range(5):
                here = [node_row(v, a, p, s) for v in range(5)]
                place = (a, p, s)
                for d in range(3):
                    for j in range(5):
                        there = list(place)
                        there[d] = j
                        cols = [node_row(v, *there) for v in range(5)]
                        coeff = -TIME_STEP * (2.0 / ELEM_SIZE[d]) * deriv[place[d], j]
                        volume[np.ix_(here, cols)] += coeff * fluxes[d]
                for d in (1, 2):
                    if place[d] == 4:
                        volume[np.ix_(here, here)] += lift_factor(d) * minus[d]
                    if place[d] == 0:
                        volume[np.ix_(here, here)] -= lift_factor(d) * plus[d]
                if p == 0:
                    cols = [s * 25 + v * 5 + a for v in range(5)]
                    lift[np.ix_(here, cols)] += lift_factor(1) * plus[1]
                    for v in range(5):
                        trace[BLOCK + s * 25 + v * 5 + a, here[v]] = 1.0
                if p == 4:
                    cols = [BLOCK + s * 25 + v * 5 + a for v in range(5)]
                    lift[np.ix_(here, cols)] -= lift_factor(1) * minus[1]
                    for v in range(5):
                        trace[s * 25 + v * 5 + a, here[v]] = 1.0
                if s == 0:
                    cols = [2 * BLOCK + c * 25 + a * 5 + p for c in range(4)]
                    lift[np.ix_(here, cols)] += lift_factor(2) * back_plus
                    rows = [3 * BLOCK + c * 25 + a * 5 + p for c in range(4)]
                    trace[np.ix_(rows, here)] += minus_sent
                if s == 4:
                    cols = [3 * BLOCK + c * 25 + a * 5 + p for c in range(4)]
                    lift[np.ix_(here, cols)] -= lift_factor(2) * back_minus
                    rows = [2 * BLOCK + c * 25 + a * 5 + p for c in range(4)]
                    trace[np.ix_(rows, here)] += plus_sent
                if a == 0:
                    cols = [4 * BLOCK + v * 25 + p * 5 + s for v in range(5)]
                    lift[np.ix_(here, cols)] += lift_factor(0) * plus[0]
    lift = lift / np.repeat(half_scales(), BLOCK)
    return volume, lift, trace, trace @ lift


def exact_table(table):
    exact = table.astype(ml_dtypes.bfloat16)
    assert np.allclose(exact.astype(np.float64), table, rtol=1e-12, atol=1e-12)
    return exact


def split_table(table):
    high = table.astype(ml_dtypes.bfloat16)
    low = (table - high.astype(np.float64)).astype(ml_dtypes.bfloat16)
    return high, low


def split(values):
    high = values.astype(jnp.bfloat16)
    low = (values - high.astype(jnp.float32)).astype(jnp.bfloat16)
    return high, low


def dot(left, right):
    return jnp.dot(left, right, preferred_element_type=jnp.float32)


def product(table, high, low):
    return dot(table, high) + dot(table, low)


def with_rows(values, first, extra):
    rows = lax.broadcasted_iota(jnp.int32, values.shape, 0)
    for k, row in enumerate(extra):
        values = jnp.where(rows == first + k, row, values)
    return values


def emit_pitch_faces(traces, wake, pitch_odd, pitch_a, pitch_b, inner):
    upper, lower = traces[0:BLOCK], traces[BLOCK : 2 * BLOCK]
    up = with_rows(upper[:, LANES:], WAKE_ROW, wake)
    down = lower[:, :LANES]
    pitch_a[...] = jnp.where(pitch_odd, down, up)
    pitch_b[...] = jnp.where(pitch_odd, up, down)
    inner[0:BLOCK] = upper[:, :LANES]
    inner[BLOCK:] = lower[:, LANES:]


def emit_span_faces(traces, span_odd, span_a, span_b):
    above, below = traces[0:SPAN_ROWS], traces[BLOCK : BLOCK + SPAN_ROWS]
    span_a[...] = jnp.where(span_odd, below, above)
    span_b[...] = jnp.where(span_odd, above, below)


def parities():
    return lax.axis_index("pitch") % 2 == 1, lax.axis_index("span") % 2 == 1


def combine(table, values):
    return [
        sum(float(table[i, j]) * values[j] for j in range(5) if table[i, j] != 0.0)
        for i in range(table.shape[0])
    ]


def begin_span_kernel(x, span_a, span_b):
    flat = x.reshape(x.shape[0], LANES)
    _, span_odd = parities()
    rest = jnp.zeros((SPAN_ROWS - 96, LANES), jnp.float32)
    for e in range(2):
        lanes = slice(e * LANES, (e + 1) * LANES)
        sides = []
        for s, sign in ((4, 1.0), (0, -1.0)):
            faces = [flat[pl.ds(v * 250 + 2 * s + e, 25, stride=10), :] for v in range(5)]
            sides.append(combine(half_flux(2, sign)[:4], faces))
        span_a[96:SPAN_ROWS, lanes] = rest
        span_b[96:SPAN_ROWS, lanes] = rest
        for c in range(4):
            above, below = (sides[0][c], sides[1][c])
            span_a[c * 25 : c * 25 + 25, lanes] = jnp.where(span_odd, below, above)
            span_b[c * 25 : c * 25 + 25, lanes] = jnp.where(span_odd, above, below)


def begin_pitch_kernel(x, wake, pitch_a, pitch_b, inner):
    flat = x.reshape(x.shape[0], LANES)
    pitch_odd, _ = parities()
    planes = wake.reshape(50, 5)[...]
    rows = lax.broadcasted_iota(jnp.int32, (50, LANES), 0)
    cols = lax.broadcasted_iota(jnp.int32, (50, LANES), 1)
    spread = jnp.zeros((50, LANES), jnp.float32)
    for s in range(5):
        mine = (cols - s) == 5 * (rows // 2)
        spread = jnp.where(mine, planes[:, s : s + 1], spread)
    own = [
        jnp.sum(jnp.where(rows % 2 == k, spread, 0.0), axis=0, keepdims=True) for k in range(2)
    ]
    tail = jnp.zeros((8, LANES), jnp.float32)
    up_tail = with_rows(tail, WAKE_ROW - 120, own)
    pitch_a[120:BLOCK] = jnp.where(pitch_odd, tail, up_tail)
    pitch_b[120:BLOCK] = jnp.where(pitch_odd, up_tail, tail)
    inner[120:BLOCK] = tail
    inner[BLOCK + 120 :] = tail
    for s in range(5):
        at = slice(s * 25, s * 25 + 25)
        upper, lower = (
            [flat[pl.ds(p * 10 + 2 * s + e, 25, stride=50), :] for e in range(2)] for p in (4, 0)
        )
        pitch_a[at] = jnp.where(pitch_odd, lower[0], upper[1])
        pitch_b[at] = jnp.where(pitch_odd, upper[1], lower[0])
        inner[at] = upper[0]
        inner[BLOCK + s * 25 : BLOCK + s * 25 + 25] = lower[1]


def load_state(x, state):
    flat = x.reshape(x.shape[0], LANES)
    for e in range(2):
        lanes = slice(e * LANES, (e + 1) * LANES)
        for v in range(5):
            base = var_start(v)
            first = v * 250 + e
            for a in range(5):
                at = base + a * MAIN
                state[at : at + MAIN, lanes] = flat[pl.ds(first + a * 50, MAIN, stride=2), :]
            tail = base + TAIL
            state[tail : tail + 8, lanes] = jnp.zeros((8, LANES), jnp.float32)
            state[tail : tail + 5, lanes] = flat[pl.ds(first + 2 * MAIN, 5, stride=50), :]


def add_axial_terms(gain, state, partial):
    lanes = lax.broadcasted_iota(jnp.int32, (MAIN + 8, LANES), 1)
    rows = lax.broadcasted_iota(jnp.int32, (8, LANES), 0)
    for e in range(2):
        own = slice(e * LANES, (e + 1) * LANES)
        upper_gap, lower_gap = ([], [])
        for v in range(5):
            base = var_start(v)
            lower = state[base : base + MAIN, own]
            upper = state[base + 4 * MAIN : base + TAIL, own]
            tail = state[base + TAIL : base + PER_VAR, own]
            turned = pltpu.roll(tail, 4, 0)
            join = lambda main, end: jnp.concatenate([main, end], axis=0)
            after = pltpu.roll(join(lower, turned), LANES - 1, 1)
            before = pltpu.roll(join(upper, turned), 1, 1)
            upper = join(upper, tail)
            upper_gap.append(jnp.where(lanes == LANES - 1, 0.0, upper - after))
            lower_gap.append(jnp.where(lanes == 0, 0.0, before) - join(lower, tail))
        mixed = []
        for gap, sign in ((upper_gap, -1.0), (lower_gap, 1.0)):
            mixed.append(combine(gain * lift_factor(0) * half_flux(0, sign), gap))
        for v in range(5):
            base = var_start(v)
            upper, lower = (mixed[0][v], mixed[1][v])
            partial[base : base + MAIN, own] += lower[:MAIN]
            partial[base + 4 * MAIN : base + TAIL, own] += upper[:MAIN]
            ends = jnp.where(rows == 0, lower[MAIN:], jnp.where(rows == 4, upper[MAIN:], 0.0))
            partial[base + TAIL : base + PER_VAR, own] += ends


def volume_rate(table, high, low):
    rate = [None] * 5
    for first, start, stop in TILES:
        part = slice(start * PER_VAR, stop * PER_VAR)
        table_high, table_low = (
            table[at + first * PER_VAR : at + ROWS, part] for at in (HIGH_AT, LOW_AT)
        )
        term = product(table_high, high[part], low[part]) + dot(table_low, high[part])
        for v in range(first, 5):
            block = term[(v - first) * PER_VAR : (v - first + 1) * PER_VAR]
            rate[v] = block if rate[v] is None else rate[v] + block
    return jnp.concatenate(rate, axis=0)


def advance_body(section, base, state, table, partial, faces):
    rate = volume_rate(table, *split(state[...]))
    gain, keep = GAIN[section], KEEP[section]
    if keep == 0.0:
        partial[...] = state[...] + rate
    else:
        partial[...] = keep * base[...] + gain * (state[...] + rate)
    add_axial_terms(gain, state, partial)
    if faces is not None:
        faces[...] = product(table[TRACE_AT : TRACE_AT + TRACES], *split(partial[...]))


def lift_table(table):
    return table[LIFT_AT : LIFT_AT + ROWS]


def first_kernel(offsets, x, table, base, partial, faces, flags):
    cols = lax.broadcasted_iota(jnp.int32, flags.shape, 1)
    moved = jnp.zeros(flags.shape, jnp.float32)
    for k in range(3):
        moved = jnp.where((cols == k) & (offsets[k] % 2 == 1), 1.0, moved)
    flags[...] = moved
    load_state(x, base)
    advance_body(0, None, base, table, partial, faces)


def later_kernel(section, base, before, halo_high, halo_low, table, partial, *refs):
    *faces, state = refs
    lifted = product(lift_table(table), halo_high[...], halo_low[...])
    state[...] = before[...] + GAIN[section - 1] * lifted
    advance_body(section, base, state, table, partial, faces[0] if faces else None)


def gather_halo(section, flags, pitch_a, pitch_b, span_a, span_b, inner, halo):
    pitch_odd, span_odd = parities()
    after = jnp.where(pitch_odd, pitch_b[...], pitch_a[...])
    before = jnp.where(pitch_odd, pitch_a[...], pitch_b[...])
    scales = half_scales()
    halo[0:BLOCK, :LANES] = scales[0] * before
    halo[0:BLOCK, LANES:] = scales[0] * inner[0:BLOCK]
    halo[BLOCK : 2 * BLOCK, :LANES] = scales[1] * inner[BLOCK:]
    halo[BLOCK : 2 * BLOCK, LANES:] = scales[1] * after
    above = jnp.where(span_odd, span_b[...], span_a[...])
    below = jnp.where(span_odd, span_a[...], span_b[...])
    rest = jnp.zeros((BLOCK - SPAN_ROWS, 2 * LANES), jnp.float32)
    halo[2 * BLOCK : 2 * BLOCK + SPAN_ROWS] = scales[2] * below
    halo[2 * BLOCK + SPAN_ROWS : 3 * BLOCK] = rest
    halo[3 * BLOCK : 3 * BLOCK + SPAN_ROWS] = scales[3] * above
    halo[3 * BLOCK + SPAN_ROWS : 4 * BLOCK] = rest
    wake = before[WAKE_ROW : WAKE_ROW + 2]
    moved = flags[0:1, section : section + 1] > 0.5
    rows = lax.broadcasted_iota(jnp.int32, (BLOCK, LANES), 0)
    cols = lax.broadcasted_iota(jnp.int32, (BLOCK, LANES), 1)
    for e in range(2):
        row = jnp.where(moved, wake[1 - e : 2 - e], wake[e : e + 1])
        column = jnp.sum(jnp.where(rows == cols, row, 0.0), axis=1, keepdims=True)
        halo[4 * BLOCK :, e * LANES : (e + 1) * LANES] = jnp.where(
            cols == 0, scales[4] * column, 0.0
        )
    return wake


def next_traces(section, side, faces, table, high, low):
    at = LINK_AT + side * 2 * BLOCK
    rows = slice(side * 2 * BLOCK, (side + 1) * 2 * BLOCK)
    return faces[rows] + GAIN[section] * product(table[at : at + 2 * BLOCK], high, low)


def span_kernel(
    section, flags, pitch_a, pitch_b, span_a, span_b, inner, faces, table,
    next_span_a, next_span_b, halo_high, halo_low, wake, halo,
):
    arrived = gather_halo(section, flags, pitch_a, pitch_b, span_a, span_b, inner, halo)
    wake[...] = jnp.concatenate([arrived, jnp.zeros((6, LANES), jnp.float32)], axis=0)
    high, low = split(halo[...])
    halo_high[...] = high
    halo_low[...] = low
    _, span_odd = parities()
    traces = next_traces(section, 1, faces, table, high, low)
    emit_span_faces(traces, span_odd, next_span_a, next_span_b)


def pitch_kernel(
    section, faces, table, halo_high, halo_low, wake, next_pitch_a, next_pitch_b, next_inner
):
    pitch_odd, _ = parities()
    traces = next_traces(section, 0, faces, table, halo_high[...], halo_low[...])
    emit_pitch_faces(
        traces, [wake[0:1], wake[1:2]], pitch_odd, next_pitch_a, next_pitch_b, next_inner
    )


def final_kernel(
    flags, pitch_a, pitch_b, span_a, span_b, inner, before, table, out, halo, result, done
):
    gather_halo(2, flags, pitch_a, pitch_b, span_a, span_b, inner, halo)
    total = before[...] + GAIN[2] * product(lift_table(table), *split(halo[...]))
    flat = result.reshape(result.shape[0], LANES)
    copies = []
    for v in ORDER:
        base = var_start(v)
        for e in range(2):
            lanes = slice(e * LANES, (e + 1) * LANES)
            first = v * 250 + e
            for a in range(5):
                at = base + a * MAIN
                flat[pl.ds(first + a * 50, MAIN, stride=2), :] = total[at : at + MAIN, lanes]
            tail = base + TAIL
            flat[pl.ds(first + 2 * MAIN, 5, stride=50), :] = total[tail : tail + 5, lanes]
        part = pl.ds(v * 250, 250)
        copies.append(pltpu.make_async_copy(result.at[part], out.at[part], done.at[v]))
        copies[-1].start()
    for copy in copies:
        copy.wait()


IN_VMEM = pl.BlockSpec(memory_space=pltpu.VMEM)
IN_SMEM = pl.BlockSpec(memory_space=pltpu.SMEM)


def call(kernel, name, outs, args, in_specs=(), scratch=(), flops=0, out_spec=IN_VMEM):
    in_specs = list(in_specs)
    return pl.pallas_call(
        kernel,
        name=name,
        out_shape=[jax.ShapeDtypeStruct(shape, dtype) for shape, dtype in outs],
        in_specs=in_specs + [IN_VMEM] * (len(args) - len(in_specs)),
        out_specs=[out_spec] * len(outs),
        scratch_shapes=list(scratch),
        compiler_params=pltpu.CompilerParams(vmem_limit_bytes=VMEM_LIMIT),
        cost_estimate=pl.CostEstimate(flops=flops, bytes_accessed=2**20, transcendentals=0),
    )(*args)


def swapped(value, axis, odd, wrap):
    size = lax.axis_size(axis)
    pairs = []
    for i in range(odd, size if wrap else size - 1, 2):
        j = (i + 1) % size
        pairs += [(i, j), (j, i)]
    return lax.ppermute(value, axis, pairs)


def span_exchanged(faces):
    return swapped(faces[0], "span", 0, False), swapped(faces[1], "span", 1, False)


def pitch_exchanged(faces):
    return swapped(faces[0], "pitch", 0, True), swapped(faces[1], "pitch", 1, True)


F32 = jnp.float32
PITCH_OUTS = [((BLOCK, LANES), F32), ((BLOCK, LANES), F32), ((2 * BLOCK, LANES), F32)]
SPAN_OUTS = [((SPAN_ROWS, 2 * LANES), F32)] * 2
SMALL_OUT = ((8, LANES), F32)
HALO_OUTS = [((HALO, 2 * LANES), jnp.bfloat16)] * 2
STATE_OUT = ((ROWS, 2 * LANES), F32)
TRACE_OUT = ((TRACES, 2 * LANES), F32)


def shards(table, state, wake_planes, bar_offsets):
    x = state.reshape(-1, 1, LANES)
    wake = wake_planes.transpose(0, 1, 3, 4, 2).reshape(50, 1, 5)
    faces = call(begin_span_kernel, "begin_span", SPAN_OUTS, [x])
    span = span_exchanged(faces)
    *faces, inner = call(begin_pitch_kernel, "begin_pitch", PITCH_OUTS, [x, wake])
    pitch = pitch_exchanged(faces)
    base, partial, traces, flags = call(
        first_kernel,
        "first",
        [STATE_OUT, STATE_OUT, TRACE_OUT, SMALL_OUT],
        [bar_offsets, x, table],
        in_specs=[IN_SMEM],
        flops=10**9,
    )
    for section in range(2):
        *faces, high, low, carried = call(
            functools.partial(span_kernel, section),
            "span_faces",
            SPAN_OUTS + HALO_OUTS + [SMALL_OUT],
            [flags, *pitch, *span, inner, traces, table],
            scratch=[pltpu.VMEM((HALO, 2 * LANES), F32)],
            flops=10**8,
        )
        span = span_exchanged(faces)
        *faces, inner = call(
            functools.partial(pitch_kernel, section),
            "pitch_faces",
            PITCH_OUTS,
            [traces, table, high, low, carried],
            flops=10**8,
        )
        pitch = pitch_exchanged(faces)
        last = section == 1
        partial, *traces = call(
            functools.partial(later_kernel, section + 1),
            "last" if last else "later",
            [STATE_OUT] if last else [STATE_OUT, TRACE_OUT],
            [base, partial, high, low, table],
            scratch=[pltpu.VMEM((ROWS, 2 * LANES), F32)],
            flops=10**9,
        )
        traces = None if last else traces[0]
    (out,) = call(
        final_kernel,
        "final",
        [(x.shape, F32)],
        [flags, *pitch, *span, inner, partial, table],
        scratch=[
            pltpu.VMEM((HALO, 2 * LANES), F32),
            pltpu.VMEM(x.shape, F32),
            pltpu.SemaphoreType.DMA((5,)),
        ],
        flops=10**8,
        out_spec=pl.BlockSpec(memory_space=pl.ANY),
    )
    return out.reshape(state.shape)


def solution(mesh):
    volume, lift, trace, link = operator_tables()
    high, low = split_table(volume)
    table = np.concatenate([exact_table(t) for t in (trace, link, lift)] + [high, low])
    assert table.shape == (TABLE_ROWS, ROWS)
    in_specs = (
        P(None, None, None, None, "pitch", "span", None),
        P(None, None, None, "pitch", "span"),
        P(),
    )
    out_specs = P(None, None, None, None, "pitch", "span", None)
    return jax.shard_map(
        functools.partial(shards, jnp.asarray(table)),
        mesh=mesh,
        in_specs=in_specs,
        out_specs=out_specs,
        check_vma=False,
    )
```

```python
import functools

import jax
import jax.numpy as jnp
import ml_dtypes
import numpy as np
from jax import lax
from jax.experimental import pallas as pl
from jax.experimental.pallas import tpu as pltpu
from jax.sharding import PartitionSpec as P

MEAN_FLOW = (0.5, 0.3, 0.0)
WAVE_SPEED = (1.5, 1.3, 1.0)
ELEM_SIZE = (1.0, 0.8, 1.2)
END_WEIGHT = 0.1
TIME_STEP = 0.01
KEEP = (0.0, 0.75, 1.0 / 3.0)
GAIN = (1.0, 0.25, 2.0 / 3.0)

ORDER = (1, 4, 2, 3, 0)
MAIN = 24
TAIL = 5 * MAIN
PER_VAR = 128
ROWS = 5 * PER_VAR
TILES = ((0, 0, 2), (1, 2, 4), (4, 4, 5))
BLOCK = 128
SPAN_ROWS = 104
TRACES = 4 * BLOCK
HALO = 5 * BLOCK
WAKE_ROW = 125
TRACE_AT, LINK_AT, LIFT_AT = (0, TRACES, 2 * TRACES)
HIGH_AT = LIFT_AT + ROWS
LOW_AT = HIGH_AT + ROWS
TABLE_ROWS = LOW_AT + ROWS
LANES = 128
VMEM_LIMIT = 24 * 1024 * 1024


def derivative_table():
    points = np.array([-1.0, -np.sqrt(3.0 / 7.0), 0.0, np.sqrt(3.0 / 7.0), 1.0])
    products = np.array(
        [np.prod([points[j] - points[k] for k in range(5) if k != j]) for j in range(5)]
    )
    matrix = np.zeros((5, 5))
    for i in range(5):
        for j in range(5):
            if i != j:
                matrix[i, j] = products[i] / (products[j] * (points[i] - points[j]))
        matrix[i, i] = sum((1.0 / (points[i] - points[k]) for k in range(5) if k != i))
    return matrix


def flux_matrix(direction):
    flux = MEAN_FLOW[direction] * np.eye(5)
    flux[0, 1 + direction] += 1.0
    flux[4, 1 + direction] += 1.0
    flux[1 + direction, 4] += 1.0
    return flux


def half_flux(direction, sign):
    return 0.5 * (flux_matrix(direction) + sign * WAVE_SPEED[direction] * np.eye(5))


def lift_factor(direction):
    return TIME_STEP * 2.0 / (ELEM_SIZE[direction] * END_WEIGHT)


def half_scales():
    return (lift_factor(1) / 10.0, lift_factor(1), lift_factor(2), lift_factor(2), lift_factor(0))


def var_start(v):
    return ORDER.index(v) * PER_VAR


def node_row(v, a, p, s):
    node = p * 5 + s
    return var_start(v) + (a * MAIN + node if node < MAIN else TAIL + a)


def operator_tables():
    deriv = derivative_table()
    volume = np.zeros((ROWS, ROWS))
    lift = np.zeros((ROWS, HALO))
    trace = np.zeros((TRACES, ROWS))
    fluxes = [flux_matrix(d) for d in range(3)]
    plus = [half_flux(d, 1.0) for d in range(3)]
    minus = [half_flux(d, -1.0) for d in range(3)]
    plus_sent, minus_sent = (plus[2][:4], minus[2][:4])
    back_plus = np.vstack([np.eye(4), [[0.0, 0.0, 0.0, 1.0]]])
    back_minus = np.vstack([np.eye(4), [[0.0, 0.0, 0.0, -1.0]]])
    assert np.allclose(back_plus @ plus_sent, plus[2])
    assert np.allclose(back_minus @ minus_sent, minus[2])
    for a in range(5):
        for p in range(5):
            for s in range(5):
                here = [node_row(v, a, p, s) for v in range(5)]
                place = (a, p, s)
                for d in range(3):
                    for j in range(5):
                        there = list(place)
                        there[d] = j
                        cols = [node_row(v, *there) for v in range(5)]
                        coeff = -TIME_STEP * (2.0 / ELEM_SIZE[d]) * deriv[place[d], j]
                        volume[np.ix_(here, cols)] += coeff * fluxes[d]
                for d in (1, 2):
                    if place[d] == 4:
                        volume[np.ix_(here, here)] += lift_factor(d) * minus[d]
                    if place[d] == 0:
                        volume[np.ix_(here, here)] -= lift_factor(d) * plus[d]
                if p == 0:
                    cols = [s * 25 + v * 5 + a for v in range(5)]
                    lift[np.ix_(here, cols)] += lift_factor(1) * plus[1]
                    for v in range(5):
                        trace[BLOCK + s * 25 + v * 5 + a, here[v]] = 1.0
                if p == 4:
                    cols = [BLOCK + s * 25 + v * 5 + a for v in range(5)]
                    lift[np.ix_(here, cols)] -= lift_factor(1) * minus[1]
                    for v in range(5):
                        trace[s * 25 + v * 5 + a, here[v]] = 1.0
                if s == 0:
                    cols = [2 * BLOCK + c * 25 + a * 5 + p for c in range(4)]
                    lift[np.ix_(here, cols)] += lift_factor(2) * back_plus
                    rows = [3 * BLOCK + c * 25 + a * 5 + p for c in range(4)]
                    trace[np.ix_(rows, here)] += minus_sent
                if s == 4:
                    cols = [3 * BLOCK + c * 25 + a * 5 + p for c in range(4)]
                    lift[np.ix_(here, cols)] -= lift_factor(2) * back_minus
                    rows = [2 * BLOCK + c * 25 + a * 5 + p for c in range(4)]
                    trace[np.ix_(rows, here)] += plus_sent
                if a == 0:
                    cols = [4 * BLOCK + v * 25 + p * 5 + s for v in range(5)]
                    lift[np.ix_(here, cols)] += lift_factor(0) * plus[0]
    lift = lift / np.repeat(half_scales(), BLOCK)
    return volume, lift, trace, trace @ lift


def exact_table(table):
    exact = table.astype(ml_dtypes.bfloat16)
    assert np.allclose(exact.astype(np.float64), table, rtol=1e-12, atol=1e-12)
    return exact


def split_table(table):
    high = table.astype(ml_dtypes.bfloat16)
    low = (table - high.astype(np.float64)).astype(ml_dtypes.bfloat16)
    return high, low


def split(values):
    high = values.astype(jnp.bfloat16)
    low = (values - high.astype(jnp.float32)).astype(jnp.bfloat16)
    return high, low


def dot(left, right):
    return jnp.dot(left, right, preferred_element_type=jnp.float32)


def product(table, high, low):
    return dot(table, high) + dot(table, low)


def with_rows(values, first, extra):
    rows = lax.broadcasted_iota(jnp.int32, values.shape, 0)
    for k, row in enumerate(extra):
        values = jnp.where(rows == first + k, row, values)
    return values


def emit_pitch_faces(traces, wake, pitch_odd, pitch_a, pitch_b, inner):
    upper, lower = traces[0:BLOCK], traces[BLOCK : 2 * BLOCK]
    up = with_rows(upper[:, LANES:], WAKE_ROW, wake)
    down = lower[:, :LANES]
    pitch_a[...] = jnp.where(pitch_odd, down, up)
    pitch_b[...] = jnp.where(pitch_odd, up, down)
    inner[0:BLOCK] = upper[:, :LANES]
    inner[BLOCK:] = lower[:, LANES:]


def emit_span_faces(traces, span_odd, span_a, span_b):
    above, below = traces[0:SPAN_ROWS], traces[BLOCK : BLOCK + SPAN_ROWS]
    span_a[...] = jnp.where(span_odd, below, above)
    span_b[...] = jnp.where(span_odd, above, below)


def parities():
    return lax.axis_index("pitch") % 2 == 1, lax.axis_index("span") % 2 == 1


def combine(table, values):
    return [
        sum(float(table[i, j]) * values[j] for j in range(5) if table[i, j] != 0.0)
        for i in range(table.shape[0])
    ]


def begin_span_kernel(x, span_a, span_b):
    flat = x.reshape(x.shape[0], LANES)
    _, span_odd = parities()
    rest = jnp.zeros((SPAN_ROWS - 96, LANES), jnp.float32)
    for e in range(2):
        lanes = slice(e * LANES, (e + 1) * LANES)
        sides = []
        for s, sign in ((4, 1.0), (0, -1.0)):
            faces = [flat[pl.ds(v * 250 + 2 * s + e, 25, stride=10), :] for v in range(5)]
            sides.append(combine(half_flux(2, sign)[:4], faces))
        span_a[96:SPAN_ROWS, lanes] = rest
        span_b[96:SPAN_ROWS, lanes] = rest
        for c in range(4):
            above, below = (sides[0][c], sides[1][c])
            span_a[c * 25 : c * 25 + 25, lanes] = jnp.where(span_odd, below, above)
            span_b[c * 25 : c * 25 + 25, lanes] = jnp.where(span_odd, above, below)


def begin_pitch_kernel(x, wake, pitch_a, pitch_b, inner):
    flat = x.reshape(x.shape[0], LANES)
    pitch_odd, _ = parities()
    planes = wake.reshape(50, 5)[...]
    rows = lax.broadcasted_iota(jnp.int32, (50, LANES), 0)
    cols = lax.broadcasted_iota(jnp.int32, (50, LANES), 1)
    spread = jnp.zeros((50, LANES), jnp.float32)
    for s in range(5):
        mine = (cols - s) == 5 * (rows // 2)
        spread = jnp.where(mine, planes[:, s : s + 1], spread)
    own = [
        jnp.sum(jnp.where(rows % 2 == k, spread, 0.0), axis=0, keepdims=True) for k in range(2)
    ]
    tail = jnp.zeros((8, LANES), jnp.float32)
    up_tail = with_rows(tail, WAKE_ROW - 120, own)
    pitch_a[120:BLOCK] = jnp.where(pitch_odd, tail, up_tail)
    pitch_b[120:BLOCK] = jnp.where(pitch_odd, up_tail, tail)
    inner[120:BLOCK] = tail
    inner[BLOCK + 120 :] = tail
    for s in range(5):
        at = slice(s * 25, s * 25 + 25)
        upper, lower = (
            [flat[pl.ds(p * 10 + 2 * s + e, 25, stride=50), :] for e in range(2)] for p in (4, 0)
        )
        pitch_a[at] = jnp.where(pitch_odd, lower[0], upper[1])
        pitch_b[at] = jnp.where(pitch_odd, upper[1], lower[0])
        inner[at] = upper[0]
        inner[BLOCK + s * 25 : BLOCK + s * 25 + 25] = lower[1]


def load_state(x, state):
    flat = x.reshape(x.shape[0], LANES)
    for e in range(2):
        lanes = slice(e * LANES, (e + 1) * LANES)
        for v in range(5):
            base = var_start(v)
            first = v * 250 + e
            for a in range(5):
                at = base + a * MAIN
                state[at : at + MAIN, lanes] = flat[pl.ds(first + a * 50, MAIN, stride=2), :]
            tail = base + TAIL
            state[tail : tail + 8, lanes] = jnp.zeros((8, LANES), jnp.float32)
            state[tail : tail + 5, lanes] = flat[pl.ds(first + 2 * MAIN, 5, stride=50), :]


def add_axial_terms(gain, state, partial):
    lanes = lax.broadcasted_iota(jnp.int32, (MAIN + 8, LANES), 1)
    rows = lax.broadcasted_iota(jnp.int32, (8, LANES), 0)
    for e in range(2):
        own = slice(e * LANES, (e + 1) * LANES)
        upper_gap, lower_gap = ([], [])
        for v in range(5):
            base = var_start(v)
            lower = state[base : base + MAIN, own]
            upper = state[base + 4 * MAIN : base + TAIL, own]
            tail = state[base + TAIL : base + PER_VAR, own]
            turned = pltpu.roll(tail, 4, 0)
            join = lambda main, end: jnp.concatenate([main, end], axis=0)
            after = pltpu.roll(join(lower, turned), LANES - 1, 1)
            before = pltpu.roll(join(upper, turned), 1, 1)
            upper = join(upper, tail)
            upper_gap.append(jnp.where(lanes == LANES - 1, 0.0, upper - after))
            lower_gap.append(jnp.where(lanes == 0, 0.0, before) - join(lower, tail))
        mixed = []
        for gap, sign in ((upper_gap, -1.0), (lower_gap, 1.0)):
            mixed.append(combine(gain * lift_factor(0) * half_flux(0, sign), gap))
        for v in range(5):
            base = var_start(v)
            upper, lower = (mixed[0][v], mixed[1][v])
            partial[base : base + MAIN, own] += lower[:MAIN]
            partial[base + 4 * MAIN : base + TAIL, own] += upper[:MAIN]
            ends = jnp.where(rows == 0, lower[MAIN:], jnp.where(rows == 4, upper[MAIN:], 0.0))
            partial[base + TAIL : base + PER_VAR, own] += ends


def volume_rate(table, high, low):
    rate = [None] * 5
    for first, start, stop in TILES:
        part = slice(start * PER_VAR, stop * PER_VAR)
        table_high, table_low = (
            table[at + first * PER_VAR : at + ROWS, part] for at in (HIGH_AT, LOW_AT)
        )
        term = product(table_high, high[part], low[part]) + dot(table_low, high[part])
        for v in range(first, 5):
            block = term[(v - first) * PER_VAR : (v - first + 1) * PER_VAR]
            rate[v] = block if rate[v] is None else rate[v] + block
    return jnp.concatenate(rate, axis=0)


def advance_body(section, base, state, table, partial, faces):
    rate = volume_rate(table, *split(state[...]))
    gain, keep = GAIN[section], KEEP[section]
    if keep == 0.0:
        partial[...] = state[...] + rate
    else:
        partial[...] = keep * base[...] + gain * (state[...] + rate)
    add_axial_terms(gain, state, partial)
    if faces is not None:
        faces[...] = product(table[TRACE_AT : TRACE_AT + TRACES], *split(partial[...]))


def lift_table(table):
    return table[LIFT_AT : LIFT_AT + ROWS]


def first_kernel(offsets, x, table, base, partial, faces, flags):
    cols = lax.broadcasted_iota(jnp.int32, flags.shape, 1)
    moved = jnp.zeros(flags.shape, jnp.float32)
    for k in range(3):
        moved = jnp.where((cols == k) & (offsets[k] % 2 == 1), 1.0, moved)
    flags[...] = moved
    load_state(x, base)
    advance_body(0, None, base, table, partial, faces)


def later_kernel(section, base, before, halo_high, halo_low, table, partial, *refs):
    *faces, state = refs
    lifted = product(lift_table(table), halo_high[...], halo_low[...])
    state[...] = before[...] + GAIN[section - 1] * lifted
    advance_body(section, base, state, table, partial, faces[0] if faces else None)


def gather_halo(section, flags, pitch_a, pitch_b, span_a, span_b, inner, halo):
    pitch_odd, span_odd = parities()
    after = jnp.where(pitch_odd, pitch_b[...], pitch_a[...])
    before = jnp.where(pitch_odd, pitch_a[...], pitch_b[...])
    scales = half_scales()
    halo[0:BLOCK, :LANES] = scales[0] * before
    halo[0:BLOCK, LANES:] = scales[0] * inner[0:BLOCK]
    halo[BLOCK : 2 * BLOCK, :LANES] = scales[1] * inner[BLOCK:]
    halo[BLOCK : 2 * BLOCK, LANES:] = scales[1] * after
    above = jnp.where(span_odd, span_b[...], span_a[...])
    below = jnp.where(span_odd, span_a[...], span_b[...])
    rest = jnp.zeros((BLOCK - SPAN_ROWS, 2 * LANES), jnp.float32)
    halo[2 * BLOCK : 2 * BLOCK + SPAN_ROWS] = scales[2] * below
    halo[2 * BLOCK + SPAN_ROWS : 3 * BLOCK] = rest
    halo[3 * BLOCK : 3 * BLOCK + SPAN_ROWS] = scales[3] * above
    halo[3 * BLOCK + SPAN_ROWS : 4 * BLOCK] = rest
    wake = before[WAKE_ROW : WAKE_ROW + 2]
    moved = flags[0:1, section : section + 1] > 0.5
    rows = lax.broadcasted_iota(jnp.int32, (BLOCK, LANES), 0)
    cols = lax.broadcasted_iota(jnp.int32, (BLOCK, LANES), 1)
    for e in range(2):
        row = jnp.where(moved, wake[1 - e : 2 - e], wake[e : e + 1])
        column = jnp.sum(jnp.where(rows == cols, row, 0.0), axis=1, keepdims=True)
        halo[4 * BLOCK :, e * LANES : (e + 1) * LANES] = jnp.where(
            cols == 0, scales[4] * column, 0.0
        )
    return wake


def next_traces(section, side, faces, table, high, low):
    at = LINK_AT + side * 2 * BLOCK
    rows = slice(side * 2 * BLOCK, (side + 1) * 2 * BLOCK)
    return faces[rows] + GAIN[section] * product(table[at : at + 2 * BLOCK], high, low)


def span_kernel(
    section, flags, pitch_a, pitch_b, span_a, span_b, inner, faces, table,
    next_span_a, next_span_b, halo_high, halo_low, wake, halo,
):
    arrived = gather_halo(section, flags, pitch_a, pitch_b, span_a, span_b, inner, halo)
    wake[...] = jnp.concatenate([arrived, jnp.zeros((6, LANES), jnp.float32)], axis=0)
    high, low = split(halo[...])
    halo_high[...] = high
    halo_low[...] = low
    _, span_odd = parities()
    traces = next_traces(section, 1, faces, table, high, low)
    emit_span_faces(traces, span_odd, next_span_a, next_span_b)


def pitch_kernel(
    section, faces, table, halo_high, halo_low, wake, next_pitch_a, next_pitch_b, next_inner
):
    pitch_odd, _ = parities()
    traces = next_traces(section, 0, faces, table, halo_high[...], halo_low[...])
    emit_pitch_faces(
        traces, [wake[0:1], wake[1:2]], pitch_odd, next_pitch_a, next_pitch_b, next_inner
    )


def final_kernel(
    flags, pitch_a, pitch_b, span_a, span_b, inner, before, table, out, halo, result, done
):
    gather_halo(2, flags, pitch_a, pitch_b, span_a, span_b, inner, halo)
    total = before[...] + GAIN[2] * product(lift_table(table), *split(halo[...]))
    flat = result.reshape(result.shape[0], LANES)
    copies = []
    for v in ORDER:
        base = var_start(v)
        for e in range(2):
            lanes = slice(e * LANES, (e + 1) * LANES)
            first = v * 250 + e
            for a in range(5):
                at = base + a * MAIN
                flat[pl.ds(first + a * 50, MAIN, stride=2), :] = total[at : at + MAIN, lanes]
            tail = base + TAIL
            flat[pl.ds(first + 2 * MAIN, 5, stride=50), :] = total[tail : tail + 5, lanes]
        part = pl.ds(v * 250, 250)
        copies.append(pltpu.make_async_copy(result.at[part], out.at[part], done.at[v]))
        copies[-1].start()
    for copy in copies:
        copy.wait()


IN_VMEM = pl.BlockSpec(memory_space=pltpu.VMEM)
IN_SMEM = pl.BlockSpec(memory_space=pltpu.SMEM)


def call(kernel, name, outs, args, in_specs=(), scratch=(), flops=0, out_spec=IN_VMEM):
    in_specs = list(in_specs)
    return pl.pallas_call(
        kernel,
        name=name,
        out_shape=[jax.ShapeDtypeStruct(shape, dtype) for shape, dtype in outs],
        in_specs=in_specs + [IN_VMEM] * (len(args) - len(in_specs)),
        out_specs=[out_spec] * len(outs),
        scratch_shapes=list(scratch),
        compiler_params=pltpu.CompilerParams(vmem_limit_bytes=VMEM_LIMIT),
        cost_estimate=pl.CostEstimate(flops=flops, bytes_accessed=2**20, transcendentals=0),
    )(*args)


def swapped(value, axis, odd, wrap):
    size = lax.axis_size(axis)
    pairs = []
    for i in range(odd, size if wrap else size - 1, 2):
        j = (i + 1) % size
        pairs += [(i, j), (j, i)]
    return lax.ppermute(value, axis, pairs)


def span_exchanged(faces):
    return swapped(faces[0], "span", 0, False), swapped(faces[1], "span", 1, False)


def pitch_exchanged(faces):
    return swapped(faces[0], "pitch", 0, True), swapped(faces[1], "pitch", 1, True)


F32 = jnp.float32
PITCH_OUTS = [((BLOCK, LANES), F32), ((BLOCK, LANES), F32), ((2 * BLOCK, LANES), F32)]
SPAN_OUTS = [((SPAN_ROWS, 2 * LANES), F32)] * 2
SMALL_OUT = ((8, LANES), F32)
HALO_OUTS = [((HALO, 2 * LANES), jnp.bfloat16)] * 2
STATE_OUT = ((ROWS, 2 * LANES), F32)
TRACE_OUT = ((TRACES, 2 * LANES), F32)


def shards(table, state, wake_planes, bar_offsets):
    x = state.reshape(-1, 1, LANES)
    wake = wake_planes.transpose(0, 1, 3, 4, 2).reshape(50, 1, 5)
    faces = call(begin_span_kernel, "begin_span", SPAN_OUTS, [x], flops=10**10)
    span = span_exchanged(faces)
    *faces, inner = call(begin_pitch_kernel, "begin_pitch", PITCH_OUTS, [x, wake], flops=10**10)
    pitch = pitch_exchanged(faces)
    base, partial, traces, flags = call(
        first_kernel,
        "first",
        [STATE_OUT, STATE_OUT, TRACE_OUT, SMALL_OUT],
        [bar_offsets, x, table],
        in_specs=[IN_SMEM],
        flops=10**9,
    )
    for section in range(2):
        *faces, high, low, carried = call(
            functools.partial(span_kernel, section),
            "span_faces",
            SPAN_OUTS + HALO_OUTS + [SMALL_OUT],
            [flags, *pitch, *span, inner, traces, table],
            scratch=[pltpu.VMEM((HALO, 2 * LANES), F32)],
            flops=10**8,
        )
        span = span_exchanged(faces)
        *faces, inner = call(
            functools.partial(pitch_kernel, section),
            "pitch_faces",
            PITCH_OUTS,
            [traces, table, high, low, carried],
            flops=10**8,
        )
        pitch = pitch_exchanged(faces)
        last = section == 1
        partial, *traces = call(
            functools.partial(later_kernel, section + 1),
            "last" if last else "later",
            [STATE_OUT] if last else [STATE_OUT, TRACE_OUT],
            [base, partial, high, low, table],
            scratch=[pltpu.VMEM((ROWS, 2 * LANES), F32)],
            flops=10**9,
        )
        traces = None if last else traces[0]
    (out,) = call(
        final_kernel,
        "final",
        [(x.shape, F32)],
        [flags, *pitch, *span, inner, partial, table],
        scratch=[
            pltpu.VMEM((HALO, 2 * LANES), F32),
            pltpu.VMEM(x.shape, F32),
            pltpu.SemaphoreType.DMA((5,)),
        ],
        flops=10**8,
        out_spec=pl.BlockSpec(memory_space=pl.ANY),
    )
    return out.reshape(state.shape)


def solution(mesh):
    volume, lift, trace, link = operator_tables()
    high, low = split_table(volume)
    table = np.concatenate([exact_table(t) for t in (trace, link, lift)] + [high, low])
    assert table.shape == (TABLE_ROWS, ROWS)
    in_specs = (
        P(None, None, None, None, "pitch", "span", None),
        P(None, None, None, "pitch", "span"),
        P(),
    )
    out_specs = P(None, None, None, None, "pitch", "span", None)
    return jax.shard_map(
        functools.partial(shards, jnp.asarray(table)),
        mesh=mesh,
        in_specs=in_specs,
        out_specs=out_specs,
        check_vma=False,
    )
```

```python
import functools

import jax
import jax.numpy as jnp
import ml_dtypes
import numpy as np
from jax import lax
from jax.experimental import pallas as pl
from jax.experimental.pallas import tpu as pltpu
from jax.sharding import PartitionSpec as P

MEAN_FLOW = (0.5, 0.3, 0.0)
WAVE_SPEED = (1.5, 1.3, 1.0)
ELEM_SIZE = (1.0, 0.8, 1.2)
END_WEIGHT = 0.1
TIME_STEP = 0.01
KEEP = (0.0, 0.75, 1.0 / 3.0)
GAIN = (1.0, 0.25, 2.0 / 3.0)

ORDER = (1, 4, 2, 3, 0)
MAIN = 24
TAIL = 5 * MAIN
PER_VAR = 128
ROWS = 5 * PER_VAR
TILES = ((0, 0, 2), (1, 2, 4), (4, 4, 5))
BLOCK = 128
SPAN_ROWS = 104
TRACES = 4 * BLOCK
HALO = 5 * BLOCK
WAKE_ROW = 125
TRACE_AT, LINK_AT, LIFT_AT = (0, TRACES, 2 * TRACES)
HIGH_AT = LIFT_AT + ROWS
LOW_AT = HIGH_AT + ROWS
TABLE_ROWS = LOW_AT + ROWS
LANES = 128
VMEM_LIMIT = 24 * 1024 * 1024


def derivative_table():
    points = np.array([-1.0, -np.sqrt(3.0 / 7.0), 0.0, np.sqrt(3.0 / 7.0), 1.0])
    products = np.array(
        [np.prod([points[j] - points[k] for k in range(5) if k != j]) for j in range(5)]
    )
    matrix = np.zeros((5, 5))
    for i in range(5):
        for j in range(5):
            if i != j:
                matrix[i, j] = products[i] / (products[j] * (points[i] - points[j]))
        matrix[i, i] = sum((1.0 / (points[i] - points[k]) for k in range(5) if k != i))
    return matrix


def flux_matrix(direction):
    flux = MEAN_FLOW[direction] * np.eye(5)
    flux[0, 1 + direction] += 1.0
    flux[4, 1 + direction] += 1.0
    flux[1 + direction, 4] += 1.0
    return flux


def half_flux(direction, sign):
    return 0.5 * (flux_matrix(direction) + sign * WAVE_SPEED[direction] * np.eye(5))


def lift_factor(direction):
    return TIME_STEP * 2.0 / (ELEM_SIZE[direction] * END_WEIGHT)


def half_scales():
    return (lift_factor(1) / 10.0, lift_factor(1), lift_factor(2), lift_factor(2), lift_factor(0))


def var_start(v):
    return ORDER.index(v) * PER_VAR


def node_row(v, a, p, s):
    node = p * 5 + s
    return var_start(v) + (a * MAIN + node if node < MAIN else TAIL + a)


def operator_tables():
    deriv = derivative_table()
    volume = np.zeros((ROWS, ROWS))
    lift = np.zeros((ROWS, HALO))
    trace = np.zeros((TRACES, ROWS))
    fluxes = [flux_matrix(d) for d in range(3)]
    plus = [half_flux(d, 1.0) for d in range(3)]
    minus = [half_flux(d, -1.0) for d in range(3)]
    plus_sent, minus_sent = (plus[2][:4], minus[2][:4])
    back_plus = np.vstack([np.eye(4), [[0.0, 0.0, 0.0, 1.0]]])
    back_minus = np.vstack([np.eye(4), [[0.0, 0.0, 0.0, -1.0]]])
    assert np.allclose(back_plus @ plus_sent, plus[2])
    assert np.allclose(back_minus @ minus_sent, minus[2])
    for a in range(5):
        for p in range(5):
            for s in range(5):
                here = [node_row(v, a, p, s) for v in range(5)]
                place = (a, p, s)
                for d in range(3):
                    for j in range(5):
                        there = list(place)
                        there[d] = j
                        cols = [node_row(v, *there) for v in range(5)]
                        coeff = -TIME_STEP * (2.0 / ELEM_SIZE[d]) * deriv[place[d], j]
                        volume[np.ix_(here, cols)] += coeff * fluxes[d]
                for d in (1, 2):
                    if place[d] == 4:
                        volume[np.ix_(here, here)] += lift_factor(d) * minus[d]
                    if place[d] == 0:
                        volume[np.ix_(here, here)] -= lift_factor(d) * plus[d]
                if p == 0:
                    cols = [s * 25 + v * 5 + a for v in range(5)]
                    lift[np.ix_(here, cols)] += lift_factor(1) * plus[1]
                    for v in range(5):
                        trace[BLOCK + s * 25 + v * 5 + a, here[v]] = 1.0
                if p == 4:
                    cols = [BLOCK + s * 25 + v * 5 + a for v in range(5)]
                    lift[np.ix_(here, cols)] -= lift_factor(1) * minus[1]
                    for v in range(5):
                        trace[s * 25 + v * 5 + a, here[v]] = 1.0
                if s == 0:
                    cols = [2 * BLOCK + c * 25 + a * 5 + p for c in range(4)]
                    lift[np.ix_(here, cols)] += lift_factor(2) * back_plus
                    rows = [3 * BLOCK + c * 25 + a * 5 + p for c in range(4)]
                    trace[np.ix_(rows, here)] += minus_sent
                if s == 4:
                    cols = [3 * BLOCK + c * 25 + a * 5 + p for c in range(4)]
                    lift[np.ix_(here, cols)] -= lift_factor(2) * back_minus
                    rows = [2 * BLOCK + c * 25 + a * 5 + p for c in range(4)]
                    trace[np.ix_(rows, here)] += plus_sent
                if a == 0:
                    cols = [4 * BLOCK + v * 25 + p * 5 + s for v in range(5)]
                    lift[np.ix_(here, cols)] += lift_factor(0) * plus[0]
    lift = lift / np.repeat(half_scales(), BLOCK)
    return volume, lift, trace, trace @ lift


def exact_table(table):
    exact = table.astype(ml_dtypes.bfloat16)
    assert np.allclose(exact.astype(np.float64), table, rtol=1e-12, atol=1e-12)
    return exact


def split_table(table):
    high = table.astype(ml_dtypes.bfloat16)
    low = (table - high.astype(np.float64)).astype(ml_dtypes.bfloat16)
    return high, low


def split(values):
    high = values.astype(jnp.bfloat16)
    low = (values - high.astype(jnp.float32)).astype(jnp.bfloat16)
    return high, low


def dot(left, right):
    return jnp.dot(left, right, preferred_element_type=jnp.float32)


def product(table, high, low):
    return dot(table, high) + dot(table, low)


def with_rows(values, first, extra):
    rows = lax.broadcasted_iota(jnp.int32, values.shape, 0)
    for k, row in enumerate(extra):
        values = jnp.where(rows == first + k, row, values)
    return values


def emit_pitch_faces(traces, wake, pitch_odd, pitch_a, pitch_b, inner):
    upper, lower = traces[0:BLOCK], traces[BLOCK : 2 * BLOCK]
    up = with_rows(upper[:, LANES:], WAKE_ROW, wake)
    down = lower[:, :LANES]
    pitch_a[...] = jnp.where(pitch_odd, down, up)
    pitch_b[...] = jnp.where(pitch_odd, up, down)
    inner[0:BLOCK] = upper[:, :LANES]
    inner[BLOCK:] = lower[:, LANES:]


def emit_span_faces(traces, span_odd, span_a, span_b):
    above, below = traces[0:SPAN_ROWS], traces[BLOCK : BLOCK + SPAN_ROWS]
    span_a[...] = jnp.where(span_odd, below, above)
    span_b[...] = jnp.where(span_odd, above, below)


def parities():
    return lax.axis_index("pitch") % 2 == 1, lax.axis_index("span") % 2 == 1


def combine(table, values):
    return [
        sum(float(table[i, j]) * values[j] for j in range(5) if table[i, j] != 0.0)
        for i in range(table.shape[0])
    ]


def begin_span_kernel(x, span_a, span_b):
    flat = x.reshape(x.shape[0], LANES)
    _, span_odd = parities()
    rest = jnp.zeros((SPAN_ROWS - 96, LANES), jnp.float32)
    for e in range(2):
        lanes = slice(e * LANES, (e + 1) * LANES)
        sides = []
        for s, sign in ((4, 1.0), (0, -1.0)):
            faces = [flat[pl.ds(v * 250 + 2 * s + e, 25, stride=10), :] for v in range(5)]
            sides.append(combine(half_flux(2, sign)[:4], faces))
        span_a[96:SPAN_ROWS, lanes] = rest
        span_b[96:SPAN_ROWS, lanes] = rest
        for c in range(4):
            above, below = (sides[0][c], sides[1][c])
            span_a[c * 25 : c * 25 + 25, lanes] = jnp.where(span_odd, below, above)
            span_b[c * 25 : c * 25 + 25, lanes] = jnp.where(span_odd, above, below)


def begin_pitch_kernel(x, wake, pitch_a, pitch_b, inner):
    flat = x.reshape(x.shape[0], LANES)
    pitch_odd, _ = parities()
    planes = wake.reshape(50, 5)[...]
    rows = lax.broadcasted_iota(jnp.int32, (50, LANES), 0)
    cols = lax.broadcasted_iota(jnp.int32, (50, LANES), 1)
    spread = jnp.zeros((50, LANES), jnp.float32)
    for s in range(5):
        mine = (cols - s) == 5 * (rows // 2)
        spread = jnp.where(mine, planes[:, s : s + 1], spread)
    own = [
        jnp.sum(jnp.where(rows % 2 == k, spread, 0.0), axis=0, keepdims=True) for k in range(2)
    ]
    tail = jnp.zeros((8, LANES), jnp.float32)
    up_tail = with_rows(tail, WAKE_ROW - 120, own)
    pitch_a[120:BLOCK] = jnp.where(pitch_odd, tail, up_tail)
    pitch_b[120:BLOCK] = jnp.where(pitch_odd, up_tail, tail)
    inner[120:BLOCK] = tail
    inner[BLOCK + 120 :] = tail
    for s in range(5):
        at = slice(s * 25, s * 25 + 25)
        upper, lower = (
            [flat[pl.ds(p * 10 + 2 * s + e, 25, stride=50), :] for e in range(2)] for p in (4, 0)
        )
        pitch_a[at] = jnp.where(pitch_odd, lower[0], upper[1])
        pitch_b[at] = jnp.where(pitch_odd, upper[1], lower[0])
        inner[at] = upper[0]
        inner[BLOCK + s * 25 : BLOCK + s * 25 + 25] = lower[1]


def load_state(x, state):
    flat = x.reshape(x.shape[0], LANES)
    for e in range(2):
        lanes = slice(e * LANES, (e + 1) * LANES)
        for v in range(5):
            base = var_start(v)
            first = v * 250 + e
            for a in range(5):
                at = base + a * MAIN
                state[at : at + MAIN, lanes] = flat[pl.ds(first + a * 50, MAIN, stride=2), :]
            tail = base + TAIL
            state[tail : tail + 8, lanes] = jnp.zeros((8, LANES), jnp.float32)
            state[tail : tail + 5, lanes] = flat[pl.ds(first + 2 * MAIN, 5, stride=50), :]


def add_axial_terms(gain, state, partial):
    lanes = lax.broadcasted_iota(jnp.int32, (MAIN + 8, LANES), 1)
    rows = lax.broadcasted_iota(jnp.int32, (8, LANES), 0)
    for e in range(2):
        own = slice(e * LANES, (e + 1) * LANES)
        upper_gap, lower_gap = ([], [])
        for v in range(5):
            base = var_start(v)
            lower = state[base : base + MAIN, own]
            upper = state[base + 4 * MAIN : base + TAIL, own]
            tail = state[base + TAIL : base + PER_VAR, own]
            turned = pltpu.roll(tail, 4, 0)
            join = lambda main, end: jnp.concatenate([main, end], axis=0)
            after = pltpu.roll(join(lower, turned), LANES - 1, 1)
            before = pltpu.roll(join(upper, turned), 1, 1)
            upper = join(upper, tail)
            upper_gap.append(jnp.where(lanes == LANES - 1, 0.0, upper - after))
            lower_gap.append(jnp.where(lanes == 0, 0.0, before) - join(lower, tail))
        mixed = []
        for gap, sign in ((upper_gap, -1.0), (lower_gap, 1.0)):
            mixed.append(combine(gain * lift_factor(0) * half_flux(0, sign), gap))
        for v in range(5):
            base = var_start(v)
            upper, lower = (mixed[0][v], mixed[1][v])
            partial[base : base + MAIN, own] += lower[:MAIN]
            partial[base + 4 * MAIN : base + TAIL, own] += upper[:MAIN]
            ends = jnp.where(rows == 0, lower[MAIN:], jnp.where(rows == 4, upper[MAIN:], 0.0))
            partial[base + TAIL : base + PER_VAR, own] += ends


def volume_rate(table, high, low):
    rate = [None] * 5
    for first, start, stop in TILES:
        part = slice(start * PER_VAR, stop * PER_VAR)
        table_high, table_low = (
            table[at + first * PER_VAR : at + ROWS, part] for at in (HIGH_AT, LOW_AT)
        )
        term = product(table_high, high[part], low[part]) + dot(table_low, high[part])
        for v in range(first, 5):
            block = term[(v - first) * PER_VAR : (v - first + 1) * PER_VAR]
            rate[v] = block if rate[v] is None else rate[v] + block
    return jnp.concatenate(rate, axis=0)


def advance_body(section, base, state, table, partial, faces):
    rate = volume_rate(table, *split(state[...]))
    gain, keep = GAIN[section], KEEP[section]
    if keep == 0.0:
        partial[...] = state[...] + rate
    else:
        partial[...] = keep * base[...] + gain * (state[...] + rate)
    add_axial_terms(gain, state, partial)
    if faces is not None:
        faces[...] = product(table[TRACE_AT : TRACE_AT + TRACES], *split(partial[...]))


def lift_table(table):
    return table[LIFT_AT : LIFT_AT + ROWS]


def first_kernel(offsets, x, table, base, partial, faces, flags):
    cols = lax.broadcasted_iota(jnp.int32, flags.shape, 1)
    moved = jnp.zeros(flags.shape, jnp.float32)
    for k in range(3):
        moved = jnp.where((cols == k) & (offsets[k] % 2 == 1), 1.0, moved)
    flags[...] = moved
    load_state(x, base)
    advance_body(0, None, base, table, partial, faces)


def later_kernel(section, base, before, halo_high, halo_low, table, partial, *refs):
    *faces, state = refs
    lifted = product(lift_table(table), halo_high[...], halo_low[...])
    state[...] = before[...] + GAIN[section - 1] * lifted
    advance_body(section, base, state, table, partial, faces[0] if faces else None)


def gather_halo(section, flags, pitch_a, pitch_b, span_a, span_b, inner, halo):
    pitch_odd, span_odd = parities()
    after = jnp.where(pitch_odd, pitch_b[...], pitch_a[...])
    before = jnp.where(pitch_odd, pitch_a[...], pitch_b[...])
    scales = half_scales()
    halo[0:BLOCK, :LANES] = scales[0] * before
    halo[0:BLOCK, LANES:] = scales[0] * inner[0:BLOCK]
    halo[BLOCK : 2 * BLOCK, :LANES] = scales[1] * inner[BLOCK:]
    halo[BLOCK : 2 * BLOCK, LANES:] = scales[1] * after
    above = jnp.where(span_odd, span_b[...], span_a[...])
    below = jnp.where(span_odd, span_a[...], span_b[...])
    place = lax.axis_index("span")
    above = jnp.where(place == lax.axis_size("span") - 1, 0.0, above)
    below = jnp.where(place == 0, 0.0, below)
    rest = jnp.zeros((BLOCK - SPAN_ROWS, 2 * LANES), jnp.float32)
    halo[2 * BLOCK : 2 * BLOCK + SPAN_ROWS] = scales[2] * below
    halo[2 * BLOCK + SPAN_ROWS : 3 * BLOCK] = rest
    halo[3 * BLOCK : 3 * BLOCK + SPAN_ROWS] = scales[3] * above
    halo[3 * BLOCK + SPAN_ROWS : 4 * BLOCK] = rest
    wake = before[WAKE_ROW : WAKE_ROW + 2]
    moved = flags[0:1, section : section + 1] > 0.5
    rows = lax.broadcasted_iota(jnp.int32, (BLOCK, LANES), 0)
    cols = lax.broadcasted_iota(jnp.int32, (BLOCK, LANES), 1)
    for e in range(2):
        row = jnp.where(moved, wake[1 - e : 2 - e], wake[e : e + 1])
        column = jnp.sum(jnp.where(rows == cols, row, 0.0), axis=1, keepdims=True)
        halo[4 * BLOCK :, e * LANES : (e + 1) * LANES] = jnp.where(
            cols == 0, scales[4] * column, 0.0
        )
    return wake


def next_traces(section, side, faces, table, high, low):
    at = LINK_AT + side * 2 * BLOCK
    rows = slice(side * 2 * BLOCK, (side + 1) * 2 * BLOCK)
    return faces[rows] + GAIN[section] * product(table[at : at + 2 * BLOCK], high, low)


def span_kernel(
    section, flags, pitch_a, pitch_b, span_a, span_b, inner, faces, table,
    next_span_a, next_span_b, halo_high, halo_low, wake, halo,
):
    arrived = gather_halo(section, flags, pitch_a, pitch_b, span_a, span_b, inner, halo)
    wake[...] = jnp.concatenate([arrived, jnp.zeros((6, LANES), jnp.float32)], axis=0)
    high, low = split(halo[...])
    halo_high[...] = high
    halo_low[...] = low
    _, span_odd = parities()
    traces = next_traces(section, 1, faces, table, high, low)
    emit_span_faces(traces, span_odd, next_span_a, next_span_b)


def pitch_kernel(
    section, faces, table, halo_high, halo_low, wake, next_pitch_a, next_pitch_b, next_inner
):
    pitch_odd, _ = parities()
    traces = next_traces(section, 0, faces, table, halo_high[...], halo_low[...])
    emit_pitch_faces(
        traces, [wake[0:1], wake[1:2]], pitch_odd, next_pitch_a, next_pitch_b, next_inner
    )


def final_kernel(
    flags, pitch_a, pitch_b, span_a, span_b, inner, before, table, out, halo, result, done
):
    gather_halo(2, flags, pitch_a, pitch_b, span_a, span_b, inner, halo)
    total = before[...] + GAIN[2] * product(lift_table(table), *split(halo[...]))
    flat = result.reshape(result.shape[0], LANES)
    copies = []
    for v in ORDER:
        base = var_start(v)
        for e in range(2):
            lanes = slice(e * LANES, (e + 1) * LANES)
            first = v * 250 + e
            for a in range(5):
                at = base + a * MAIN
                flat[pl.ds(first + a * 50, MAIN, stride=2), :] = total[at : at + MAIN, lanes]
            tail = base + TAIL
            flat[pl.ds(first + 2 * MAIN, 5, stride=50), :] = total[tail : tail + 5, lanes]
        part = pl.ds(v * 250, 250)
        copies.append(pltpu.make_async_copy(result.at[part], out.at[part], done.at[v]))
        copies[-1].start()
    for copy in copies:
        copy.wait()


IN_VMEM = pl.BlockSpec(memory_space=pltpu.VMEM)
IN_SMEM = pl.BlockSpec(memory_space=pltpu.SMEM)


def call(kernel, name, outs, args, in_specs=(), scratch=(), flops=0, out_spec=IN_VMEM):
    in_specs = list(in_specs)
    return pl.pallas_call(
        kernel,
        name=name,
        out_shape=[jax.ShapeDtypeStruct(shape, dtype) for shape, dtype in outs],
        in_specs=in_specs + [IN_VMEM] * (len(args) - len(in_specs)),
        out_specs=[out_spec] * len(outs),
        scratch_shapes=list(scratch),
        compiler_params=pltpu.CompilerParams(vmem_limit_bytes=VMEM_LIMIT),
        cost_estimate=pl.CostEstimate(flops=flops, bytes_accessed=2**20, transcendentals=0),
    )(*args)


def swapped(value, axis, odd):
    pitch, span = (lax.axis_size("pitch"), lax.axis_size("span"))
    pairs = []
    for i in range(pitch):
        for j in range(span):
            if axis == "pitch":
                other = ((i + (1 if i % 2 == odd else -1)) % pitch, j)
            else:
                other = (i, j + (1 if j % 2 == odd else -1))
                if not 0 <= other[1] < span:
                    other = (i ^ 1, j)
            pairs.append((i * span + j, other[0] * span + other[1]))
    return lax.ppermute(value, ("pitch", "span"), pairs)


def span_exchanged(faces):
    return swapped(faces[0], "span", 0), swapped(faces[1], "span", 1)


def pitch_exchanged(faces):
    return swapped(faces[0], "pitch", 0), swapped(faces[1], "pitch", 1)


F32 = jnp.float32
PITCH_OUTS = [((BLOCK, LANES), F32), ((BLOCK, LANES), F32), ((2 * BLOCK, LANES), F32)]
SPAN_OUTS = [((SPAN_ROWS, 2 * LANES), F32)] * 2
SMALL_OUT = ((8, LANES), F32)
HALO_OUTS = [((HALO, 2 * LANES), jnp.bfloat16)] * 2
STATE_OUT = ((ROWS, 2 * LANES), F32)
TRACE_OUT = ((TRACES, 2 * LANES), F32)


def shards(table, state, wake_planes, bar_offsets):
    x = state.reshape(-1, 1, LANES)
    wake = wake_planes.transpose(0, 1, 3, 4, 2).reshape(50, 1, 5)
    faces = call(begin_span_kernel, "begin_span", SPAN_OUTS, [x], flops=10**10)
    span = span_exchanged(faces)
    *faces, inner = call(begin_pitch_kernel, "begin_pitch", PITCH_OUTS, [x, wake], flops=10**10)
    pitch = pitch_exchanged(faces)
    base, partial, traces, flags = call(
        first_kernel,
        "first",
        [STATE_OUT, STATE_OUT, TRACE_OUT, SMALL_OUT],
        [bar_offsets, x, table],
        in_specs=[IN_SMEM],
        flops=10**9,
    )
    for section in range(2):
        *faces, high, low, carried = call(
            functools.partial(span_kernel, section),
            "span_faces",
            SPAN_OUTS + HALO_OUTS + [SMALL_OUT],
            [flags, *pitch, *span, inner, traces, table],
            scratch=[pltpu.VMEM((HALO, 2 * LANES), F32)],
            flops=10**8,
        )
        span = span_exchanged(faces)
        *faces, inner = call(
            functools.partial(pitch_kernel, section),
            "pitch_faces",
            PITCH_OUTS,
            [traces, table, high, low, carried],
            flops=10**8,
        )
        pitch = pitch_exchanged(faces)
        last = section == 1
        partial, *traces = call(
            functools.partial(later_kernel, section + 1),
            "last" if last else "later",
            [STATE_OUT] if last else [STATE_OUT, TRACE_OUT],
            [base, partial, high, low, table],
            scratch=[pltpu.VMEM((ROWS, 2 * LANES), F32)],
            flops=10**9,
        )
        traces = None if last else traces[0]
    (out,) = call(
        final_kernel,
        "final",
        [(x.shape, F32)],
        [flags, *pitch, *span, inner, partial, table],
        scratch=[
            pltpu.VMEM((HALO, 2 * LANES), F32),
            pltpu.VMEM(x.shape, F32),
            pltpu.SemaphoreType.DMA((5,)),
        ],
        flops=10**8,
        out_spec=pl.BlockSpec(memory_space=pl.ANY),
    )
    return out.reshape(state.shape)


def solution(mesh):
    volume, lift, trace, link = operator_tables()
    high, low = split_table(volume)
    table = np.concatenate([exact_table(t) for t in (trace, link, lift)] + [high, low])
    assert table.shape == (TABLE_ROWS, ROWS)
    in_specs = (
        P(None, None, None, None, "pitch", "span", None),
        P(None, None, None, "pitch", "span"),
        P(),
    )
    out_specs = P(None, None, None, None, "pitch", "span", None)
    return jax.shard_map(
        functools.partial(shards, jnp.asarray(table)),
        mesh=mesh,
        in_specs=in_specs,
        out_specs=out_specs,
        check_vma=False,
    )
```

```python
import functools

import jax
import jax.numpy as jnp
import ml_dtypes
import numpy as np
from jax import lax
from jax.experimental import pallas as pl
from jax.experimental.pallas import tpu as pltpu
from jax.sharding import PartitionSpec as P

MEAN_FLOW = (0.5, 0.3, 0.0)
WAVE_SPEED = (1.5, 1.3, 1.0)
ELEM_SIZE = (1.0, 0.8, 1.2)
END_WEIGHT = 0.1
TIME_STEP = 0.01
KEEP = (0.0, 0.75, 1.0 / 3.0)
GAIN = (1.0, 0.25, 2.0 / 3.0)

ORDER = (1, 4, 2, 3, 0)
MAIN = 24
TAIL = 5 * MAIN
PER_VAR = 128
ROWS = 5 * PER_VAR
TILES = ((0, 0, 2), (1, 2, 4), (4, 4, 5))
BLOCK = 128
SPAN_ROWS = 104
TRACES = 4 * BLOCK
HALO = 5 * BLOCK
WAKE_ROW = 125
TRACE_AT, LINK_AT, LIFT_AT = (0, TRACES, 2 * TRACES)
HIGH_AT = LIFT_AT + ROWS
LOW_AT = HIGH_AT + ROWS
TABLE_ROWS = LOW_AT + ROWS
LANES = 128
VMEM_LIMIT = 24 * 1024 * 1024


def derivative_table():
    points = np.array([-1.0, -np.sqrt(3.0 / 7.0), 0.0, np.sqrt(3.0 / 7.0), 1.0])
    products = np.array(
        [np.prod([points[j] - points[k] for k in range(5) if k != j]) for j in range(5)]
    )
    matrix = np.zeros((5, 5))
    for i in range(5):
        for j in range(5):
            if i != j:
                matrix[i, j] = products[i] / (products[j] * (points[i] - points[j]))
        matrix[i, i] = sum((1.0 / (points[i] - points[k]) for k in range(5) if k != i))
    return matrix


def flux_matrix(direction):
    flux = MEAN_FLOW[direction] * np.eye(5)
    flux[0, 1 + direction] += 1.0
    flux[4, 1 + direction] += 1.0
    flux[1 + direction, 4] += 1.0
    return flux


def half_flux(direction, sign):
    return 0.5 * (flux_matrix(direction) + sign * WAVE_SPEED[direction] * np.eye(5))


def lift_factor(direction):
    return TIME_STEP * 2.0 / (ELEM_SIZE[direction] * END_WEIGHT)


def half_scales():
    return (lift_factor(1) / 10.0, lift_factor(1), lift_factor(2), lift_factor(2), lift_factor(0))


def var_start(v):
    return ORDER.index(v) * PER_VAR


def node_row(v, a, p, s):
    node = p * 5 + s
    return var_start(v) + (a * MAIN + node if node < MAIN else TAIL + a)


def operator_tables():
    deriv = derivative_table()
    volume = np.zeros((ROWS, ROWS))
    lift = np.zeros((ROWS, HALO))
    trace = np.zeros((TRACES, ROWS))
    fluxes = [flux_matrix(d) for d in range(3)]
    plus = [half_flux(d, 1.0) for d in range(3)]
    minus = [half_flux(d, -1.0) for d in range(3)]
    plus_sent, minus_sent = (plus[2][:4], minus[2][:4])
    back_plus = np.vstack([np.eye(4), [[0.0, 0.0, 0.0, 1.0]]])
    back_minus = np.vstack([np.eye(4), [[0.0, 0.0, 0.0, -1.0]]])
    assert np.allclose(back_plus @ plus_sent, plus[2])
    assert np.allclose(back_minus @ minus_sent, minus[2])
    for a in range(5):
        for p in range(5):
            for s in range(5):
                here = [node_row(v, a, p, s) for v in range(5)]
                place = (a, p, s)
                for d in range(3):
                    for j in range(5):
                        there = list(place)
                        there[d] = j
                        cols = [node_row(v, *there) for v in range(5)]
                        coeff = -TIME_STEP * (2.0 / ELEM_SIZE[d]) * deriv[place[d], j]
                        volume[np.ix_(here, cols)] += coeff * fluxes[d]
                for d in (1, 2):
                    if place[d] == 4:
                        volume[np.ix_(here, here)] += lift_factor(d) * minus[d]
                    if place[d] == 0:
                        volume[np.ix_(here, here)] -= lift_factor(d) * plus[d]
                if p == 0:
                    cols = [s * 25 + v * 5 + a for v in range(5)]
                    lift[np.ix_(here, cols)] += lift_factor(1) * plus[1]
                    for v in range(5):
                        trace[BLOCK + s * 25 + v * 5 + a, here[v]] = 1.0
                if p == 4:
                    cols = [BLOCK + s * 25 + v * 5 + a for v in range(5)]
                    lift[np.ix_(here, cols)] -= lift_factor(1) * minus[1]
                    for v in range(5):
                        trace[s * 25 + v * 5 + a, here[v]] = 1.0
                if s == 0:
                    cols = [2 * BLOCK + c * 25 + a * 5 + p for c in range(4)]
                    lift[np.ix_(here, cols)] += lift_factor(2) * back_plus
                    rows = [3 * BLOCK + c * 25 + a * 5 + p for c in range(4)]
                    trace[np.ix_(rows, here)] += minus_sent
                if s == 4:
                    cols = [3 * BLOCK + c * 25 + a * 5 + p for c in range(4)]
                    lift[np.ix_(here, cols)] -= lift_factor(2) * back_minus
                    rows = [2 * BLOCK + c * 25 + a * 5 + p for c in range(4)]
                    trace[np.ix_(rows, here)] += plus_sent
                if a == 0:
                    cols = [4 * BLOCK + v * 25 + p * 5 + s for v in range(5)]
                    lift[np.ix_(here, cols)] += lift_factor(0) * plus[0]
    lift = lift / np.repeat(half_scales(), BLOCK)
    return volume, lift, trace, trace @ lift


def exact_table(table):
    exact = table.astype(ml_dtypes.bfloat16)
    assert np.allclose(exact.astype(np.float64), table, rtol=1e-12, atol=1e-12)
    return exact


def split_table(table):
    high = table.astype(ml_dtypes.bfloat16)
    low = (table - high.astype(np.float64)).astype(ml_dtypes.bfloat16)
    return high, low


def split(values):
    high = values.astype(jnp.bfloat16)
    low = (values - high.astype(jnp.float32)).astype(jnp.bfloat16)
    return high, low


def dot(left, right):
    return jnp.dot(left, right, preferred_element_type=jnp.float32)


def product(table, high, low):
    return dot(table, high) + dot(table, low)


def with_rows(values, first, extra):
    rows = lax.broadcasted_iota(jnp.int32, values.shape, 0)
    for k, row in enumerate(extra):
        values = jnp.where(rows == first + k, row, values)
    return values


def emit_pitch_faces(traces, wake, pitch_odd, pitch_a, pitch_b, inner):
    upper, lower = traces[0:BLOCK], traces[BLOCK : 2 * BLOCK]
    up = with_rows(upper[:, LANES:], WAKE_ROW, wake)
    down = lower[:, :LANES]
    pitch_a[...] = jnp.where(pitch_odd, down, up)
    pitch_b[...] = jnp.where(pitch_odd, up, down)
    inner[0:BLOCK] = upper[:, :LANES]
    inner[BLOCK:] = lower[:, LANES:]


def emit_span_faces(traces, span_odd, span_a, span_b):
    above, below = traces[0:SPAN_ROWS], traces[BLOCK : BLOCK + SPAN_ROWS]
    span_a[...] = jnp.where(span_odd, below, above)
    span_b[...] = jnp.where(span_odd, above, below)


def parities():
    return lax.axis_index("pitch") % 2 == 1, lax.axis_index("span") % 2 == 1


def combine(table, values):
    return [
        sum(float(table[i, j]) * values[j] for j in range(5) if table[i, j] != 0.0)
        for i in range(table.shape[0])
    ]


def begin_span_kernel(x, span_a, span_b):
    flat = x.reshape(x.shape[0], LANES)
    _, span_odd = parities()
    rest = jnp.zeros((SPAN_ROWS - 96, LANES), jnp.float32)
    for e in range(2):
        lanes = slice(e * LANES, (e + 1) * LANES)
        sides = []
        for s, sign in ((4, 1.0), (0, -1.0)):
            faces = [flat[pl.ds(v * 250 + 2 * s + e, 25, stride=10), :] for v in range(5)]
            sides.append(combine(half_flux(2, sign)[:4], faces))
        span_a[96:SPAN_ROWS, lanes] = rest
        span_b[96:SPAN_ROWS, lanes] = rest
        for c in range(4):
            above, below = (sides[0][c], sides[1][c])
            span_a[c * 25 : c * 25 + 25, lanes] = jnp.where(span_odd, below, above)
            span_b[c * 25 : c * 25 + 25, lanes] = jnp.where(span_odd, above, below)


def begin_pitch_kernel(x, wake, pitch_a, pitch_b, inner):
    flat = x.reshape(x.shape[0], LANES)
    pitch_odd, _ = parities()
    planes = wake.reshape(50, 5)[...]
    rows = lax.broadcasted_iota(jnp.int32, (50, LANES), 0)
    cols = lax.broadcasted_iota(jnp.int32, (50, LANES), 1)
    spread = jnp.zeros((50, LANES), jnp.float32)
    for s in range(5):
        mine = (cols - s) == 5 * (rows // 2)
        spread = jnp.where(mine, planes[:, s : s + 1], spread)
    own = [
        jnp.sum(jnp.where(rows % 2 == k, spread, 0.0), axis=0, keepdims=True) for k in range(2)
    ]
    tail = jnp.zeros((8, LANES), jnp.float32)
    up_tail = with_rows(tail, WAKE_ROW - 120, own)
    pitch_a[120:BLOCK] = jnp.where(pitch_odd, tail, up_tail)
    pitch_b[120:BLOCK] = jnp.where(pitch_odd, up_tail, tail)
    inner[120:BLOCK] = tail
    inner[BLOCK + 120 :] = tail
    for s in range(5):
        at = slice(s * 25, s * 25 + 25)
        upper, lower = (
            [flat[pl.ds(p * 10 + 2 * s + e, 25, stride=50), :] for e in range(2)] for p in (4, 0)
        )
        pitch_a[at] = jnp.where(pitch_odd, lower[0], upper[1])
        pitch_b[at] = jnp.where(pitch_odd, upper[1], lower[0])
        inner[at] = upper[0]
        inner[BLOCK + s * 25 : BLOCK + s * 25 + 25] = lower[1]


def load_state(x, state):
    flat = x.reshape(x.shape[0], LANES)
    for e in range(2):
        lanes = slice(e * LANES, (e + 1) * LANES)
        for v in range(5):
            base = var_start(v)
            first = v * 250 + e
            for a in range(5):
                at = base + a * MAIN
                state[at : at + MAIN, lanes] = flat[pl.ds(first + a * 50, MAIN, stride=2), :]
            tail = base + TAIL
            state[tail : tail + 8, lanes] = jnp.zeros((8, LANES), jnp.float32)
            state[tail : tail + 5, lanes] = flat[pl.ds(first + 2 * MAIN, 5, stride=50), :]


def add_axial_terms(gain, state, partial):
    lanes = lax.broadcasted_iota(jnp.int32, (MAIN + 8, LANES), 1)
    rows = lax.broadcasted_iota(jnp.int32, (8, LANES), 0)
    for e in range(2):
        own = slice(e * LANES, (e + 1) * LANES)
        upper_gap, lower_gap = ([], [])
        for v in range(5):
            base = var_start(v)
            lower = state[base : base + MAIN, own]
            upper = state[base + 4 * MAIN : base + TAIL, own]
            tail = state[base + TAIL : base + PER_VAR, own]
            turned = pltpu.roll(tail, 4, 0)
            join = lambda main, end: jnp.concatenate([main, end], axis=0)
            after = pltpu.roll(join(lower, turned), LANES - 1, 1)
            before = pltpu.roll(join(upper, turned), 1, 1)
            upper = join(upper, tail)
            upper_gap.append(jnp.where(lanes == LANES - 1, 0.0, upper - after))
            lower_gap.append(jnp.where(lanes == 0, 0.0, before) - join(lower, tail))
        mixed = []
        for gap, sign in ((upper_gap, -1.0), (lower_gap, 1.0)):
            mixed.append(combine(gain * lift_factor(0) * half_flux(0, sign), gap))
        for v in range(5):
            base = var_start(v)
            upper, lower = (mixed[0][v], mixed[1][v])
            partial[base : base + MAIN, own] += lower[:MAIN]
            partial[base + 4 * MAIN : base + TAIL, own] += upper[:MAIN]
            ends = jnp.where(rows == 0, lower[MAIN:], jnp.where(rows == 4, upper[MAIN:], 0.0))
            partial[base + TAIL : base + PER_VAR, own] += ends


def volume_rate(table, high, low):
    rate = [None] * 5
    for first, start, stop in TILES:
        part = slice(start * PER_VAR, stop * PER_VAR)
        table_high, table_low = (
            table[at + first * PER_VAR : at + ROWS, part] for at in (HIGH_AT, LOW_AT)
        )
        term = product(table_high, high[part], low[part]) + dot(table_low, high[part])
        for v in range(first, 5):
            block = term[(v - first) * PER_VAR : (v - first + 1) * PER_VAR]
            rate[v] = block if rate[v] is None else rate[v] + block
    return jnp.concatenate(rate, axis=0)


def advance_body(section, base, state, table, partial, faces):
    rate = volume_rate(table, *split(state[...]))
    gain, keep = GAIN[section], KEEP[section]
    if keep == 0.0:
        partial[...] = state[...] + rate
    else:
        partial[...] = keep * base[...] + gain * (state[...] + rate)
    add_axial_terms(gain, state, partial)
    if faces is not None:
        faces[...] = product(table[TRACE_AT : TRACE_AT + TRACES], *split(partial[...]))


def lift_table(table):
    return table[LIFT_AT : LIFT_AT + ROWS]


def first_kernel(offsets, x, table, base, partial, faces, flags):
    cols = lax.broadcasted_iota(jnp.int32, flags.shape, 1)
    moved = jnp.zeros(flags.shape, jnp.float32)
    for k in range(3):
        moved = jnp.where((cols == k) & (offsets[k] % 2 == 1), 1.0, moved)
    flags[...] = moved
    load_state(x, base)
    advance_body(0, None, base, table, partial, faces)


def later_kernel(section, base, before, halo_high, halo_low, table, partial, *refs):
    *faces, state = refs
    lifted = product(lift_table(table), halo_high[...], halo_low[...])
    state[...] = before[...] + GAIN[section - 1] * lifted
    advance_body(section, base, state, table, partial, faces[0] if faces else None)


def gather_halo(section, flags, pitch_a, pitch_b, span_a, span_b, inner, halo):
    pitch_odd, span_odd = parities()
    after = jnp.where(pitch_odd, pitch_b[...], pitch_a[...])
    before = jnp.where(pitch_odd, pitch_a[...], pitch_b[...])
    scales = half_scales()
    halo[0:BLOCK, :LANES] = scales[0] * before
    halo[0:BLOCK, LANES:] = scales[0] * inner[0:BLOCK]
    halo[BLOCK : 2 * BLOCK, :LANES] = scales[1] * inner[BLOCK:]
    halo[BLOCK : 2 * BLOCK, LANES:] = scales[1] * after
    above = jnp.where(span_odd, span_b[...], span_a[...])
    below = jnp.where(span_odd, span_a[...], span_b[...])
    place = lax.axis_index("span")
    above = jnp.where(place == lax.axis_size("span") - 1, 0.0, above)
    below = jnp.where(place == 0, 0.0, below)
    rest = jnp.zeros((BLOCK - SPAN_ROWS, 2 * LANES), jnp.float32)
    halo[2 * BLOCK : 2 * BLOCK + SPAN_ROWS] = scales[2] * below
    halo[2 * BLOCK + SPAN_ROWS : 3 * BLOCK] = rest
    halo[3 * BLOCK : 3 * BLOCK + SPAN_ROWS] = scales[3] * above
    halo[3 * BLOCK + SPAN_ROWS : 4 * BLOCK] = rest
    wake = before[WAKE_ROW : WAKE_ROW + 2]
    moved = flags[0:1, section : section + 1] > 0.5
    rows = lax.broadcasted_iota(jnp.int32, (BLOCK, LANES), 0)
    cols = lax.broadcasted_iota(jnp.int32, (BLOCK, LANES), 1)
    for e in range(2):
        row = jnp.where(moved, wake[1 - e : 2 - e], wake[e : e + 1])
        column = jnp.sum(jnp.where(rows == cols, row, 0.0), axis=1, keepdims=True)
        halo[4 * BLOCK :, e * LANES : (e + 1) * LANES] = jnp.where(
            cols == 0, scales[4] * column, 0.0
        )
    return wake


def next_traces(section, side, faces, table, high, low):
    at = LINK_AT + side * 2 * BLOCK
    rows = slice(side * 2 * BLOCK, (side + 1) * 2 * BLOCK)
    return faces[rows] + GAIN[section] * product(table[at : at + 2 * BLOCK], high, low)


def span_kernel(
    section, flags, pitch_b, pitch_a, span_a, span_b, inner, faces, table,
    next_span_a, next_span_b, halo_high, halo_low, wake, halo,
):
    arrived = gather_halo(section, flags, pitch_a, pitch_b, span_a, span_b, inner, halo)
    wake[...] = jnp.concatenate([arrived, jnp.zeros((6, LANES), jnp.float32)], axis=0)
    high, low = split(halo[...])
    halo_high[...] = high
    halo_low[...] = low
    _, span_odd = parities()
    traces = next_traces(section, 1, faces, table, high, low)
    emit_span_faces(traces, span_odd, next_span_a, next_span_b)


def pitch_kernel(
    section, faces, table, halo_high, halo_low, wake, next_pitch_a, next_pitch_b, next_inner
):
    pitch_odd, _ = parities()
    traces = next_traces(section, 0, faces, table, halo_high[...], halo_low[...])
    emit_pitch_faces(
        traces, [wake[0:1], wake[1:2]], pitch_odd, next_pitch_a, next_pitch_b, next_inner
    )


def final_kernel(
    flags, pitch_b, pitch_a, span_a, span_b, inner, before, table, out, halo, result, done
):
    gather_halo(2, flags, pitch_a, pitch_b, span_a, span_b, inner, halo)
    total = before[...] + GAIN[2] * product(lift_table(table), *split(halo[...]))
    flat = result.reshape(result.shape[0], LANES)
    copies = []
    for v in ORDER:
        base = var_start(v)
        for e in range(2):
            lanes = slice(e * LANES, (e + 1) * LANES)
            first = v * 250 + e
            for a in range(5):
                at = base + a * MAIN
                flat[pl.ds(first + a * 50, MAIN, stride=2), :] = total[at : at + MAIN, lanes]
            tail = base + TAIL
            flat[pl.ds(first + 2 * MAIN, 5, stride=50), :] = total[tail : tail + 5, lanes]
        part = pl.ds(v * 250, 250)
        copies.append(pltpu.make_async_copy(result.at[part], out.at[part], done.at[v]))
        copies[-1].start()
    for copy in copies:
        copy.wait()


IN_VMEM = pl.BlockSpec(memory_space=pltpu.VMEM)
IN_SMEM = pl.BlockSpec(memory_space=pltpu.SMEM)


def call(kernel, name, outs, args, in_specs=(), scratch=(), flops=0, out_spec=IN_VMEM):
    in_specs = list(in_specs)
    return pl.pallas_call(
        kernel,
        name=name,
        out_shape=[jax.ShapeDtypeStruct(shape, dtype) for shape, dtype in outs],
        in_specs=in_specs + [IN_VMEM] * (len(args) - len(in_specs)),
        out_specs=[out_spec] * len(outs),
        scratch_shapes=list(scratch),
        compiler_params=pltpu.CompilerParams(vmem_limit_bytes=VMEM_LIMIT),
        cost_estimate=pl.CostEstimate(flops=flops, bytes_accessed=2**20, transcendentals=0),
    )(*args)


def swapped(value, axis, odd):
    pitch, span = (lax.axis_size("pitch"), lax.axis_size("span"))
    pairs = []
    for i in range(pitch):
        for j in range(span):
            if axis == "pitch":
                other = ((i + (1 if i % 2 == odd else -1)) % pitch, j)
            else:
                other = (i, j + (1 if j % 2 == odd else -1))
                if not 0 <= other[1] < span:
                    other = (i ^ 1, j)
            pairs.append((i * span + j, other[0] * span + other[1]))
    return lax.ppermute(value, ("pitch", "span"), pairs)


def span_exchanged(faces):
    return swapped(faces[0], "span", 0), swapped(faces[1], "span", 1)


def pitch_exchanged(faces):
    return swapped(faces[1], "pitch", 1), swapped(faces[0], "pitch", 0)


F32 = jnp.float32
PITCH_OUTS = [((BLOCK, LANES), F32), ((BLOCK, LANES), F32), ((2 * BLOCK, LANES), F32)]
SPAN_OUTS = [((SPAN_ROWS, 2 * LANES), F32)] * 2
SMALL_OUT = ((8, LANES), F32)
HALO_OUTS = [((HALO, 2 * LANES), jnp.bfloat16)] * 2
STATE_OUT = ((ROWS, 2 * LANES), F32)
TRACE_OUT = ((TRACES, 2 * LANES), F32)


def shards(table, state, wake_planes, bar_offsets):
    x = state.reshape(-1, 1, LANES)
    wake = wake_planes.transpose(0, 1, 3, 4, 2).reshape(50, 1, 5)
    faces = call(begin_span_kernel, "begin_span", SPAN_OUTS, [x], flops=10**10)
    span = span_exchanged(faces)
    *faces, inner = call(begin_pitch_kernel, "begin_pitch", PITCH_OUTS, [x, wake], flops=10**10)
    pitch = pitch_exchanged(faces)
    base, partial, traces, flags = call(
        first_kernel,
        "first",
        [STATE_OUT, STATE_OUT, TRACE_OUT, SMALL_OUT],
        [bar_offsets, x, table],
        in_specs=[IN_SMEM],
        flops=10**9,
    )
    for section in range(2):
        *faces, high, low, carried = call(
            functools.partial(span_kernel, section),
            "span_faces",
            SPAN_OUTS + HALO_OUTS + [SMALL_OUT],
            [flags, *pitch, *span, inner, traces, table],
            scratch=[pltpu.VMEM((HALO, 2 * LANES), F32)],
            flops=10**8,
        )
        span = span_exchanged(faces)
        *faces, inner = call(
            functools.partial(pitch_kernel, section),
            "pitch_faces",
            PITCH_OUTS,
            [traces, table, high, low, carried],
            flops=10**8,
        )
        pitch = pitch_exchanged(faces)
        last = section == 1
        partial, *traces = call(
            functools.partial(later_kernel, section + 1),
            "last" if last else "later",
            [STATE_OUT] if last else [STATE_OUT, TRACE_OUT],
            [base, partial, high, low, table],
            scratch=[pltpu.VMEM((ROWS, 2 * LANES), F32)],
            flops=10**9,
        )
        traces = None if last else traces[0]
    (out,) = call(
        final_kernel,
        "final",
        [(x.shape, F32)],
        [flags, *pitch, *span, inner, partial, table],
        scratch=[
            pltpu.VMEM((HALO, 2 * LANES), F32),
            pltpu.VMEM(x.shape, F32),
            pltpu.SemaphoreType.DMA((5,)),
        ],
        flops=10**8,
        out_spec=pl.BlockSpec(memory_space=pl.ANY),
    )
    return out.reshape(state.shape)


def solution(mesh):
    volume, lift, trace, link = operator_tables()
    high, low = split_table(volume)
    table = np.concatenate([exact_table(t) for t in (trace, link, lift)] + [high, low])
    assert table.shape == (TABLE_ROWS, ROWS)
    in_specs = (
        P(None, None, None, None, "pitch", "span", None),
        P(None, None, None, "pitch", "span"),
        P(),
    )
    out_specs = P(None, None, None, None, "pitch", "span", None)
    return jax.shard_map(
        functools.partial(shards, jnp.asarray(table)),
        mesh=mesh,
        in_specs=in_specs,
        out_specs=out_specs,
        check_vma=False,
    )
```

```python
import functools

import jax
import jax.numpy as jnp
import ml_dtypes
import numpy as np
from jax import lax
from jax.experimental import pallas as pl
from jax.experimental.pallas import tpu as pltpu
from jax.sharding import PartitionSpec as P

MEAN_FLOW = (0.5, 0.3, 0.0)
WAVE_SPEED = (1.5, 1.3, 1.0)
ELEM_SIZE = (1.0, 0.8, 1.2)
END_WEIGHT = 0.1
TIME_STEP = 0.01
KEEP = (0.0, 0.75, 1.0 / 3.0)
GAIN = (1.0, 0.25, 2.0 / 3.0)

ORDER = (1, 4, 2, 3, 0)
MAIN = 24
TAIL = 5 * MAIN
PER_VAR = 128
ROWS = 5 * PER_VAR
FINAL_GROUPS = ((0, 1), (2, 3, 4))
TILES = ((0, 0, 2), (1, 2, 4), (4, 4, 5))
BLOCK = 128
SPAN_ROWS = 104
TRACES = 4 * BLOCK
HALO = 5 * BLOCK
WAKE_ROW = 125
TRACE_AT, LINK_AT, LIFT_AT = (0, TRACES, 2 * TRACES)
HIGH_AT = LIFT_AT + ROWS
LOW_AT = HIGH_AT + ROWS
TABLE_ROWS = LOW_AT + ROWS
LANES = 128
VMEM_LIMIT = 24 * 1024 * 1024


def derivative_table():
    points = np.array([-1.0, -np.sqrt(3.0 / 7.0), 0.0, np.sqrt(3.0 / 7.0), 1.0])
    products = np.array(
        [np.prod([points[j] - points[k] for k in range(5) if k != j]) for j in range(5)]
    )
    matrix = np.zeros((5, 5))
    for i in range(5):
        for j in range(5):
            if i != j:
                matrix[i, j] = products[i] / (products[j] * (points[i] - points[j]))
        matrix[i, i] = sum((1.0 / (points[i] - points[k]) for k in range(5) if k != i))
    return matrix


def flux_matrix(direction):
    flux = MEAN_FLOW[direction] * np.eye(5)
    flux[0, 1 + direction] += 1.0
    flux[4, 1 + direction] += 1.0
    flux[1 + direction, 4] += 1.0
    return flux


def half_flux(direction, sign):
    return 0.5 * (flux_matrix(direction) + sign * WAVE_SPEED[direction] * np.eye(5))


def lift_factor(direction):
    return TIME_STEP * 2.0 / (ELEM_SIZE[direction] * END_WEIGHT)


def half_scales():
    return (lift_factor(1) / 10.0, lift_factor(1), lift_factor(2), lift_factor(2), lift_factor(0))


def var_start(v):
    return ORDER.index(v) * PER_VAR


def node_row(v, a, p, s):
    node = p * 5 + s
    return var_start(v) + (a * MAIN + node if node < MAIN else TAIL + a)


def operator_tables():
    deriv = derivative_table()
    volume = np.zeros((ROWS, ROWS))
    lift = np.zeros((ROWS, HALO))
    trace = np.zeros((TRACES, ROWS))
    fluxes = [flux_matrix(d) for d in range(3)]
    plus = [half_flux(d, 1.0) for d in range(3)]
    minus = [half_flux(d, -1.0) for d in range(3)]
    plus_sent, minus_sent = (plus[2][:4], minus[2][:4])
    back_plus = np.vstack([np.eye(4), [[0.0, 0.0, 0.0, 1.0]]])
    back_minus = np.vstack([np.eye(4), [[0.0, 0.0, 0.0, -1.0]]])
    assert np.allclose(back_plus @ plus_sent, plus[2])
    assert np.allclose(back_minus @ minus_sent, minus[2])
    for a in range(5):
        for p in range(5):
            for s in range(5):
                here = [node_row(v, a, p, s) for v in range(5)]
                place = (a, p, s)
                for d in range(3):
                    for j in range(5):
                        there = list(place)
                        there[d] = j
                        cols = [node_row(v, *there) for v in range(5)]
                        coeff = -TIME_STEP * (2.0 / ELEM_SIZE[d]) * deriv[place[d], j]
                        volume[np.ix_(here, cols)] += coeff * fluxes[d]
                for d in (1, 2):
                    if place[d] == 4:
                        volume[np.ix_(here, here)] += lift_factor(d) * minus[d]
                    if place[d] == 0:
                        volume[np.ix_(here, here)] -= lift_factor(d) * plus[d]
                if p == 0:
                    cols = [s * 25 + v * 5 + a for v in range(5)]
                    lift[np.ix_(here, cols)] += lift_factor(1) * plus[1]
                    for v in range(5):
                        trace[BLOCK + s * 25 + v * 5 + a, here[v]] = 1.0
                if p == 4:
                    cols = [BLOCK + s * 25 + v * 5 + a for v in range(5)]
                    lift[np.ix_(here, cols)] -= lift_factor(1) * minus[1]
                    for v in range(5):
                        trace[s * 25 + v * 5 + a, here[v]] = 1.0
                if s == 0:
                    cols = [2 * BLOCK + c * 25 + a * 5 + p for c in range(4)]
                    lift[np.ix_(here, cols)] += lift_factor(2) * back_plus
                    rows = [3 * BLOCK + c * 25 + a * 5 + p for c in range(4)]
                    trace[np.ix_(rows, here)] += minus_sent
                if s == 4:
                    cols = [3 * BLOCK + c * 25 + a * 5 + p for c in range(4)]
                    lift[np.ix_(here, cols)] -= lift_factor(2) * back_minus
                    rows = [2 * BLOCK + c * 25 + a * 5 + p for c in range(4)]
                    trace[np.ix_(rows, here)] += plus_sent
                if a == 0:
                    cols = [4 * BLOCK + v * 25 + p * 5 + s for v in range(5)]
                    lift[np.ix_(here, cols)] += lift_factor(0) * plus[0]
    lift = lift / np.repeat(half_scales(), BLOCK)
    return volume, lift, trace, trace @ lift


def exact_table(table):
    exact = table.astype(ml_dtypes.bfloat16)
    assert np.allclose(exact.astype(np.float64), table, rtol=1e-12, atol=1e-12)
    return exact


def split_table(table):
    high = table.astype(ml_dtypes.bfloat16)
    low = (table - high.astype(np.float64)).astype(ml_dtypes.bfloat16)
    return high, low


def split(values):
    high = values.astype(jnp.bfloat16)
    low = (values - high.astype(jnp.float32)).astype(jnp.bfloat16)
    return high, low


def dot(left, right):
    return jnp.dot(left, right, preferred_element_type=jnp.float32)


def product(table, high, low):
    return dot(table, high) + dot(table, low)


def with_rows(values, first, extra):
    rows = lax.broadcasted_iota(jnp.int32, values.shape, 0)
    for k, row in enumerate(extra):
        values = jnp.where(rows == first + k, row, values)
    return values


def emit_pitch_faces(traces, wake, pitch_odd, pitch_a, pitch_b, inner):
    upper, lower = traces[0:BLOCK], traces[BLOCK : 2 * BLOCK]
    up = with_rows(upper[:, LANES:], WAKE_ROW, wake)
    down = lower[:, :LANES]
    pitch_a[...] = jnp.where(pitch_odd, down, up)
    pitch_b[...] = jnp.where(pitch_odd, up, down)
    inner[0:BLOCK] = upper[:, :LANES]
    inner[BLOCK:] = lower[:, LANES:]


def emit_span_faces(traces, span_odd, span_a, span_b):
    above, below = traces[0:SPAN_ROWS], traces[BLOCK : BLOCK + SPAN_ROWS]
    span_a[...] = jnp.where(span_odd, below, above)
    span_b[...] = jnp.where(span_odd, above, below)


def parities():
    return lax.axis_index("pitch") % 2 == 1, lax.axis_index("span") % 2 == 1


def combine(table, values):
    return [
        sum(float(table[i, j]) * values[j] for j in range(5) if table[i, j] != 0.0)
        for i in range(table.shape[0])
    ]


def begin_span_kernel(x, span_a, span_b):
    flat = x.reshape(x.shape[0], LANES)
    _, span_odd = parities()
    rest = jnp.zeros((SPAN_ROWS - 96, LANES), jnp.float32)
    for e in range(2):
        lanes = slice(e * LANES, (e + 1) * LANES)
        sides = []
        for s, sign in ((4, 1.0), (0, -1.0)):
            faces = [flat[pl.ds(v * 250 + 2 * s + e, 25, stride=10), :] for v in range(5)]
            sides.append(combine(half_flux(2, sign)[:4], faces))
        span_a[96:SPAN_ROWS, lanes] = rest
        span_b[96:SPAN_ROWS, lanes] = rest
        for c in range(4):
            above, below = (sides[0][c], sides[1][c])
            span_a[c * 25 : c * 25 + 25, lanes] = jnp.where(span_odd, below, above)
            span_b[c * 25 : c * 25 + 25, lanes] = jnp.where(span_odd, above, below)


def begin_pitch_kernel(x, wake, pitch_a, pitch_b, inner):
    flat = x.reshape(x.shape[0], LANES)
    pitch_odd, _ = parities()
    planes = wake.reshape(50, 5)[...]
    rows = lax.broadcasted_iota(jnp.int32, (50, LANES), 0)
    cols = lax.broadcasted_iota(jnp.int32, (50, LANES), 1)
    spread = jnp.zeros((50, LANES), jnp.float32)
    for s in range(5):
        mine = (cols - s) == 5 * (rows // 2)
        spread = jnp.where(mine, planes[:, s : s + 1], spread)
    own = [
        jnp.sum(jnp.where(rows % 2 == k, spread, 0.0), axis=0, keepdims=True) for k in range(2)
    ]
    tail = jnp.zeros((8, LANES), jnp.float32)
    up_tail = with_rows(tail, WAKE_ROW - 120, own)
    pitch_a[120:BLOCK] = jnp.where(pitch_odd, tail, up_tail)
    pitch_b[120:BLOCK] = jnp.where(pitch_odd, up_tail, tail)
    inner[120:BLOCK] = tail
    inner[BLOCK + 120 :] = tail
    for s in range(5):
        at = slice(s * 25, s * 25 + 25)
        upper, lower = (
            [flat[pl.ds(p * 10 + 2 * s + e, 25, stride=50), :] for e in range(2)] for p in (4, 0)
        )
        pitch_a[at] = jnp.where(pitch_odd, lower[0], upper[1])
        pitch_b[at] = jnp.where(pitch_odd, upper[1], lower[0])
        inner[at] = upper[0]
        inner[BLOCK + s * 25 : BLOCK + s * 25 + 25] = lower[1]


def load_state(x, state):
    flat = x.reshape(x.shape[0], LANES)
    for e in range(2):
        lanes = slice(e * LANES, (e + 1) * LANES)
        for v in range(5):
            base = var_start(v)
            first = v * 250 + e
            for a in range(5):
                at = base + a * MAIN
                state[at : at + MAIN, lanes] = flat[pl.ds(first + a * 50, MAIN, stride=2), :]
            tail = base + TAIL
            state[tail : tail + 8, lanes] = jnp.zeros((8, LANES), jnp.float32)
            state[tail : tail + 5, lanes] = flat[pl.ds(first + 2 * MAIN, 5, stride=50), :]


def add_axial_terms(gain, state, partial):
    lanes = lax.broadcasted_iota(jnp.int32, (MAIN + 8, LANES), 1)
    rows = lax.broadcasted_iota(jnp.int32, (8, LANES), 0)
    for e in range(2):
        own = slice(e * LANES, (e + 1) * LANES)
        upper_gap, lower_gap = ([], [])
        for v in range(5):
            base = var_start(v)
            lower = state[base : base + MAIN, own]
            upper = state[base + 4 * MAIN : base + TAIL, own]
            tail = state[base + TAIL : base + PER_VAR, own]
            turned = pltpu.roll(tail, 4, 0)
            join = lambda main, end: jnp.concatenate([main, end], axis=0)
            after = pltpu.roll(join(lower, turned), LANES - 1, 1)
            before = pltpu.roll(join(upper, turned), 1, 1)
            upper = join(upper, tail)
            upper_gap.append(jnp.where(lanes == LANES - 1, 0.0, upper - after))
            lower_gap.append(jnp.where(lanes == 0, 0.0, before) - join(lower, tail))
        mixed = []
        for gap, sign in ((upper_gap, -1.0), (lower_gap, 1.0)):
            mixed.append(combine(gain * lift_factor(0) * half_flux(0, sign), gap))
        for v in range(5):
            base = var_start(v)
            upper, lower = (mixed[0][v], mixed[1][v])
            partial[base : base + MAIN, own] += lower[:MAIN]
            partial[base + 4 * MAIN : base + TAIL, own] += upper[:MAIN]
            ends = jnp.where(rows == 0, lower[MAIN:], jnp.where(rows == 4, upper[MAIN:], 0.0))
            partial[base + TAIL : base + PER_VAR, own] += ends


def volume_rate(table, high, low):
    rate = [None] * 5
    for first, start, stop in TILES:
        part = slice(start * PER_VAR, stop * PER_VAR)
        table_high, table_low = (
            table[at + first * PER_VAR : at + ROWS, part] for at in (HIGH_AT, LOW_AT)
        )
        term = product(table_high, high[part], low[part]) + dot(table_low, high[part])
        for v in range(first, 5):
            block = term[(v - first) * PER_VAR : (v - first + 1) * PER_VAR]
            rate[v] = block if rate[v] is None else rate[v] + block
    return jnp.concatenate(rate, axis=0)


def advance_body(section, base, state, table, partial, faces):
    rate = volume_rate(table, *split(state[...]))
    gain, keep = GAIN[section], KEEP[section]
    if keep == 0.0:
        partial[...] = state[...] + rate
    else:
        partial[...] = keep * base[...] + gain * (state[...] + rate)
    add_axial_terms(gain, state, partial)
    if faces is not None:
        faces[...] = product(table[TRACE_AT : TRACE_AT + TRACES], *split(partial[...]))


def lift_table(table):
    return table[LIFT_AT : LIFT_AT + ROWS]


def first_kernel(offsets, x, table, base, partial, faces, flags):
    cols = lax.broadcasted_iota(jnp.int32, flags.shape, 1)
    moved = jnp.zeros(flags.shape, jnp.float32)
    for k in range(3):
        moved = jnp.where((cols == k) & (offsets[k] % 2 == 1), 1.0, moved)
    flags[...] = moved
    load_state(x, base)
    advance_body(0, None, base, table, partial, faces)


def later_kernel(section, base, before, halo_high, halo_low, table, partial, *refs):
    *faces, state = refs
    lifted = product(lift_table(table), halo_high[...], halo_low[...])
    state[...] = before[...] + GAIN[section - 1] * lifted
    advance_body(section, base, state, table, partial, faces[0] if faces else None)


def gather_halo(section, flags, pitch_a, pitch_b, span_a, span_b, inner, halo_high, halo_low):
    def put(block, first, values):
        at = (slice(block * BLOCK, (block + 1) * BLOCK), slice(first, first + values.shape[1]))
        halo_high[at], halo_low[at] = split(half_scales()[block] * values)

    pitch_odd, span_odd = parities()
    after = jnp.where(pitch_odd, pitch_b[...], pitch_a[...])
    before = jnp.where(pitch_odd, pitch_a[...], pitch_b[...])
    put(0, 0, before)
    put(0, LANES, inner[0:BLOCK])
    put(1, 0, inner[BLOCK:])
    put(1, LANES, after)
    above = jnp.where(span_odd, span_b[...], span_a[...])
    below = jnp.where(span_odd, span_a[...], span_b[...])
    place = lax.axis_index("span")
    above = jnp.where(place == lax.axis_size("span") - 1, 0.0, above)
    below = jnp.where(place == 0, 0.0, below)
    rest = jnp.zeros((BLOCK - SPAN_ROWS, 2 * LANES), jnp.float32)
    put(2, 0, jnp.concatenate([below, rest], axis=0))
    put(3, 0, jnp.concatenate([above, rest], axis=0))
    wake = before[WAKE_ROW : WAKE_ROW + 2]
    moved = flags[0:1, section : section + 1] > 0.5
    rows = lax.broadcasted_iota(jnp.int32, (BLOCK, LANES), 0)
    cols = lax.broadcasted_iota(jnp.int32, (BLOCK, LANES), 1)
    for e in range(2):
        row = jnp.where(moved, wake[1 - e : 2 - e], wake[e : e + 1])
        column = jnp.sum(jnp.where(rows == cols, row, 0.0), axis=1, keepdims=True)
        put(4, e * LANES, jnp.where(cols == 0, column, 0.0))
    return wake


def next_traces(section, side, faces, table, high, low):
    at = LINK_AT + side * 2 * BLOCK
    rows = slice(side * 2 * BLOCK, (side + 1) * 2 * BLOCK)
    return faces[rows] + GAIN[section] * dot(table[at : at + 2 * BLOCK], high)


def exchange_kernel(
    section, flags, span_a, span_b, pitch_b, pitch_a, inner, faces, table,
    next_pitch_a, next_pitch_b, next_inner, next_span_a, next_span_b, halo_high, halo_low,
):
    wake = gather_halo(
        section, flags, pitch_a, pitch_b, span_a, span_b, inner, halo_high, halo_low
    )
    pitch_odd, span_odd = parities()
    traces = faces[...] + GAIN[section] * dot(
        table[LINK_AT : LINK_AT + TRACES], halo_high[...]
    )
    emit_span_faces(traces[2 * BLOCK :], span_odd, next_span_a, next_span_b)
    emit_pitch_faces(
        traces, [wake[0:1], wake[1:2]], pitch_odd, next_pitch_a, next_pitch_b, next_inner
    )


def final_kernel(
    flags, span_a, span_b, pitch_b, pitch_a, inner, before, table, out,
    halo_high, halo_low, result, done,
):
    gather_halo(2, flags, pitch_a, pitch_b, span_a, span_b, inner, halo_high, halo_low)
    flat = result.reshape(result.shape[0], LANES)
    copies = []
    for group in FINAL_GROUPS:
        start, stop = (group[0] * PER_VAR, (group[-1] + 1) * PER_VAR)
        lifted = product(
            table[LIFT_AT + start : LIFT_AT + stop], halo_high[...], halo_low[...]
        )
        total = before[start:stop] + GAIN[2] * lifted
        for place in group:
            v, base = (ORDER[place], place * PER_VAR - start)
            for e in range(2):
                lanes = slice(e * LANES, (e + 1) * LANES)
                first = v * 250 + e
                for a in range(5):
                    at = base + a * MAIN
                    flat[pl.ds(first + a * 50, MAIN, stride=2), :] = total[at : at + MAIN, lanes]
                tail = base + TAIL
                flat[pl.ds(first + 2 * MAIN, 5, stride=50), :] = total[tail : tail + 5, lanes]
            part = pl.ds(v * 250, 250)
            copies.append(pltpu.make_async_copy(result.at[part], out.at[part], done.at[v]))
            copies[-1].start()
    for copy in copies:
        copy.wait()


IN_VMEM = pl.BlockSpec(memory_space=pltpu.VMEM)
IN_SMEM = pl.BlockSpec(memory_space=pltpu.SMEM)


def call(kernel, name, outs, args, in_specs=(), scratch=(), flops=0, out_spec=IN_VMEM):
    in_specs = list(in_specs)
    return pl.pallas_call(
        kernel,
        name=name,
        out_shape=[jax.ShapeDtypeStruct(shape, dtype) for shape, dtype in outs],
        in_specs=in_specs + [IN_VMEM] * (len(args) - len(in_specs)),
        out_specs=[out_spec] * len(outs),
        scratch_shapes=list(scratch),
        compiler_params=pltpu.CompilerParams(vmem_limit_bytes=VMEM_LIMIT),
        cost_estimate=pl.CostEstimate(flops=flops, bytes_accessed=2**20, transcendentals=0),
    )(*args)


def swapped(value, axis, odd):
    pitch, span = (lax.axis_size("pitch"), lax.axis_size("span"))
    pairs = []
    for i in range(pitch):
        for j in range(span):
            if axis == "pitch":
                other = ((i + (1 if i % 2 == odd else -1)) % pitch, j)
            else:
                other = (i, j + (1 if j % 2 == odd else -1))
                if not 0 <= other[1] < span:
                    other = (i ^ 1, j)
            pairs.append((i * span + j, other[0] * span + other[1]))
    return lax.ppermute(value, ("pitch", "span"), pairs)


def span_exchanged(faces):
    return swapped(faces[0], "span", 0), swapped(faces[1], "span", 1)


def pitch_exchanged(faces):
    return swapped(faces[1], "pitch", 1), swapped(faces[0], "pitch", 0)


F32 = jnp.float32
PITCH_OUTS = [((BLOCK, LANES), F32), ((BLOCK, LANES), F32), ((2 * BLOCK, LANES), F32)]
SPAN_OUTS = [((SPAN_ROWS, 2 * LANES), F32)] * 2
SMALL_OUT = ((8, LANES), F32)
HALO_OUTS = [((HALO, 2 * LANES), jnp.bfloat16)] * 2
STATE_OUT = ((ROWS, 2 * LANES), F32)
TRACE_OUT = ((TRACES, 2 * LANES), F32)


def shards(table, state, wake_planes, bar_offsets):
    x = state.reshape(-1, 1, LANES)
    wake = wake_planes.transpose(0, 1, 3, 4, 2).reshape(50, 1, 5)
    faces = call(begin_span_kernel, "begin_span", SPAN_OUTS, [x], flops=10**10)
    span = span_exchanged(faces)
    *faces, inner = call(begin_pitch_kernel, "begin_pitch", PITCH_OUTS, [x, wake], flops=10**10)
    pitch = pitch_exchanged(faces)
    base, partial, traces, flags = call(
        first_kernel,
        "first",
        [STATE_OUT, STATE_OUT, TRACE_OUT, SMALL_OUT],
        [bar_offsets, x, table],
        in_specs=[IN_SMEM],
        flops=10**9,
    )
    for section in range(2):
        next_a, next_b, inner, *faces, high, low = call(
            functools.partial(exchange_kernel, section),
            "exchange",
            PITCH_OUTS + SPAN_OUTS + HALO_OUTS,
            [flags, span[0], span[1], pitch[0], pitch[1], inner, traces, table],
            flops=10**8,
        )
        span = span_exchanged(faces)
        pitch = pitch_exchanged([next_a, next_b])
        last = section == 1
        partial, *traces = call(
            functools.partial(later_kernel, section + 1),
            "last" if last else "later",
            [STATE_OUT] if last else [STATE_OUT, TRACE_OUT],
            [base, partial, high, low, table],
            scratch=[pltpu.VMEM((ROWS, 2 * LANES), F32)],
            flops=10**9,
        )
        traces = None if last else traces[0]
    (out,) = call(
        final_kernel,
        "final",
        [(x.shape, F32)],
        [flags, span[0], span[1], pitch[0], pitch[1], inner, partial, table],
        scratch=[
            *[pltpu.VMEM(shape, dtype) for shape, dtype in HALO_OUTS],
            pltpu.VMEM(x.shape, F32),
            pltpu.SemaphoreType.DMA((5,)),
        ],
        flops=10**8,
        out_spec=pl.BlockSpec(memory_space=pl.ANY),
    )
    return out.reshape(state.shape)


def solution(mesh):
    volume, lift, trace, link = operator_tables()
    high, low = split_table(volume)
    table = np.concatenate([exact_table(t) for t in (trace, link, lift)] + [high, low])
    assert table.shape == (TABLE_ROWS, ROWS)
    in_specs = (
        P(None, None, None, None, "pitch", "span", None),
        P(None, None, None, "pitch", "span"),
        P(),
    )
    out_specs = P(None, None, None, None, "pitch", "span", None)
    return jax.shard_map(
        functools.partial(shards, jnp.asarray(table)),
        mesh=mesh,
        in_specs=in_specs,
        out_specs=out_specs,
        check_vma=False,
    )
```

```python
import functools

import jax
import jax.numpy as jnp
import ml_dtypes
import numpy as np
from jax import lax
from jax.experimental import pallas as pl
from jax.experimental.pallas import tpu as pltpu
from jax.sharding import PartitionSpec as P

MEAN_FLOW = (0.5, 0.3, 0.0)
WAVE_SPEED = (1.5, 1.3, 1.0)
ELEM_SIZE = (1.0, 0.8, 1.2)
END_WEIGHT = 0.1
TIME_STEP = 0.01
KEEP = (0.0, 0.75, 1.0 / 3.0)
GAIN = (1.0, 0.25, 2.0 / 3.0)

ORDER = (1, 4, 2, 3, 0)
MAIN = 24
TAIL = 5 * MAIN
PER_VAR = 128
ROWS = 5 * PER_VAR
TILES = ((0, 0, 2), (1, 2, 4), (4, 4, 5))
BLOCK = 128
SPAN_ROWS = 104
TRACES = 4 * BLOCK
HALO = 5 * BLOCK
WAKE_ROW = 125
FACE_PAD = 16
TRACE_AT, LINK_AT, LIFT_AT = (0, TRACES, 2 * TRACES)
HIGH_AT = LIFT_AT + ROWS
LOW_AT = HIGH_AT + ROWS
TABLE_ROWS = LOW_AT + ROWS
LANES = 128
VMEM_LIMIT = 24 * 1024 * 1024


def derivative_table():
    points = np.array([-1.0, -np.sqrt(3.0 / 7.0), 0.0, np.sqrt(3.0 / 7.0), 1.0])
    products = np.array(
        [np.prod([points[j] - points[k] for k in range(5) if k != j]) for j in range(5)]
    )
    matrix = np.zeros((5, 5))
    for i in range(5):
        for j in range(5):
            if i != j:
                matrix[i, j] = products[i] / (products[j] * (points[i] - points[j]))
        matrix[i, i] = sum((1.0 / (points[i] - points[k]) for k in range(5) if k != i))
    return matrix


def flux_matrix(direction):
    flux = MEAN_FLOW[direction] * np.eye(5)
    flux[0, 1 + direction] += 1.0
    flux[4, 1 + direction] += 1.0
    flux[1 + direction, 4] += 1.0
    return flux


def half_flux(direction, sign):
    return 0.5 * (flux_matrix(direction) + sign * WAVE_SPEED[direction] * np.eye(5))


def lift_factor(direction):
    return TIME_STEP * 2.0 / (ELEM_SIZE[direction] * END_WEIGHT)


def half_scales():
    return (lift_factor(1) / 10.0, lift_factor(1), lift_factor(2), lift_factor(2), lift_factor(0))


def var_start(v):
    return ORDER.index(v) * PER_VAR


def node_row(v, a, p, s):
    node = p * 5 + s
    return var_start(v) + (a * MAIN + node if node < MAIN else TAIL + a)


def operator_tables():
    deriv = derivative_table()
    volume = np.zeros((ROWS, ROWS))
    lift = np.zeros((ROWS, HALO))
    trace = np.zeros((TRACES, ROWS))
    fluxes = [flux_matrix(d) for d in range(3)]
    plus = [half_flux(d, 1.0) for d in range(3)]
    minus = [half_flux(d, -1.0) for d in range(3)]
    plus_sent, minus_sent = (plus[2][:4], minus[2][:4])
    back_plus = np.vstack([np.eye(4), [[0.0, 0.0, 0.0, 1.0]]])
    back_minus = np.vstack([np.eye(4), [[0.0, 0.0, 0.0, -1.0]]])
    assert np.allclose(back_plus @ plus_sent, plus[2])
    assert np.allclose(back_minus @ minus_sent, minus[2])
    for a in range(5):
        for p in range(5):
            for s in range(5):
                here = [node_row(v, a, p, s) for v in range(5)]
                place = (a, p, s)
                for d in range(3):
                    for j in range(5):
                        there = list(place)
                        there[d] = j
                        cols = [node_row(v, *there) for v in range(5)]
                        coeff = -TIME_STEP * (2.0 / ELEM_SIZE[d]) * deriv[place[d], j]
                        volume[np.ix_(here, cols)] += coeff * fluxes[d]
                for d in (1, 2):
                    if place[d] == 4:
                        volume[np.ix_(here, here)] += lift_factor(d) * minus[d]
                    if place[d] == 0:
                        volume[np.ix_(here, here)] -= lift_factor(d) * plus[d]
                if p == 0:
                    cols = [s * 25 + v * 5 + a for v in range(5)]
                    lift[np.ix_(here, cols)] += lift_factor(1) * plus[1]
                    for v in range(5):
                        trace[BLOCK + s * 25 + v * 5 + a, here[v]] = 1.0
                if p == 4:
                    cols = [BLOCK + s * 25 + v * 5 + a for v in range(5)]
                    lift[np.ix_(here, cols)] -= lift_factor(1) * minus[1]
                    for v in range(5):
                        trace[s * 25 + v * 5 + a, here[v]] = 1.0
                if s == 0:
                    cols = [2 * BLOCK + c * 25 + a * 5 + p for c in range(4)]
                    lift[np.ix_(here, cols)] += lift_factor(2) * back_plus
                    rows = [3 * BLOCK + c * 25 + a * 5 + p for c in range(4)]
                    trace[np.ix_(rows, here)] += minus_sent
                if s == 4:
                    cols = [3 * BLOCK + c * 25 + a * 5 + p for c in range(4)]
                    lift[np.ix_(here, cols)] -= lift_factor(2) * back_minus
                    rows = [2 * BLOCK + c * 25 + a * 5 + p for c in range(4)]
                    trace[np.ix_(rows, here)] += plus_sent
                if a == 0:
                    cols = [4 * BLOCK + v * 25 + p * 5 + s for v in range(5)]
                    lift[np.ix_(here, cols)] += lift_factor(0) * plus[0]
    lift = lift / np.repeat(half_scales(), BLOCK)
    return volume, lift, trace, trace @ lift


def exact_table(table):
    exact = table.astype(ml_dtypes.bfloat16)
    assert np.allclose(exact.astype(np.float64), table, rtol=1e-12, atol=1e-12)
    return exact


def split_table(table):
    high = table.astype(ml_dtypes.bfloat16)
    low = (table - high.astype(np.float64)).astype(ml_dtypes.bfloat16)
    return high, low


def split(values):
    high = values.astype(jnp.bfloat16)
    low = (values - high.astype(jnp.float32)).astype(jnp.bfloat16)
    return high, low


def dot(left, right):
    return jnp.dot(left, right, preferred_element_type=jnp.float32)


def product(table, high, low):
    return dot(table, high) + dot(table, low)


def with_rows(values, first, extra):
    rows = lax.broadcasted_iota(jnp.int32, values.shape, 0)
    for k, row in enumerate(extra):
        values = jnp.where(rows == first + k, row, values)
    return values


def emit_pitch_faces(traces, wake, pitch_odd, pitch_a, pitch_b, inner):
    upper, lower = traces[0:BLOCK], traces[BLOCK : 2 * BLOCK]
    up = with_rows(upper[:, LANES:], WAKE_ROW, wake)
    down = lower[:, :LANES]
    pitch_a[...] = jnp.where(pitch_odd, down, up)
    pitch_b[...] = jnp.where(pitch_odd, up, down)
    inner[0:BLOCK] = upper[:, :LANES]
    inner[BLOCK:] = lower[:, LANES:]


def emit_span_faces(traces, span_odd, span_a, span_b):
    above, below = traces[0:SPAN_ROWS], traces[BLOCK : BLOCK + SPAN_ROWS]
    span_a[...] = jnp.where(span_odd, below, above)
    span_b[...] = jnp.where(span_odd, above, below)


def parities():
    return lax.axis_index("pitch") % 2 == 1, lax.axis_index("span") % 2 == 1


def combine(table, values):
    return [
        sum(float(table[i, j]) * values[j] for j in range(5) if table[i, j] != 0.0)
        for i in range(table.shape[0])
    ]


def begin_span_kernel(x, span_a, span_b):
    flat = x.reshape(x.shape[0], LANES)
    _, span_odd = parities()
    rest = jnp.zeros((SPAN_ROWS - 96, LANES), jnp.float32)
    for e in range(2):
        lanes = slice(e * LANES, (e + 1) * LANES)
        sides = []
        for s, sign in ((4, 1.0), (0, -1.0)):
            faces = [flat[pl.ds(v * 250 + 2 * s + e, 25, stride=10), :] for v in range(5)]
            sides.append(combine(half_flux(2, sign)[:4], faces))
        span_a[96:SPAN_ROWS, lanes] = rest
        span_b[96:SPAN_ROWS, lanes] = rest
        for c in range(4):
            above, below = (sides[0][c], sides[1][c])
            span_a[c * 25 : c * 25 + 25, lanes] = jnp.where(span_odd, below, above)
            span_b[c * 25 : c * 25 + 25, lanes] = jnp.where(span_odd, above, below)


def begin_pitch_kernel(x, wake, pitch_a, pitch_b, inner):
    flat = x.reshape(x.shape[0], LANES)
    pitch_odd, _ = parities()
    planes = wake.reshape(50, 5)[...]
    rows = lax.broadcasted_iota(jnp.int32, (50, LANES), 0)
    cols = lax.broadcasted_iota(jnp.int32, (50, LANES), 1)
    spread = jnp.zeros((50, LANES), jnp.float32)
    for s in range(5):
        mine = (cols - s) == 5 * (rows // 2)
        spread = jnp.where(mine, planes[:, s : s + 1], spread)
    own = [
        jnp.sum(jnp.where(rows % 2 == k, spread, 0.0), axis=0, keepdims=True) for k in range(2)
    ]
    tail = jnp.zeros((8, LANES), jnp.float32)
    up_tail = with_rows(tail, WAKE_ROW - 120, own)
    pitch_a[120:BLOCK] = jnp.where(pitch_odd, tail, up_tail)
    pitch_b[120:BLOCK] = jnp.where(pitch_odd, up_tail, tail)
    inner[120:BLOCK] = tail
    inner[BLOCK + 120 :] = tail
    for s in range(5):
        at = slice(s * 25, s * 25 + 25)
        upper, lower = (
            [flat[pl.ds(p * 10 + 2 * s + e, 25, stride=50), :] for e in range(2)] for p in (4, 0)
        )
        pitch_a[at] = jnp.where(pitch_odd, lower[0], upper[1])
        pitch_b[at] = jnp.where(pitch_odd, upper[1], lower[0])
        inner[at] = upper[0]
        inner[BLOCK + s * 25 : BLOCK + s * 25 + 25] = lower[1]


def load_state(x, state):
    flat = x.reshape(x.shape[0], LANES)
    for e in range(2):
        lanes = slice(e * LANES, (e + 1) * LANES)
        for v in range(5):
            base = var_start(v)
            first = v * 250 + e
            for a in range(5):
                at = base + a * MAIN
                state[at : at + MAIN, lanes] = flat[pl.ds(first + a * 50, MAIN, stride=2), :]
            tail = base + TAIL
            state[tail : tail + 8, lanes] = jnp.zeros((8, LANES), jnp.float32)
            state[tail : tail + 5, lanes] = flat[pl.ds(first + 2 * MAIN, 5, stride=50), :]


def add_axial_terms(gain, state, partial):
    lanes = lax.broadcasted_iota(jnp.int32, (MAIN + 8, LANES), 1)
    rows = lax.broadcasted_iota(jnp.int32, (8, LANES), 0)
    for e in range(2):
        own = slice(e * LANES, (e + 1) * LANES)
        upper_gap, lower_gap = ([], [])
        for v in range(5):
            base = var_start(v)
            lower = state[base : base + MAIN, own]
            upper = state[base + 4 * MAIN : base + TAIL, own]
            tail = state[base + TAIL : base + PER_VAR, own]
            turned = pltpu.roll(tail, 4, 0)
            join = lambda main, end: jnp.concatenate([main, end], axis=0)
            after = pltpu.roll(join(lower, turned), LANES - 1, 1)
            before = pltpu.roll(join(upper, turned), 1, 1)
            upper = join(upper, tail)
            upper_gap.append(jnp.where(lanes == LANES - 1, 0.0, upper - after))
            lower_gap.append(jnp.where(lanes == 0, 0.0, before) - join(lower, tail))
        mixed = []
        for gap, sign in ((upper_gap, -1.0), (lower_gap, 1.0)):
            mixed.append(combine(gain * lift_factor(0) * half_flux(0, sign), gap))
        for v in range(5):
            base = var_start(v)
            upper, lower = (mixed[0][v], mixed[1][v])
            partial[base : base + MAIN, own] += lower[:MAIN]
            partial[base + 4 * MAIN : base + TAIL, own] += upper[:MAIN]
            ends = jnp.where(rows == 0, lower[MAIN:], jnp.where(rows == 4, upper[MAIN:], 0.0))
            partial[base + TAIL : base + PER_VAR, own] += ends


def volume_rate(table, high, low):
    rate = [None] * 5
    for first, start, stop in TILES:
        part = slice(start * PER_VAR, stop * PER_VAR)
        table_high, table_low = (
            table[at + first * PER_VAR : at + ROWS, part] for at in (HIGH_AT, LOW_AT)
        )
        term = product(table_high, high[part], low[part]) + dot(table_low, high[part])
        for v in range(first, 5):
            block = term[(v - first) * PER_VAR : (v - first + 1) * PER_VAR]
            rate[v] = block if rate[v] is None else rate[v] + block
    return jnp.concatenate(rate, axis=0)


def advance_body(section, base, state, table, partial, faces):
    rate = volume_rate(table, *split(state[...]))
    gain, keep = GAIN[section], KEEP[section]
    if keep == 0.0:
        partial[...] = state[...] + rate
    else:
        partial[...] = keep * base[...] + gain * (state[...] + rate)
    add_axial_terms(gain, state, partial)
    if faces is not None:
        faces[...] = product(table[TRACE_AT : TRACE_AT + TRACES], *split(partial[...]))


def lift_table(table):
    return table[LIFT_AT : LIFT_AT + ROWS]


def first_kernel(offsets, x, table, base, partial, faces, flags):
    cols = lax.broadcasted_iota(jnp.int32, flags.shape, 1)
    moved = jnp.zeros(flags.shape, jnp.float32)
    for k in range(3):
        moved = jnp.where((cols == k) & (offsets[k] % 2 == 1), 1.0, moved)
    flags[...] = moved
    load_state(x, base)
    advance_body(0, None, base, table, partial, faces)


def later_kernel(section, base, before, halo_high, halo_low, table, partial, *refs):
    faces, state = refs
    lifted = product(lift_table(table), halo_high[...], halo_low[...])
    state[...] = before[...] + GAIN[section - 1] * lifted
    advance_body(section, base, state, table, partial, faces)


def gather_halo(section, flags, pitch_a, pitch_b, span_a, span_b, inner, halo_high, halo_low):
    def put(block, first, values):
        at = (slice(block * BLOCK, (block + 1) * BLOCK), slice(first, first + values.shape[1]))
        halo_high[at], halo_low[at] = split(half_scales()[block] * values)

    pitch_odd, span_odd = parities()
    after = jnp.where(pitch_odd, pitch_b[...], pitch_a[...])
    before = jnp.where(pitch_odd, pitch_a[...], pitch_b[...])
    put(0, 0, before)
    put(0, LANES, inner[0:BLOCK])
    put(1, 0, inner[BLOCK:])
    put(1, LANES, after)
    above = jnp.where(span_odd, span_b[...], span_a[...])
    below = jnp.where(span_odd, span_a[...], span_b[...])
    place = lax.axis_index("span")
    above = jnp.where(place == lax.axis_size("span") - 1, 0.0, above)
    below = jnp.where(place == 0, 0.0, below)
    rest = jnp.zeros((BLOCK - SPAN_ROWS, 2 * LANES), jnp.float32)
    put(2, 0, jnp.concatenate([below, rest], axis=0))
    put(3, 0, jnp.concatenate([above, rest], axis=0))
    wake = before[WAKE_ROW : WAKE_ROW + 2]
    moved = flags[0:1, section : section + 1] > 0.5
    rows = lax.broadcasted_iota(jnp.int32, (BLOCK, LANES), 0)
    cols = lax.broadcasted_iota(jnp.int32, (BLOCK, LANES), 1)
    for e in range(2):
        row = jnp.where(moved, wake[1 - e : 2 - e], wake[e : e + 1])
        column = jnp.sum(jnp.where(rows == cols, row, 0.0), axis=1, keepdims=True)
        put(4, e * LANES, jnp.where(cols == 0, column, 0.0))
    return wake


def next_traces(section, side, faces, table, high, low):
    at = LINK_AT + side * 2 * BLOCK
    rows = slice(side * 2 * BLOCK, (side + 1) * 2 * BLOCK)
    return faces[rows] + GAIN[section] * dot(table[at : at + 2 * BLOCK], high)


def exchange_kernel(
    section, flags, span_a, span_b, pitch_b, pitch_a, inner, faces, table,
    next_pitch_a, next_pitch_b, next_inner, next_span_a, next_span_b, halo_high, halo_low,
):
    wake = gather_halo(
        section, flags, pitch_a, pitch_b, span_a, span_b, inner, halo_high, halo_low
    )
    pitch_odd, span_odd = parities()
    traces = faces[...] + GAIN[section] * dot(
        table[LINK_AT : LINK_AT + TRACES], halo_high[...]
    )
    emit_span_faces(traces[2 * BLOCK :], span_odd, next_span_a, next_span_b)
    emit_pitch_faces(
        traces, [wake[0:1], wake[1:2]], pitch_odd, next_pitch_a, next_pitch_b, next_inner
    )


def last_kernel(base, before, halo_high, halo_low, table, rows, state, partial):
    lifted = product(lift_table(table), halo_high[...], halo_low[...])
    state[...] = before[...] + GAIN[1] * lifted
    advance_body(2, base, state, table, partial, None)
    flat = rows.reshape(rows.shape[0], LANES)
    for e in range(2):
        lanes = slice(e * LANES, (e + 1) * LANES)
        for v in range(5):
            start = var_start(v)
            first = v * 250 + e
            for a in range(5):
                at = start + a * MAIN
                flat[pl.ds(first + a * 50, MAIN, stride=2), :] = partial[at : at + MAIN, lanes]
            tail = start + TAIL
            flat[pl.ds(first + 2 * MAIN, 5, stride=50), :] = partial[tail : tail + 5, lanes]


def mixed_faces(faces, s, lanes, direction, sign):
    table = half_flux(direction, sign)
    at = FACE_PAD + s * 25
    rows = lax.broadcasted_iota(jnp.int32, (25, LANES), 0)
    own = faces[at : at + 25, lanes]
    total = float(table[0, 0]) * own
    for i in range(5):
        for j in range(5):
            if i != j and table[i, j] != 0.0:
                moved = faces[at + 5 * (j - i) : at + 5 * (j - i) + 25, lanes]
                here = (rows >= 5 * i) & (rows < 5 * i + 5)
                total = total + jnp.where(here, float(table[i, j]) * moved, 0.0)
    return total


def final_kernel(
    flags, span_a, span_b, pitch_b, pitch_a, inner, before, out, result, after_faces,
    before_faces, done,
):
    flat = result.reshape(result.shape[0], LANES)
    flat[...] = before.reshape(before.shape[0], LANES)[...]
    pitch_odd, span_odd = parities()
    gain = GAIN[2]

    def add(start, stride, values):
        at = pl.ds(start, values.shape[0], stride=stride)
        flat[at, :] = flat[at, :] + values

    place = lax.axis_index("span")
    scale = gain * lift_factor(2)
    up_scale = jnp.where(place == lax.axis_size("span") - 1, 0.0, -scale)
    down_scale = jnp.where(place == 0, 0.0, scale)
    for e in range(2):
        lanes = slice(e * LANES, (e + 1) * LANES)
        for c in range(4):
            at = slice(c * 25, c * 25 + 25)
            first, second = (span_a[at, lanes], span_b[at, lanes])
            above = up_scale * jnp.where(span_odd, second, first)
            below = down_scale * jnp.where(span_odd, first, second)
            add(c * 250 + 8 + e, 10, above)
            add(c * 250 + e, 10, below)
            if c == 3:
                add(4 * 250 + 8 + e, 10, -above)
                add(4 * 250 + e, 10, below)

    at = slice(FACE_PAD, FACE_PAD + BLOCK)
    arrived = jnp.where(pitch_odd, pitch_a[...], pitch_b[...])
    before_faces[at, :LANES] = arrived
    before_faces[at, LANES:] = inner[0:BLOCK]
    after_faces[at, :LANES] = inner[BLOCK:]
    after_faces[at, LANES:] = jnp.where(pitch_odd, pitch_b[...], pitch_a[...])
    scale = gain * lift_factor(1)
    for e in range(2):
        lanes = slice(e * LANES, (e + 1) * LANES)
        for s in range(5):
            add(40 + 2 * s + e, 50, -scale * mixed_faces(after_faces, s, lanes, 1, -1.0))
            add(2 * s + e, 50, scale * mixed_faces(before_faces, s, lanes, 1, 1.0))

    wake = arrived[WAKE_ROW : WAKE_ROW + 2]
    moved = flags[0:1, 2:3] > 0.5
    rows = lax.broadcasted_iota(jnp.int32, (25, LANES), 0)
    cols = lax.broadcasted_iota(jnp.int32, (25, LANES), 1)
    for e in range(2):
        row = jnp.where(moved, wake[1 - e : 2 - e], wake[e : e + 1])
        columns = [
            jnp.sum(jnp.where(cols == rows + 25 * v, row, 0.0), axis=1, keepdims=True)
            for v in range(5)
        ]
        inlet = combine(gain * lift_factor(0) * half_flux(0, 1.0), columns)
        for v in range(5):
            add(v * 250 + e, 2, jnp.where(cols == 0, inlet[v], 0.0))

    copies = []
    for v in range(5):
        part = pl.ds(v * 250, 250)
        copies.append(pltpu.make_async_copy(result.at[part], out.at[part], done.at[v]))
        copies[-1].start()
    for copy in copies:
        copy.wait()


IN_VMEM = pl.BlockSpec(memory_space=pltpu.VMEM)
IN_SMEM = pl.BlockSpec(memory_space=pltpu.SMEM)


def call(kernel, name, outs, args, in_specs=(), scratch=(), flops=0, out_spec=IN_VMEM):
    in_specs = list(in_specs)
    return pl.pallas_call(
        kernel,
        name=name,
        out_shape=[jax.ShapeDtypeStruct(shape, dtype) for shape, dtype in outs],
        in_specs=in_specs + [IN_VMEM] * (len(args) - len(in_specs)),
        out_specs=[out_spec] * len(outs),
        scratch_shapes=list(scratch),
        compiler_params=pltpu.CompilerParams(vmem_limit_bytes=VMEM_LIMIT),
        cost_estimate=pl.CostEstimate(flops=flops, bytes_accessed=2**20, transcendentals=0),
    )(*args)


def swapped(value, axis, odd):
    pitch, span = (lax.axis_size("pitch"), lax.axis_size("span"))
    pairs = []
    for i in range(pitch):
        for j in range(span):
            if axis == "pitch":
                other = ((i + (1 if i % 2 == odd else -1)) % pitch, j)
            else:
                other = (i, j + (1 if j % 2 == odd else -1))
                if not 0 <= other[1] < span:
                    other = (i ^ 1, j)
            pairs.append((i * span + j, other[0] * span + other[1]))
    return lax.ppermute(value, ("pitch", "span"), pairs)


def span_exchanged(faces):
    return swapped(faces[0], "span", 0), swapped(faces[1], "span", 1)


def pitch_exchanged(faces):
    return swapped(faces[1], "pitch", 1), swapped(faces[0], "pitch", 0)


F32 = jnp.float32
PITCH_OUTS = [((BLOCK, LANES), F32), ((BLOCK, LANES), F32), ((2 * BLOCK, LANES), F32)]
SPAN_OUTS = [((SPAN_ROWS, 2 * LANES), F32)] * 2
SMALL_OUT = ((8, LANES), F32)
HALO_OUTS = [((HALO, 2 * LANES), jnp.bfloat16)] * 2
STATE_OUT = ((ROWS, 2 * LANES), F32)
TRACE_OUT = ((TRACES, 2 * LANES), F32)


def shards(table, state, wake_planes, bar_offsets):
    x = state.reshape(-1, 1, LANES)
    wake = wake_planes.transpose(0, 1, 3, 4, 2).reshape(50, 1, 5)
    faces = call(begin_span_kernel, "begin_span", SPAN_OUTS, [x], flops=10**10)
    span = span_exchanged(faces)
    *faces, inner = call(begin_pitch_kernel, "begin_pitch", PITCH_OUTS, [x, wake], flops=10**10)
    pitch = pitch_exchanged(faces)
    base, partial, traces, flags = call(
        first_kernel,
        "first",
        [STATE_OUT, STATE_OUT, TRACE_OUT, SMALL_OUT],
        [bar_offsets, x, table],
        in_specs=[IN_SMEM],
        flops=10**9,
    )
    for section in range(2):
        next_a, next_b, inner, *faces, high, low = call(
            functools.partial(exchange_kernel, section),
            "exchange",
            PITCH_OUTS + SPAN_OUTS + HALO_OUTS,
            [flags, span[0], span[1], pitch[0], pitch[1], inner, traces, table],
            flops=10**8,
        )
        span = span_exchanged(faces)
        pitch = pitch_exchanged([next_a, next_b])
        if section == 0:
            partial, traces = call(
                functools.partial(later_kernel, section + 1),
                "later",
                [STATE_OUT, TRACE_OUT],
                [base, partial, high, low, table],
                scratch=[pltpu.VMEM((ROWS, 2 * LANES), F32)],
                flops=10**9,
            )
    (rows,) = call(
        last_kernel,
        "last",
        [(x.shape, F32)],
        [base, partial, high, low, table],
        scratch=[pltpu.VMEM((ROWS, 2 * LANES), F32)] * 2,
        flops=10**9,
    )
    (out,) = call(
        final_kernel,
        "final",
        [(x.shape, F32)],
        [flags, span[0], span[1], pitch[0], pitch[1], inner, rows],
        scratch=[
            pltpu.VMEM(x.shape, F32),
            *[pltpu.VMEM((BLOCK + 2 * FACE_PAD, 2 * LANES), F32)] * 2,
            pltpu.SemaphoreType.DMA((5,)),
        ],
        flops=10**8,
        out_spec=pl.BlockSpec(memory_space=pl.ANY),
    )
    return out.reshape(state.shape)


def solution(mesh):
    volume, lift, trace, link = operator_tables()
    high, low = split_table(volume)
    table = np.concatenate([exact_table(t) for t in (trace, link, lift)] + [high, low])
    assert table.shape == (TABLE_ROWS, ROWS)
    in_specs = (
        P(None, None, None, None, "pitch", "span", None),
        P(None, None, None, "pitch", "span"),
        P(),
    )
    out_specs = P(None, None, None, None, "pitch", "span", None)
    return jax.shard_map(
        functools.partial(shards, jnp.asarray(table)),
        mesh=mesh,
        in_specs=in_specs,
        out_specs=out_specs,
        check_vma=False,
    )
```

```python
import functools

import jax
import jax.numpy as jnp
import ml_dtypes
import numpy as np
from jax import lax
from jax.experimental import pallas as pl
from jax.experimental.pallas import tpu as pltpu
from jax.sharding import PartitionSpec as P

MEAN_FLOW = (0.5, 0.3, 0.0)
WAVE_SPEED = (1.5, 1.3, 1.0)
ELEM_SIZE = (1.0, 0.8, 1.2)
END_WEIGHT = 0.1
TIME_STEP = 0.01
KEEP = (0.0, 0.75, 1.0 / 3.0)
GAIN = (1.0, 0.25, 2.0 / 3.0)

ORDER = (1, 4, 2, 3, 0)
MAIN = 24
TAIL = 5 * MAIN
PER_VAR = 128
ROWS = 5 * PER_VAR
INLET_ROWS = 32
TILES = ((0, 0, 2), (1, 2, 4), (4, 4, 5))
BLOCK = 128
SPAN_ROWS = 104
TRACES = 4 * BLOCK
HALO = 5 * BLOCK
WAKE_ROW = 125
FACE_PAD = 16
HIGH_AT = TRACES
LOW_AT = HIGH_AT + ROWS
LIFT_AT = TRACES
INLET_AT = LIFT_AT + ROWS
LANES = 128
VMEM_LIMIT = 24 * 1024 * 1024


def derivative_table():
    points = np.array([-1.0, -np.sqrt(3.0 / 7.0), 0.0, np.sqrt(3.0 / 7.0), 1.0])
    products = np.array(
        [np.prod([points[j] - points[k] for k in range(5) if k != j]) for j in range(5)]
    )
    matrix = np.zeros((5, 5))
    for i in range(5):
        for j in range(5):
            if i != j:
                matrix[i, j] = products[i] / (products[j] * (points[i] - points[j]))
        matrix[i, i] = sum((1.0 / (points[i] - points[k]) for k in range(5) if k != i))
    return matrix


def flux_matrix(direction):
    flux = MEAN_FLOW[direction] * np.eye(5)
    flux[0, 1 + direction] += 1.0
    flux[4, 1 + direction] += 1.0
    flux[1 + direction, 4] += 1.0
    return flux


def half_flux(direction, sign):
    return 0.5 * (flux_matrix(direction) + sign * WAVE_SPEED[direction] * np.eye(5))


def lift_factor(direction):
    return TIME_STEP * 2.0 / (ELEM_SIZE[direction] * END_WEIGHT)


def half_scales():
    return (lift_factor(1) / 10.0, lift_factor(1), lift_factor(2), lift_factor(2), lift_factor(0))


def var_start(v):
    return ORDER.index(v) * PER_VAR


def node_row(v, a, p, s):
    node = p * 5 + s
    return var_start(v) + (a * MAIN + node if node < MAIN else TAIL + a)


def operator_tables():
    deriv = derivative_table()
    volume = np.zeros((ROWS, ROWS))
    lift = np.zeros((ROWS, HALO))
    trace = np.zeros((TRACES, ROWS))
    fluxes = [flux_matrix(d) for d in range(3)]
    plus = [half_flux(d, 1.0) for d in range(3)]
    minus = [half_flux(d, -1.0) for d in range(3)]
    plus_sent, minus_sent = (plus[2][:4], minus[2][:4])
    back_plus = np.vstack([np.eye(4), [[0.0, 0.0, 0.0, 1.0]]])
    back_minus = np.vstack([np.eye(4), [[0.0, 0.0, 0.0, -1.0]]])
    assert np.allclose(back_plus @ plus_sent, plus[2])
    assert np.allclose(back_minus @ minus_sent, minus[2])
    for a in range(5):
        for p in range(5):
            for s in range(5):
                here = [node_row(v, a, p, s) for v in range(5)]
                place = (a, p, s)
                for d in range(3):
                    for j in range(5):
                        there = list(place)
                        there[d] = j
                        cols = [node_row(v, *there) for v in range(5)]
                        coeff = -TIME_STEP * (2.0 / ELEM_SIZE[d]) * deriv[place[d], j]
                        volume[np.ix_(here, cols)] += coeff * fluxes[d]
                for d in (1, 2):
                    if place[d] == 4:
                        volume[np.ix_(here, here)] += lift_factor(d) * minus[d]
                    if place[d] == 0:
                        volume[np.ix_(here, here)] -= lift_factor(d) * plus[d]
                if p == 0:
                    cols = [s * 25 + v * 5 + a for v in range(5)]
                    lift[np.ix_(here, cols)] += lift_factor(1) * plus[1]
                    for v in range(5):
                        trace[BLOCK + s * 25 + v * 5 + a, here[v]] = 1.0
                if p == 4:
                    cols = [BLOCK + s * 25 + v * 5 + a for v in range(5)]
                    lift[np.ix_(here, cols)] -= lift_factor(1) * minus[1]
                    for v in range(5):
                        trace[s * 25 + v * 5 + a, here[v]] = 1.0
                if s == 0:
                    cols = [2 * BLOCK + c * 25 + a * 5 + p for c in range(4)]
                    lift[np.ix_(here, cols)] += lift_factor(2) * back_plus
                    rows = [3 * BLOCK + c * 25 + a * 5 + p for c in range(4)]
                    trace[np.ix_(rows, here)] += minus_sent
                if s == 4:
                    cols = [3 * BLOCK + c * 25 + a * 5 + p for c in range(4)]
                    lift[np.ix_(here, cols)] -= lift_factor(2) * back_minus
                    rows = [2 * BLOCK + c * 25 + a * 5 + p for c in range(4)]
                    trace[np.ix_(rows, here)] += plus_sent
                if a == 0:
                    cols = [4 * BLOCK + v * 25 + p * 5 + s for v in range(5)]
                    lift[np.ix_(here, cols)] += lift_factor(0) * plus[0]
    lift = lift / np.repeat(half_scales(), BLOCK)
    return volume, lift, trace, trace @ lift


def exact_table(table):
    exact = table.astype(ml_dtypes.bfloat16)
    assert np.allclose(exact.astype(np.float64), table, rtol=1e-12, atol=1e-12)
    return exact


def split_table(table):
    high = table.astype(ml_dtypes.bfloat16)
    low = (table - high.astype(np.float64)).astype(ml_dtypes.bfloat16)
    return high, low


def split(values):
    high = values.astype(jnp.bfloat16)
    low = (values - high.astype(jnp.float32)).astype(jnp.bfloat16)
    return high, low


def dot(left, right):
    return jnp.dot(left, right, preferred_element_type=jnp.float32)


def product(table, high, low):
    return dot(table, high) + dot(table, low)


def with_rows(values, first, extra):
    rows = lax.broadcasted_iota(jnp.int32, values.shape, 0)
    for k, row in enumerate(extra):
        values = jnp.where(rows == first + k, row, values)
    return values


def emit_pitch_faces(traces, wake, pitch_odd, pitch_a, pitch_b, inner):
    upper, lower = traces[0:BLOCK], traces[BLOCK : 2 * BLOCK]
    up = with_rows(upper[:, LANES:], WAKE_ROW, wake)
    down = lower[:, :LANES]
    pitch_a[...] = jnp.where(pitch_odd, down, up)
    pitch_b[...] = jnp.where(pitch_odd, up, down)
    inner[0:BLOCK] = upper[:, :LANES]
    inner[BLOCK:] = lower[:, LANES:]


def emit_span_faces(traces, span_odd, span_a, span_b):
    above, below = traces[0:SPAN_ROWS], traces[BLOCK : BLOCK + SPAN_ROWS]
    span_a[...] = jnp.where(span_odd, below, above)
    span_b[...] = jnp.where(span_odd, above, below)


def parities():
    return lax.axis_index("pitch") % 2 == 1, lax.axis_index("span") % 2 == 1


def combine(table, values):
    return [
        sum(float(table[i, j]) * values[j] for j in range(5) if table[i, j] != 0.0)
        for i in range(table.shape[0])
    ]


def begin_span_kernel(x, span_a, span_b):
    flat = x.reshape(x.shape[0], LANES)
    _, span_odd = parities()
    rest = jnp.zeros((SPAN_ROWS - 96, LANES), jnp.float32)
    for e in range(2):
        lanes = slice(e * LANES, (e + 1) * LANES)
        sides = []
        for s, sign in ((4, 1.0), (0, -1.0)):
            faces = [flat[pl.ds(v * 250 + 2 * s + e, 25, stride=10), :] for v in range(5)]
            sides.append(combine(half_flux(2, sign)[:4], faces))
        span_a[96:SPAN_ROWS, lanes] = rest
        span_b[96:SPAN_ROWS, lanes] = rest
        for c in range(4):
            above, below = (sides[0][c], sides[1][c])
            span_a[c * 25 : c * 25 + 25, lanes] = jnp.where(span_odd, below, above)
            span_b[c * 25 : c * 25 + 25, lanes] = jnp.where(span_odd, above, below)


def begin_pitch_kernel(x, wake, pitch_a, pitch_b, inner):
    flat = x.reshape(x.shape[0], LANES)
    pitch_odd, _ = parities()
    planes = wake.reshape(50, 5)[...]
    rows = lax.broadcasted_iota(jnp.int32, (50, LANES), 0)
    cols = lax.broadcasted_iota(jnp.int32, (50, LANES), 1)
    spread = jnp.zeros((50, LANES), jnp.float32)
    for s in range(5):
        mine = (cols - s) == 5 * (rows // 2)
        spread = jnp.where(mine, planes[:, s : s + 1], spread)
    own = [
        jnp.sum(jnp.where(rows % 2 == k, spread, 0.0), axis=0, keepdims=True) for k in range(2)
    ]
    tail = jnp.zeros((8, LANES), jnp.float32)
    up_tail = with_rows(tail, WAKE_ROW - 120, own)
    pitch_a[120:BLOCK] = jnp.where(pitch_odd, tail, up_tail)
    pitch_b[120:BLOCK] = jnp.where(pitch_odd, up_tail, tail)
    inner[120:BLOCK] = tail
    inner[BLOCK + 120 :] = tail
    for s in range(5):
        at = slice(s * 25, s * 25 + 25)
        upper, lower = (
            [flat[pl.ds(p * 10 + 2 * s + e, 25, stride=50), :] for e in range(2)] for p in (4, 0)
        )
        pitch_a[at] = jnp.where(pitch_odd, lower[0], upper[1])
        pitch_b[at] = jnp.where(pitch_odd, upper[1], lower[0])
        inner[at] = upper[0]
        inner[BLOCK + s * 25 : BLOCK + s * 25 + 25] = lower[1]


def load_state(x, state):
    flat = x.reshape(x.shape[0], LANES)
    for e in range(2):
        lanes = slice(e * LANES, (e + 1) * LANES)
        for v in range(5):
            base = var_start(v)
            first = v * 250 + e
            for a in range(5):
                at = base + a * MAIN
                state[at : at + MAIN, lanes] = flat[pl.ds(first + a * 50, MAIN, stride=2), :]
            tail = base + TAIL
            state[tail : tail + 8, lanes] = jnp.zeros((8, LANES), jnp.float32)
            state[tail : tail + 5, lanes] = flat[pl.ds(first + 2 * MAIN, 5, stride=50), :]


def add_axial_terms(gain, state, partial):
    lanes = lax.broadcasted_iota(jnp.int32, (MAIN + 8, LANES), 1)
    rows = lax.broadcasted_iota(jnp.int32, (8, LANES), 0)
    for e in range(2):
        own = slice(e * LANES, (e + 1) * LANES)
        upper_gap, lower_gap = ([], [])
        for v in range(5):
            base = var_start(v)
            lower = state[base : base + MAIN, own]
            upper = state[base + 4 * MAIN : base + TAIL, own]
            tail = state[base + TAIL : base + PER_VAR, own]
            turned = pltpu.roll(tail, 4, 0)
            join = lambda main, end: jnp.concatenate([main, end], axis=0)
            after = pltpu.roll(join(lower, turned), LANES - 1, 1)
            before = pltpu.roll(join(upper, turned), 1, 1)
            upper = join(upper, tail)
            upper_gap.append(jnp.where(lanes == LANES - 1, 0.0, upper - after))
            lower_gap.append(jnp.where(lanes == 0, 0.0, before) - join(lower, tail))
        mixed = []
        for gap, sign in ((upper_gap, -1.0), (lower_gap, 1.0)):
            mixed.append(combine(gain * lift_factor(0) * half_flux(0, sign), gap))
        for v in range(5):
            base = var_start(v)
            upper, lower = (mixed[0][v], mixed[1][v])
            partial[base : base + MAIN, own] += lower[:MAIN]
            partial[base + 4 * MAIN : base + TAIL, own] += upper[:MAIN]
            ends = jnp.where(rows == 0, lower[MAIN:], jnp.where(rows == 4, upper[MAIN:], 0.0))
            partial[base + TAIL : base + PER_VAR, own] += ends


def volume_rate(table, high, low):
    rate = [None] * 5
    for first, start, stop in TILES:
        part = slice(start * PER_VAR, stop * PER_VAR)
        table_high, table_low = (
            table[at + first * PER_VAR : at + ROWS, part] for at in (HIGH_AT, LOW_AT)
        )
        term = product(table_high, high[part], low[part]) + dot(table_low, high[part])
        for v in range(first, 5):
            block = term[(v - first) * PER_VAR : (v - first + 1) * PER_VAR]
            rate[v] = block if rate[v] is None else rate[v] + block
    return jnp.concatenate(rate, axis=0)


def phase(run):
    pl.when(lax.axis_index("span") >= 0)(run)


def advance_body(section, base, state, table, partial, faces):
    gain, keep = GAIN[section], KEEP[section]

    @phase
    def _():
        rate = volume_rate(table, *split(state[...]))
        if keep == 0.0:
            partial[...] = state[...] + rate
        else:
            partial[...] = keep * base[...] + gain * (state[...] + rate)

    @phase
    def _():
        add_axial_terms(gain, state, partial)

    if faces is not None:
        faces[...] = product(table[0:TRACES], *split(partial[...]))


def add_halo(section, before, near, far, links, state, far_high, far_low):
    gain = GAIN[section]
    gather_far(section, *far, far_high, far_low)
    side = pl.multiple_of(lax.axis_index("pitch") % 2 * BLOCK, BLOCK)
    rows = slice(LIFT_AT, LIFT_AT + ROWS)
    near_high, near_low = near
    state[...] = before[...] + gain * (
        product(links[rows, : 4 * BLOCK], near_high[...], near_low[...])
        + product(links[rows, pl.ds(side, BLOCK)], far_high[0:BLOCK], far_low[0:BLOCK])
    )
    added = gain * product(
        links[INLET_AT : INLET_AT + 5 * INLET_ROWS, 0:BLOCK], far_high[BLOCK:], far_low[BLOCK:]
    )
    for k in range(5):
        start, at = (k * PER_VAR, k * INLET_ROWS)
        state[start : start + MAIN] += added[at : at + MAIN]
        state[start + TAIL : start + PER_VAR] += added[at + MAIN : at + INLET_ROWS]


def first_kernel(offsets, x, table, base, partial, faces, flags):
    cols = lax.broadcasted_iota(jnp.int32, flags.shape, 1)
    moved = jnp.zeros(flags.shape, jnp.float32)
    for k in range(3):
        moved = jnp.where((cols == k) & (offsets[k] % 2 == 1), 1.0, moved)
    flags[...] = moved
    load_state(x, base)
    advance_body(0, None, base, table, partial, faces)


def later_kernel(
    base, before, near_high, near_low, flags, pitch_b, pitch_a, table, links, partial, faces,
    state, far_high, far_low,
):
    near, far = ((near_high, near_low), (flags, pitch_a, pitch_b))
    add_halo(0, before, near, far, links, state, far_high, far_low)
    advance_body(1, base, state, table, partial, faces)


def put_halo(halo_high, halo_low, block, first, scale, values):
    at = (slice(block * BLOCK, (block + 1) * BLOCK), slice(first, first + values.shape[1]))
    halo_high[at], halo_low[at] = split(scale * values)


def gather_near(pitch_a, span_a, span_b, inner, halo_high, halo_low):
    put = functools.partial(put_halo, halo_high, halo_low)
    scales = half_scales()
    pitch_odd, span_odd = parities()
    near = pitch_a[...]
    put(0, 0, scales[0], jnp.where(pitch_odd, near, 0.0))
    put(0, LANES, scales[0], inner[0:BLOCK])
    put(1, 0, scales[1], inner[BLOCK:])
    put(1, LANES, scales[1], jnp.where(pitch_odd, 0.0, near))
    above = jnp.where(span_odd, span_b[...], span_a[...])
    below = jnp.where(span_odd, span_a[...], span_b[...])
    place = lax.axis_index("span")
    above = jnp.where(place == lax.axis_size("span") - 1, 0.0, above)
    below = jnp.where(place == 0, 0.0, below)
    rest = jnp.zeros((BLOCK - SPAN_ROWS, 2 * LANES), jnp.float32)
    put(2, 0, scales[2], jnp.concatenate([below, rest], axis=0))
    put(3, 0, scales[3], jnp.concatenate([above, rest], axis=0))


def arrived_wake(pitch_a, pitch_b):
    pitch_odd, _ = parities()
    rows = slice(WAKE_ROW, WAKE_ROW + 2)
    return jnp.where(pitch_odd, pitch_a[rows], pitch_b[rows])


def inlet_row(section, flags, wake, e):
    moved = flags[0:1, section : section + 1] > 0.5
    return jnp.where(moved, wake[1 - e : 2 - e], wake[e : e + 1])


def gather_far(section, flags, pitch_a, pitch_b, halo_high, halo_low):
    put = functools.partial(put_halo, halo_high, halo_low)
    scales = half_scales()
    pitch_odd, _ = parities()
    far = jnp.where(pitch_odd, scales[1], scales[0]) * pitch_b[...]
    put(0, 0, 1.0, jnp.where(pitch_odd, 0.0, far))
    put(0, LANES, 1.0, jnp.where(pitch_odd, far, 0.0))
    wake = arrived_wake(pitch_a, pitch_b)
    rows = lax.broadcasted_iota(jnp.int32, (BLOCK, LANES), 0)
    cols = lax.broadcasted_iota(jnp.int32, (BLOCK, LANES), 1)
    for e in range(2):
        row = inlet_row(section, flags, wake, e)
        column = jnp.sum(jnp.where(rows == cols, row, 0.0), axis=1, keepdims=True)
        put(1, e * LANES, scales[4], jnp.where(cols == 0, column, 0.0))


def near_kernel(
    section, span_a, span_b, pitch_a, inner, faces, links, near_faces, halo_high, halo_low
):
    gather_near(pitch_a, span_a, span_b, inner, halo_high, halo_low)
    for half in range(2):
        at = slice(half * 2 * BLOCK, (half + 1) * 2 * BLOCK)
        near_faces[at] = faces[at] + GAIN[section] * dot(
            links[at, : 4 * BLOCK], halo_high[...]
        )


def from_lanes(row, moves):
    lanes = lax.broadcasted_iota(jnp.int32, row.shape, 1)
    total = None
    for factor, start, stop, distance in moves:
        moved = pltpu.roll(row, distance % LANES, 1) if distance else row
        term = jnp.where((lanes >= start) & (lanes < stop), factor * moved, 0.0)
        total = term if total is None else total + term
    return total


def lane_moves(table):
    return [
        (float(table[i, j]), 25 * i, 25 * i + 25, 25 * (i - j))
        for i in range(table.shape[0])
        for j in range(table.shape[1])
        if table[i, j] != 0.0
    ]


def far_kernel(
    section, flags, pitch_b, pitch_a, near_faces,
    next_pitch_a, next_pitch_b, next_inner, next_span_a, next_span_b, *refs
):
    *traces, faces, lifted = refs
    pitch_odd, span_odd = parities()
    gain = GAIN[section]
    for e in range(2):
        traces[e][...] = near_faces[:, e * LANES : (e + 1) * LANES]

    def add(start, count, stride, e, values):
        at = pl.ds(start, count, stride=stride) if stride > 1 else pl.ds(start, count)
        traces[e][at, :] = traces[e][at, :] + values

    faces[FACE_PAD : FACE_PAD + BLOCK] = pitch_b[...]
    plus, minus = (half_flux(1, 1.0), half_flux(1, -1.0))
    scale = gain * lift_factor(1)
    assert np.allclose(plus - np.diag(np.diag(plus)), minus - np.diag(np.diag(minus)))
    factor = lambda i, j: jnp.where(
        pitch_odd, -scale * float(minus[i, j]), scale * float(plus[i, j])
    )
    rows = lax.broadcasted_iota(jnp.int32, (BLOCK, LANES), 0)
    place = rows - 25 * sum((rows >= 25 * s).astype(jnp.int32) for s in range(1, 5))
    total = factor(0, 0) * pitch_b[...]
    for i in range(5):
        for j in range(5):
            if i != j and plus[i, j] != 0.0:
                at = FACE_PAD + 5 * (j - i)
                here = (place >= 5 * i) & (place < 5 * i + 5)
                total = total + jnp.where(here, factor(i, j) * faces[at : at + BLOCK], 0.0)
    total = jnp.where(rows < WAKE_ROW, total, 0.0)
    lifted[...] = total
    add(0, BLOCK, 1, 1, jnp.where(pitch_odd, total, 0.0))
    add(BLOCK, BLOCK, 1, 0, jnp.where(pitch_odd, 0.0, total))
    for block, s, sign in ((2, 4, 1.0), (3, 0, -1.0)):
        edge = [lifted[s * 25 + 5 * v : s * 25 + 5 * v + 5] for v in range(5)]
        for c, values in enumerate(combine(half_flux(2, sign)[:4], edge)):
            start = block * BLOCK + c * 25
            add(start + 4, 5, 5, 1, jnp.where(pitch_odd, values, 0.0))
            add(start, 5, 5, 0, jnp.where(pitch_odd, 0.0, values))

    wake = arrived_wake(pitch_a, pitch_b)
    rows = lax.broadcasted_iota(jnp.int32, (5, LANES), 0)
    cols = lax.broadcasted_iota(jnp.int32, (5, LANES), 1)
    for e in range(2):

        def add_column(start, stride, row, first, step):
            picked = jnp.where(cols == first + step * rows, row, 0.0)
            column = jnp.sum(picked, axis=1, keepdims=True)
            add(start, 5, stride, e, jnp.where(cols == 0, column, 0.0))

        row = jnp.broadcast_to(inlet_row(section, flags, wake, e), (8, LANES))
        row = from_lanes(row, lane_moves(gain * lift_factor(0) * half_flux(0, 1.0)))
        for block, p in ((0, 4), (1, 0)):
            for s in range(5):
                add_column(block * BLOCK + s * 25, 5, row[0:1], p * 5 + s, 25)
        for block, s, sign in ((2, 4, 1.0), (3, 0, -1.0)):
            sent = from_lanes(row, lane_moves(half_flux(2, sign)[:4]))
            for c in range(4):
                add_column(block * BLOCK + c * 25, 1, sent[0:1], c * 25 + s, 5)

    both = jnp.concatenate([traces[0][...], traces[1][...]], axis=1)
    emit_span_faces(both[2 * BLOCK :], span_odd, next_span_a, next_span_b)
    emit_pitch_faces(
        both[: 2 * BLOCK], [wake[0:1], wake[1:2]], pitch_odd, next_pitch_a, next_pitch_b,
        next_inner,
    )


def last_kernel(
    base, before, near_high, near_low, flags, pitch_b, pitch_a, table, links, rows,
    state, far_high, far_low, partial,
):
    near, far = ((near_high, near_low), (flags, pitch_a, pitch_b))
    add_halo(1, before, near, far, links, state, far_high, far_low)
    advance_body(2, base, state, table, partial, None)
    flat = rows.reshape(rows.shape[0], LANES)
    for e in range(2):
        lanes = slice(e * LANES, (e + 1) * LANES)
        for v in range(5):
            start = var_start(v)
            first = v * 250 + e
            for a in range(5):
                at = start + a * MAIN
                flat[pl.ds(first + a * 50, MAIN, stride=2), :] = partial[at : at + MAIN, lanes]
            tail = start + TAIL
            flat[pl.ds(first + 2 * MAIN, 5, stride=50), :] = partial[tail : tail + 5, lanes]


def mixed_faces(faces, s, lanes, direction, sign):
    table = half_flux(direction, sign)
    at = FACE_PAD + s * 25
    rows = lax.broadcasted_iota(jnp.int32, (25, LANES), 0)
    own = faces[at : at + 25, lanes]
    total = float(table[0, 0]) * own
    for i in range(5):
        for j in range(5):
            if i != j and table[i, j] != 0.0:
                moved = faces[at + 5 * (j - i) : at + 5 * (j - i) + 25, lanes]
                here = (rows >= 5 * i) & (rows < 5 * i + 5)
                total = total + jnp.where(here, float(table[i, j]) * moved, 0.0)
    return total


def final_kernel(
    flags, span_a, span_b, pitch_b, pitch_a, inner, before, out, result, after_faces,
    before_faces, done,
):
    flat = result.reshape(result.shape[0], LANES)
    flat[...] = before.reshape(before.shape[0], LANES)[...]
    pitch_odd, span_odd = parities()
    gain = GAIN[2]

    def add(start, stride, values):
        at = pl.ds(start, values.shape[0], stride=stride)
        flat[at, :] = flat[at, :] + values

    place = lax.axis_index("span")
    scale = gain * lift_factor(2)
    up_scale = jnp.where(place == lax.axis_size("span") - 1, 0.0, -scale)
    down_scale = jnp.where(place == 0, 0.0, scale)
    for e in range(2):
        lanes = slice(e * LANES, (e + 1) * LANES)
        for c in range(4):
            at = slice(c * 25, c * 25 + 25)
            first, second = (span_a[at, lanes], span_b[at, lanes])
            above = up_scale * jnp.where(span_odd, second, first)
            below = down_scale * jnp.where(span_odd, first, second)
            add(c * 250 + 8 + e, 10, above)
            add(c * 250 + e, 10, below)
            if c == 3:
                add(4 * 250 + 8 + e, 10, -above)
                add(4 * 250 + e, 10, below)

    at = slice(FACE_PAD, FACE_PAD + BLOCK)
    arrived = jnp.where(pitch_odd, pitch_a[...], pitch_b[...])
    before_faces[at, :LANES] = arrived
    before_faces[at, LANES:] = inner[0:BLOCK]
    after_faces[at, :LANES] = inner[BLOCK:]
    after_faces[at, LANES:] = jnp.where(pitch_odd, pitch_b[...], pitch_a[...])
    scale = gain * lift_factor(1)
    for e in range(2):
        lanes = slice(e * LANES, (e + 1) * LANES)
        for s in range(5):
            add(40 + 2 * s + e, 50, -scale * mixed_faces(after_faces, s, lanes, 1, -1.0))
            add(2 * s + e, 50, scale * mixed_faces(before_faces, s, lanes, 1, 1.0))

    wake = arrived[WAKE_ROW : WAKE_ROW + 2]
    moved = flags[0:1, 2:3] > 0.5
    rows = lax.broadcasted_iota(jnp.int32, (25, LANES), 0)
    cols = lax.broadcasted_iota(jnp.int32, (25, LANES), 1)
    for e in range(2):
        row = jnp.where(moved, wake[1 - e : 2 - e], wake[e : e + 1])
        columns = [
            jnp.sum(jnp.where(cols == rows + 25 * v, row, 0.0), axis=1, keepdims=True)
            for v in range(5)
        ]
        inlet = combine(gain * lift_factor(0) * half_flux(0, 1.0), columns)
        for v in range(5):
            add(v * 250 + e, 2, jnp.where(cols == 0, inlet[v], 0.0))

    copies = []
    for v in range(5):
        part = pl.ds(v * 250, 250)
        copies.append(pltpu.make_async_copy(result.at[part], out.at[part], done.at[v]))
        copies[-1].start()
    for copy in copies:
        copy.wait()


IN_VMEM = pl.BlockSpec(memory_space=pltpu.VMEM)
IN_SMEM = pl.BlockSpec(memory_space=pltpu.SMEM)


def call(kernel, name, outs, args, in_specs=(), scratch=(), flops=0, out_spec=IN_VMEM):
    in_specs = list(in_specs)
    return pl.pallas_call(
        kernel,
        name=name,
        out_shape=[jax.ShapeDtypeStruct(shape, dtype) for shape, dtype in outs],
        in_specs=in_specs + [IN_VMEM] * (len(args) - len(in_specs)),
        out_specs=[out_spec] * len(outs),
        scratch_shapes=list(scratch),
        compiler_params=pltpu.CompilerParams(vmem_limit_bytes=VMEM_LIMIT),
        cost_estimate=pl.CostEstimate(flops=flops, bytes_accessed=2**20, transcendentals=0),
    )(*args)


def swapped(value, axis, odd):
    pitch, span = (lax.axis_size("pitch"), lax.axis_size("span"))
    pairs = []
    for i in range(pitch):
        for j in range(span):
            if axis == "pitch":
                other = ((i + (1 if i % 2 == odd else -1)) % pitch, j)
            else:
                other = (i, j + (1 if j % 2 == odd else -1))
                if not 0 <= other[1] < span:
                    other = (i ^ 1, j)
            pairs.append((i * span + j, other[0] * span + other[1]))
    return lax.ppermute(value, ("pitch", "span"), pairs)


def span_exchanged(faces):
    return swapped(faces[0], "span", 0), swapped(faces[1], "span", 1)


def pitch_exchanged(faces):
    return swapped(faces[1], "pitch", 1), swapped(faces[0], "pitch", 0)


F32 = jnp.float32
PITCH_OUTS = [((BLOCK, LANES), F32), ((BLOCK, LANES), F32), ((2 * BLOCK, LANES), F32)]
SPAN_OUTS = [((SPAN_ROWS, 2 * LANES), F32)] * 2
SMALL_OUT = ((8, LANES), F32)
NEAR_OUTS = [((4 * BLOCK, 2 * LANES), jnp.bfloat16)] * 2
FAR_OUTS = [((2 * BLOCK, 2 * LANES), jnp.bfloat16)] * 2
STATE_OUT = ((ROWS, 2 * LANES), F32)
TRACE_OUT = ((TRACES, 2 * LANES), F32)


def shards(table, links, state, wake_planes, bar_offsets):
    x = state.reshape(-1, 1, LANES)
    wake = wake_planes.transpose(0, 1, 3, 4, 2).reshape(50, 1, 5)
    faces = call(begin_span_kernel, "begin_span", SPAN_OUTS, [x], flops=10**10)
    span = span_exchanged(faces)
    *faces, inner = call(begin_pitch_kernel, "begin_pitch", PITCH_OUTS, [x, wake], flops=10**10)
    pitch = pitch_exchanged(faces)
    base, partial, traces, flags = call(
        first_kernel,
        "first",
        [STATE_OUT, STATE_OUT, TRACE_OUT, SMALL_OUT],
        [bar_offsets, x, table],
        in_specs=[IN_SMEM],
        flops=10**9,
    )
    buffers = [pltpu.VMEM(shape, dtype) for shape, dtype in [STATE_OUT] + FAR_OUTS]
    for section in range(2):
        odd, even = pitch
        near_faces, *near = call(
            functools.partial(near_kernel, section),
            "near",
            [TRACE_OUT] + NEAR_OUTS,
            [*span, even, inner, traces, links],
            flops=10**8,
        )
        next_a, next_b, inner, *faces = call(
            functools.partial(far_kernel, section),
            "far",
            PITCH_OUTS + SPAN_OUTS,
            [flags, odd, even, near_faces],
            scratch=[
                pltpu.VMEM(shape, F32)
                for shape in (
                    (TRACES, LANES),
                    (TRACES, LANES),
                    (BLOCK + 2 * FACE_PAD, LANES),
                    (BLOCK, LANES),
                )
            ],
            flops=10**8,
        )
        span = span_exchanged(faces)
        pitch = pitch_exchanged([next_a, next_b])
        args = [base, partial, *near, flags, odd, even, table, links]
        if section == 0:
            partial, traces = call(
                later_kernel, "later", [STATE_OUT, TRACE_OUT], args, scratch=buffers, flops=10**9
            )
    (rows,) = call(
        last_kernel,
        "last",
        [(x.shape, F32)],
        args,
        scratch=buffers + buffers[:1],
        flops=10**9,
    )
    (out,) = call(
        final_kernel,
        "final",
        [(x.shape, F32)],
        [flags, span[0], span[1], pitch[0], pitch[1], inner, rows],
        scratch=[
            pltpu.VMEM(x.shape, F32),
            *[pltpu.VMEM((BLOCK + 2 * FACE_PAD, 2 * LANES), F32)] * 2,
            pltpu.SemaphoreType.DMA((5,)),
        ],
        flops=10**8,
        out_spec=pl.BlockSpec(memory_space=pl.ANY),
    )
    return out.reshape(state.shape)


def solution(mesh):
    volume, lift, trace, link = operator_tables()
    high, low = split_table(volume)
    table = np.concatenate([exact_table(trace), high, low])
    reached = [
        v * PER_VAR + r for v in range(5) for r in (*range(MAIN), *range(TAIL, PER_VAR))
    ]
    inlet = np.zeros((5 * INLET_ROWS, HALO))
    inlet[:, :BLOCK] = lift[reached, 4 * BLOCK :]
    lift[reached, 4 * BLOCK :] = 0.0
    assert not lift[:, 4 * BLOCK :].any()
    links = np.concatenate([exact_table(t) for t in (link, lift, inlet)])
    in_specs = (
        P(None, None, None, None, "pitch", "span", None),
        P(None, None, None, "pitch", "span"),
        P(),
    )
    out_specs = P(None, None, None, None, "pitch", "span", None)
    return jax.shard_map(
        functools.partial(shards, jnp.asarray(table), jnp.asarray(links)),
        mesh=mesh,
        in_specs=in_specs,
        out_specs=out_specs,
        check_vma=False,
    )
```

```python
import functools

import jax
import jax.numpy as jnp
import ml_dtypes
import numpy as np
from jax import lax
from jax.experimental import pallas as pl
from jax.experimental.pallas import tpu as pltpu
from jax.sharding import PartitionSpec as P

MEAN_FLOW = (0.5, 0.3, 0.0)
WAVE_SPEED = (1.5, 1.3, 1.0)
ELEM_SIZE = (1.0, 0.8, 1.2)
END_WEIGHT = 0.1
TIME_STEP = 0.01
KEEP = (0.0, 0.75, 1.0 / 3.0)
GAIN = (1.0, 0.25, 2.0 / 3.0)

ORDER = (1, 4, 2, 3, 0)
MAIN = 24
TAIL = 5 * MAIN
PER_VAR = 128
ROWS = 5 * PER_VAR
INLET_ROWS = 32
TILES = ((0, 0, 2), (1, 2, 4), (4, 4, 5))
BLOCK = 128
SPAN_ROWS = 104
TRACES = 4 * BLOCK
HALO = 5 * BLOCK
WAKE_ROW = 125
FACE_PAD = 16
HIGH_AT = TRACES
LOW_AT = HIGH_AT + ROWS
LIFT_AT = TRACES
INLET_AT = LIFT_AT + ROWS
LANES = 128
VMEM_LIMIT = 24 * 1024 * 1024


def derivative_table():
    points = np.array([-1.0, -np.sqrt(3.0 / 7.0), 0.0, np.sqrt(3.0 / 7.0), 1.0])
    products = np.array(
        [np.prod([points[j] - points[k] for k in range(5) if k != j]) for j in range(5)]
    )
    matrix = np.zeros((5, 5))
    for i in range(5):
        for j in range(5):
            if i != j:
                matrix[i, j] = products[i] / (products[j] * (points[i] - points[j]))
        matrix[i, i] = sum((1.0 / (points[i] - points[k]) for k in range(5) if k != i))
    return matrix


def flux_matrix(direction):
    flux = MEAN_FLOW[direction] * np.eye(5)
    flux[0, 1 + direction] += 1.0
    flux[4, 1 + direction] += 1.0
    flux[1 + direction, 4] += 1.0
    return flux


def half_flux(direction, sign):
    return 0.5 * (flux_matrix(direction) + sign * WAVE_SPEED[direction] * np.eye(5))


def lift_factor(direction):
    return TIME_STEP * 2.0 / (ELEM_SIZE[direction] * END_WEIGHT)


def half_scales():
    return (lift_factor(1) / 10.0, lift_factor(1), lift_factor(2), lift_factor(2), lift_factor(0))


def var_start(v):
    return ORDER.index(v) * PER_VAR


def node_row(v, a, p, s):
    node = p * 5 + s
    return var_start(v) + (a * MAIN + node if node < MAIN else TAIL + a)


def operator_tables():
    deriv = derivative_table()
    volume = np.zeros((ROWS, ROWS))
    lift = np.zeros((ROWS, HALO))
    trace = np.zeros((TRACES, ROWS))
    fluxes = [flux_matrix(d) for d in range(3)]
    plus = [half_flux(d, 1.0) for d in range(3)]
    minus = [half_flux(d, -1.0) for d in range(3)]
    plus_sent, minus_sent = (plus[2][:4], minus[2][:4])
    back_plus = np.vstack([np.eye(4), [[0.0, 0.0, 0.0, 1.0]]])
    back_minus = np.vstack([np.eye(4), [[0.0, 0.0, 0.0, -1.0]]])
    assert np.allclose(back_plus @ plus_sent, plus[2])
    assert np.allclose(back_minus @ minus_sent, minus[2])
    for a in range(5):
        for p in range(5):
            for s in range(5):
                here = [node_row(v, a, p, s) for v in range(5)]
                place = (a, p, s)
                for d in range(3):
                    for j in range(5):
                        there = list(place)
                        there[d] = j
                        cols = [node_row(v, *there) for v in range(5)]
                        coeff = -TIME_STEP * (2.0 / ELEM_SIZE[d]) * deriv[place[d], j]
                        volume[np.ix_(here, cols)] += coeff * fluxes[d]
                for d in (1, 2):
                    if place[d] == 4:
                        volume[np.ix_(here, here)] += lift_factor(d) * minus[d]
                    if place[d] == 0:
                        volume[np.ix_(here, here)] -= lift_factor(d) * plus[d]
                if p == 0:
                    cols = [s * 25 + v * 5 + a for v in range(5)]
                    lift[np.ix_(here, cols)] += lift_factor(1) * plus[1]
                    for v in range(5):
                        trace[BLOCK + s * 25 + v * 5 + a, here[v]] = 1.0
                if p == 4:
                    cols = [BLOCK + s * 25 + v * 5 + a for v in range(5)]
                    lift[np.ix_(here, cols)] -= lift_factor(1) * minus[1]
                    for v in range(5):
                        trace[s * 25 + v * 5 + a, here[v]] = 1.0
                if s == 0:
                    cols = [2 * BLOCK + c * 25 + a * 5 + p for c in range(4)]
                    lift[np.ix_(here, cols)] += lift_factor(2) * back_plus
                    rows = [3 * BLOCK + c * 25 + a * 5 + p for c in range(4)]
                    trace[np.ix_(rows, here)] += minus_sent
                if s == 4:
                    cols = [3 * BLOCK + c * 25 + a * 5 + p for c in range(4)]
                    lift[np.ix_(here, cols)] -= lift_factor(2) * back_minus
                    rows = [2 * BLOCK + c * 25 + a * 5 + p for c in range(4)]
                    trace[np.ix_(rows, here)] += plus_sent
                if a == 0:
                    cols = [4 * BLOCK + v * 25 + p * 5 + s for v in range(5)]
                    lift[np.ix_(here, cols)] += lift_factor(0) * plus[0]
    lift = lift / np.repeat(half_scales(), BLOCK)
    return volume, lift, trace, trace @ lift


def exact_table(table):
    exact = table.astype(ml_dtypes.bfloat16)
    assert np.allclose(exact.astype(np.float64), table, rtol=1e-12, atol=1e-12)
    return exact


def split_table(table):
    high = table.astype(ml_dtypes.bfloat16)
    low = (table - high.astype(np.float64)).astype(ml_dtypes.bfloat16)
    return high, low


def split(values):
    high = values.astype(jnp.bfloat16)
    low = (values - high.astype(jnp.float32)).astype(jnp.bfloat16)
    return high, low


def dot(left, right):
    return jnp.dot(left, right, preferred_element_type=jnp.float32)


def product(table, high, low):
    return dot(table, high) + dot(table, low)


def with_rows(values, first, extra):
    rows = lax.broadcasted_iota(jnp.int32, values.shape, 0)
    for k, row in enumerate(extra):
        values = jnp.where(rows == first + k, row, values)
    return values


def emit_pitch_faces(traces, wake, pitch_odd, pitch_a, pitch_b, inner):
    upper, lower = traces[0:BLOCK], traces[BLOCK : 2 * BLOCK]
    up = with_rows(upper[:, LANES:], WAKE_ROW, wake)
    down = lower[:, :LANES]
    pitch_a[...] = jnp.where(pitch_odd, down, up)
    pitch_b[...] = jnp.where(pitch_odd, up, down)
    inner[0:BLOCK] = upper[:, :LANES]
    inner[BLOCK:] = lower[:, LANES:]


def emit_span_faces(traces, span_odd, span_a, span_b):
    above, below = traces[0:SPAN_ROWS], traces[BLOCK : BLOCK + SPAN_ROWS]
    span_a[...] = jnp.where(span_odd, below, above)
    span_b[...] = jnp.where(span_odd, above, below)


def parities():
    return lax.axis_index("pitch") % 2 == 1, lax.axis_index("span") % 2 == 1


def combine(table, values):
    return [
        sum(float(table[i, j]) * values[j] for j in range(5) if table[i, j] != 0.0)
        for i in range(table.shape[0])
    ]


def begin_span_kernel(x, span_a, span_b):
    flat = x.reshape(x.shape[0], LANES)
    _, span_odd = parities()
    rest = jnp.zeros((SPAN_ROWS - 96, LANES), jnp.float32)
    for e in range(2):
        lanes = slice(e * LANES, (e + 1) * LANES)
        sides = []
        for s, sign in ((4, 1.0), (0, -1.0)):
            faces = [flat[pl.ds(v * 250 + 2 * s + e, 25, stride=10), :] for v in range(5)]
            sides.append(combine(half_flux(2, sign)[:4], faces))
        span_a[96:SPAN_ROWS, lanes] = rest
        span_b[96:SPAN_ROWS, lanes] = rest
        for c in range(4):
            above, below = (sides[0][c], sides[1][c])
            span_a[c * 25 : c * 25 + 25, lanes] = jnp.where(span_odd, below, above)
            span_b[c * 25 : c * 25 + 25, lanes] = jnp.where(span_odd, above, below)


def begin_pitch_kernel(x, wake, pitch_a, pitch_b, inner):
    flat = x.reshape(x.shape[0], LANES)
    pitch_odd, _ = parities()
    planes = wake.reshape(50, 5)[...]
    rows = lax.broadcasted_iota(jnp.int32, (50, LANES), 0)
    cols = lax.broadcasted_iota(jnp.int32, (50, LANES), 1)
    spread = jnp.zeros((50, LANES), jnp.float32)
    for s in range(5):
        mine = (cols - s) == 5 * (rows // 2)
        spread = jnp.where(mine, planes[:, s : s + 1], spread)
    own = [
        jnp.sum(jnp.where(rows % 2 == k, spread, 0.0), axis=0, keepdims=True) for k in range(2)
    ]
    tail = jnp.zeros((8, LANES), jnp.float32)
    up_tail = with_rows(tail, WAKE_ROW - 120, own)
    pitch_a[120:BLOCK] = jnp.where(pitch_odd, tail, up_tail)
    pitch_b[120:BLOCK] = jnp.where(pitch_odd, up_tail, tail)
    inner[120:BLOCK] = tail
    inner[BLOCK + 120 :] = tail
    for s in range(5):
        at = slice(s * 25, s * 25 + 25)
        upper, lower = (
            [flat[pl.ds(p * 10 + 2 * s + e, 25, stride=50), :] for e in range(2)] for p in (4, 0)
        )
        pitch_a[at] = jnp.where(pitch_odd, lower[0], upper[1])
        pitch_b[at] = jnp.where(pitch_odd, upper[1], lower[0])
        inner[at] = upper[0]
        inner[BLOCK + s * 25 : BLOCK + s * 25 + 25] = lower[1]


def load_state(x, state):
    flat = x.reshape(x.shape[0], LANES)
    for e in range(2):
        lanes = slice(e * LANES, (e + 1) * LANES)
        for v in range(5):
            base = var_start(v)
            first = v * 250 + e
            for a in range(5):
                at = base + a * MAIN
                state[at : at + MAIN, lanes] = flat[pl.ds(first + a * 50, MAIN, stride=2), :]
            tail = base + TAIL
            state[tail : tail + 8, lanes] = jnp.zeros((8, LANES), jnp.float32)
            state[tail : tail + 5, lanes] = flat[pl.ds(first + 2 * MAIN, 5, stride=50), :]


def add_axial_terms(gain, state, partial):
    lanes = lax.broadcasted_iota(jnp.int32, (MAIN + 8, LANES), 1)
    rows = lax.broadcasted_iota(jnp.int32, (8, LANES), 0)
    for e in range(2):
        own = slice(e * LANES, (e + 1) * LANES)
        upper_gap, lower_gap = ([], [])
        for v in range(5):
            base = var_start(v)
            lower = state[base : base + MAIN, own]
            upper = state[base + 4 * MAIN : base + TAIL, own]
            tail = state[base + TAIL : base + PER_VAR, own]
            turned = pltpu.roll(tail, 4, 0)
            join = lambda main, end: jnp.concatenate([main, end], axis=0)
            after = pltpu.roll(join(lower, turned), LANES - 1, 1)
            before = pltpu.roll(join(upper, turned), 1, 1)
            upper = join(upper, tail)
            upper_gap.append(jnp.where(lanes == LANES - 1, 0.0, upper - after))
            lower_gap.append(jnp.where(lanes == 0, 0.0, before) - join(lower, tail))
        mixed = []
        for gap, sign in ((upper_gap, -1.0), (lower_gap, 1.0)):
            mixed.append(combine(gain * lift_factor(0) * half_flux(0, sign), gap))
        for v in range(5):
            base = var_start(v)
            upper, lower = (mixed[0][v], mixed[1][v])
            partial[base : base + MAIN, own] += lower[:MAIN]
            partial[base + 4 * MAIN : base + TAIL, own] += upper[:MAIN]
            ends = jnp.where(rows == 0, lower[MAIN:], jnp.where(rows == 4, upper[MAIN:], 0.0))
            partial[base + TAIL : base + PER_VAR, own] += ends


def volume_rate(table, high, low):
    rate = [None] * 5
    for first, start, stop in TILES:
        part = slice(start * PER_VAR, stop * PER_VAR)
        table_high, table_low = (
            table[at + first * PER_VAR : at + ROWS, part] for at in (HIGH_AT, LOW_AT)
        )
        term = product(table_high, high[part], low[part]) + dot(table_low, high[part])
        for v in range(first, 5):
            block = term[(v - first) * PER_VAR : (v - first + 1) * PER_VAR]
            rate[v] = block if rate[v] is None else rate[v] + block
    return jnp.concatenate(rate, axis=0)


def phase(run):
    pl.when(lax.axis_index("span") >= 0)(run)


def advance_body(section, base, state, table, partial, faces):
    gain, keep = GAIN[section], KEEP[section]

    @phase
    def _():
        rate = volume_rate(table, *split(state[...]))
        if keep == 0.0:
            partial[...] = state[...] + rate
        else:
            partial[...] = keep * base[...] + gain * (state[...] + rate)

    @phase
    def _():
        add_axial_terms(gain, state, partial)

    if faces is not None:
        faces[...] = product(table[0:TRACES], *split(partial[...]))


def add_halo(section, before, near, far, links, state, far_high, far_low):
    gain = GAIN[section]
    gather_far(section, *far, far_high, far_low)
    side = pl.multiple_of(lax.axis_index("pitch") % 2 * BLOCK, BLOCK)
    rows = slice(LIFT_AT, LIFT_AT + ROWS)
    near_high, near_low = near
    state[...] = before[...] + gain * (
        product(links[rows, : 4 * BLOCK], near_high[...], near_low[...])
        + product(links[rows, pl.ds(side, BLOCK)], far_high[0:BLOCK], far_low[0:BLOCK])
    )
    added = gain * product(
        links[INLET_AT : INLET_AT + 5 * INLET_ROWS, 0:BLOCK], far_high[BLOCK:], far_low[BLOCK:]
    )
    for k in range(5):
        start, at = (k * PER_VAR, k * INLET_ROWS)
        state[start : start + MAIN] += added[at : at + MAIN]
        state[start + TAIL : start + PER_VAR] += added[at + MAIN : at + INLET_ROWS]


def first_kernel(offsets, x, table, base, partial, faces, flags):
    cols = lax.broadcasted_iota(jnp.int32, flags.shape, 1)
    moved = jnp.zeros(flags.shape, jnp.float32)
    for k in range(3):
        moved = jnp.where((cols == k) & (offsets[k] % 2 == 1), 1.0, moved)
    flags[...] = moved
    load_state(x, base)
    advance_body(0, None, base, table, partial, faces)


def later_kernel(
    base, before, near_high, near_low, flags, pitch_b, pitch_a, table, links, partial, faces,
    state, far_high, far_low,
):
    near, far = ((near_high, near_low), (flags, pitch_a, pitch_b))
    add_halo(0, before, near, far, links, state, far_high, far_low)
    advance_body(1, base, state, table, partial, faces)


def put_halo(halo_high, halo_low, block, first, scale, values):
    at = (slice(block * BLOCK, (block + 1) * BLOCK), slice(first, first + values.shape[1]))
    halo_high[at], halo_low[at] = split(scale * values)


def gather_near(pitch_a, span_a, span_b, inner, halo_high, halo_low):
    put = functools.partial(put_halo, halo_high, halo_low)
    scales = half_scales()
    pitch_odd, span_odd = parities()
    near = pitch_a[...]
    put(0, 0, scales[0], jnp.where(pitch_odd, near, 0.0))
    put(0, LANES, scales[0], inner[0:BLOCK])
    put(1, 0, scales[1], inner[BLOCK:])
    put(1, LANES, scales[1], jnp.where(pitch_odd, 0.0, near))
    above = jnp.where(span_odd, span_b[...], span_a[...])
    below = jnp.where(span_odd, span_a[...], span_b[...])
    place = lax.axis_index("span")
    above = jnp.where(place == lax.axis_size("span") - 1, 0.0, above)
    below = jnp.where(place == 0, 0.0, below)
    rest = jnp.zeros((BLOCK - SPAN_ROWS, 2 * LANES), jnp.float32)
    put(2, 0, scales[2], jnp.concatenate([below, rest], axis=0))
    put(3, 0, scales[3], jnp.concatenate([above, rest], axis=0))


def arrived_wake(pitch_a, pitch_b):
    pitch_odd, _ = parities()
    rows = slice(WAKE_ROW, WAKE_ROW + 2)
    return jnp.where(pitch_odd, pitch_a[rows], pitch_b[rows])


def inlet_row(section, flags, wake, e):
    moved = flags[0:1, section : section + 1] > 0.5
    return jnp.where(moved, wake[1 - e : 2 - e], wake[e : e + 1])


def gather_far(section, flags, pitch_a, pitch_b, halo_high, halo_low):
    put = functools.partial(put_halo, halo_high, halo_low)
    scales = half_scales()
    pitch_odd, _ = parities()
    far = jnp.where(pitch_odd, scales[1], scales[0]) * pitch_b[...]
    put(0, 0, 1.0, jnp.where(pitch_odd, 0.0, far))
    put(0, LANES, 1.0, jnp.where(pitch_odd, far, 0.0))
    wake = arrived_wake(pitch_a, pitch_b)
    rows = lax.broadcasted_iota(jnp.int32, (BLOCK, LANES), 0)
    cols = lax.broadcasted_iota(jnp.int32, (BLOCK, LANES), 1)
    for e in range(2):
        row = inlet_row(section, flags, wake, e)
        column = jnp.sum(jnp.where(rows == cols, row, 0.0), axis=1, keepdims=True)
        put(1, e * LANES, scales[4], jnp.where(cols == 0, column, 0.0))


def near_kernel(
    section, span_a, span_b, pitch_a, inner, faces, links, near_faces, halo_high, halo_low
):
    gather_near(pitch_a, span_a, span_b, inner, halo_high, halo_low)
    for half in range(2):
        at = slice(half * 2 * BLOCK, (half + 1) * 2 * BLOCK)
        near_faces[at] = faces[at] + GAIN[section] * dot(
            links[at, : 4 * BLOCK], halo_high[...]
        )


def from_lanes(row, moves):
    lanes = lax.broadcasted_iota(jnp.int32, row.shape, 1)
    total = None
    for factor, start, stop, distance in moves:
        moved = pltpu.roll(row, distance % LANES, 1) if distance else row
        term = jnp.where((lanes >= start) & (lanes < stop), factor * moved, 0.0)
        total = term if total is None else total + term
    return total


def lane_moves(table):
    return [
        (float(table[i, j]), 25 * i, 25 * i + 25, 25 * (i - j))
        for i in range(table.shape[0])
        for j in range(table.shape[1])
        if table[i, j] != 0.0
    ]


def far_lift(gain, pitch_b, faces):
    pitch_odd, _ = parities()
    faces[FACE_PAD : FACE_PAD + BLOCK] = pitch_b[...]
    plus, minus = (half_flux(1, 1.0), half_flux(1, -1.0))
    scale = gain * lift_factor(1)
    assert np.allclose(plus - np.diag(np.diag(plus)), minus - np.diag(np.diag(minus)))
    factor = lambda i, j: jnp.where(
        pitch_odd, -scale * float(minus[i, j]), scale * float(plus[i, j])
    )
    rows = lax.broadcasted_iota(jnp.int32, (BLOCK, LANES), 0)
    place = rows - 25 * sum((rows >= 25 * s).astype(jnp.int32) for s in range(1, 5))
    total = factor(0, 0) * pitch_b[...]
    for i in range(5):
        for j in range(5):
            if i != j and plus[i, j] != 0.0:
                at = FACE_PAD + 5 * (j - i)
                here = (place >= 5 * i) & (place < 5 * i + 5)
                total = total + jnp.where(here, factor(i, j) * faces[at : at + BLOCK], 0.0)
    return jnp.where(rows < WAKE_ROW, total, 0.0)


def far_kernel(
    section, flags, pitch_b, pitch_a, near_faces,
    next_pitch_a, next_pitch_b, next_inner, next_span_a, next_span_b, *refs
):
    *traces, faces, lifted = refs
    pitch_odd, span_odd = parities()
    gain = GAIN[section]
    for e in range(2):
        traces[e][...] = near_faces[:, e * LANES : (e + 1) * LANES]

    def add(start, count, stride, e, values):
        at = pl.ds(start, count, stride=stride) if stride > 1 else pl.ds(start, count)
        traces[e][at, :] = traces[e][at, :] + values

    total = far_lift(gain, pitch_b, faces)
    lifted[...] = total
    add(0, BLOCK, 1, 1, jnp.where(pitch_odd, total, 0.0))
    add(BLOCK, BLOCK, 1, 0, jnp.where(pitch_odd, 0.0, total))
    for block, s, sign in ((2, 4, 1.0), (3, 0, -1.0)):
        edge = [lifted[s * 25 + 5 * v : s * 25 + 5 * v + 5] for v in range(5)]
        for c, values in enumerate(combine(half_flux(2, sign)[:4], edge)):
            start = block * BLOCK + c * 25
            add(start + 4, 5, 5, 1, jnp.where(pitch_odd, values, 0.0))
            add(start, 5, 5, 0, jnp.where(pitch_odd, 0.0, values))

    wake = arrived_wake(pitch_a, pitch_b)
    rows = lax.broadcasted_iota(jnp.int32, (5, LANES), 0)
    cols = lax.broadcasted_iota(jnp.int32, (5, LANES), 1)
    for e in range(2):

        def add_column(start, stride, row, first, step):
            picked = jnp.where(cols == first + step * rows, row, 0.0)
            column = jnp.sum(picked, axis=1, keepdims=True)
            add(start, 5, stride, e, jnp.where(cols == 0, column, 0.0))

        row = jnp.broadcast_to(inlet_row(section, flags, wake, e), (8, LANES))
        row = from_lanes(row, lane_moves(gain * lift_factor(0) * half_flux(0, 1.0)))
        for block, p in ((0, 4), (1, 0)):
            for s in range(5):
                add_column(block * BLOCK + s * 25, 5, row[0:1], p * 5 + s, 25)
        for block, s, sign in ((2, 4, 1.0), (3, 0, -1.0)):
            sent = from_lanes(row, lane_moves(half_flux(2, sign)[:4]))
            for c in range(4):
                add_column(block * BLOCK + c * 25, 1, sent[0:1], c * 25 + s, 5)

    both = jnp.concatenate([traces[0][...], traces[1][...]], axis=1)
    emit_span_faces(both[2 * BLOCK :], span_odd, next_span_a, next_span_b)
    emit_pitch_faces(
        both[: 2 * BLOCK], [wake[0:1], wake[1:2]], pitch_odd, next_pitch_a, next_pitch_b,
        next_inner,
    )


def last_kernel(
    base, before, near_high, near_low, flags, pitch_b, pitch_a, table, links, rows,
    state, far_high, far_low, partial,
):
    near, far = ((near_high, near_low), (flags, pitch_a, pitch_b))
    add_halo(1, before, near, far, links, state, far_high, far_low)
    advance_body(2, base, state, table, partial, None)
    flat = rows.reshape(rows.shape[0], LANES)
    for e in range(2):
        lanes = slice(e * LANES, (e + 1) * LANES)
        for v in range(5):
            start = var_start(v)
            first = v * 250 + e
            for a in range(5):
                at = start + a * MAIN
                flat[pl.ds(first + a * 50, MAIN, stride=2), :] = partial[at : at + MAIN, lanes]
            tail = start + TAIL
            flat[pl.ds(first + 2 * MAIN, 5, stride=50), :] = partial[tail : tail + 5, lanes]


def mixed_faces(faces, s, lanes, direction, sign):
    table = half_flux(direction, sign)
    at = FACE_PAD + s * 25
    rows = lax.broadcasted_iota(jnp.int32, (25, LANES), 0)
    own = faces[at : at + 25, lanes]
    total = float(table[0, 0]) * own
    for i in range(5):
        for j in range(5):
            if i != j and table[i, j] != 0.0:
                moved = faces[at + 5 * (j - i) : at + 5 * (j - i) + 25, lanes]
                here = (rows >= 5 * i) & (rows < 5 * i + 5)
                total = total + jnp.where(here, float(table[i, j]) * moved, 0.0)
    return total


def final_near_kernel(
    span_a, span_b, pitch_a, inner, before, result, after_faces, before_faces
):
    flat = result.reshape(result.shape[0], LANES)
    flat[...] = before.reshape(before.shape[0], LANES)[...]
    pitch_odd, span_odd = parities()
    gain = GAIN[2]

    def add(start, stride, values):
        at = pl.ds(start, values.shape[0], stride=stride)
        flat[at, :] = flat[at, :] + values

    place = lax.axis_index("span")
    scale = gain * lift_factor(2)
    up_scale = jnp.where(place == lax.axis_size("span") - 1, 0.0, -scale)
    down_scale = jnp.where(place == 0, 0.0, scale)
    for e in range(2):
        lanes = slice(e * LANES, (e + 1) * LANES)
        for c in range(4):
            at = slice(c * 25, c * 25 + 25)
            first, second = (span_a[at, lanes], span_b[at, lanes])
            above = up_scale * jnp.where(span_odd, second, first)
            below = down_scale * jnp.where(span_odd, first, second)
            add(c * 250 + 8 + e, 10, above)
            add(c * 250 + e, 10, below)
            if c == 3:
                add(4 * 250 + 8 + e, 10, -above)
                add(4 * 250 + e, 10, below)

    at = slice(FACE_PAD, FACE_PAD + BLOCK)
    near = pitch_a[...]
    before_faces[at, :LANES] = jnp.where(pitch_odd, near, 0.0)
    before_faces[at, LANES:] = inner[0:BLOCK]
    after_faces[at, :LANES] = inner[BLOCK:]
    after_faces[at, LANES:] = jnp.where(pitch_odd, 0.0, near)
    scale = gain * lift_factor(1)
    for e in range(2):
        lanes = slice(e * LANES, (e + 1) * LANES)
        for s in range(5):
            add(40 + 2 * s + e, 50, -scale * mixed_faces(after_faces, s, lanes, 1, -1.0))
            add(2 * s + e, 50, scale * mixed_faces(before_faces, s, lanes, 1, 1.0))


def final_kernel(flags, pitch_b, pitch_a, near, out, result, faces, lifted, done):
    flat = result.reshape(result.shape[0], LANES)
    flat[...] = near.reshape(near.shape[0], LANES)[...]
    pitch_odd, _ = parities()
    gain = GAIN[2]

    def add(start, stride, values):
        at = pl.ds(start, values.shape[0], stride=stride)
        flat[at, :] = flat[at, :] + values

    lifted[...] = far_lift(gain, pitch_b, faces)
    for s in range(5):
        values = lifted[s * 25 : s * 25 + 25]
        add(40 + 2 * s + 1, 50, jnp.where(pitch_odd, values, 0.0))
        add(2 * s, 50, jnp.where(pitch_odd, 0.0, values))

    wake = arrived_wake(pitch_a, pitch_b)
    rows = lax.broadcasted_iota(jnp.int32, (25, LANES), 0)
    cols = lax.broadcasted_iota(jnp.int32, (25, LANES), 1)
    for e in range(2):
        row = inlet_row(2, flags, wake, e)
        columns = [
            jnp.sum(jnp.where(cols == rows + 25 * v, row, 0.0), axis=1, keepdims=True)
            for v in range(5)
        ]
        inlet = combine(gain * lift_factor(0) * half_flux(0, 1.0), columns)
        for v in range(5):
            add(v * 250 + e, 2, jnp.where(cols == 0, inlet[v], 0.0))

    copies = []
    for v in range(5):
        part = pl.ds(v * 250, 250)
        copies.append(pltpu.make_async_copy(result.at[part], out.at[part], done.at[v]))
        copies[-1].start()
    for copy in copies:
        copy.wait()


IN_VMEM = pl.BlockSpec(memory_space=pltpu.VMEM)
IN_SMEM = pl.BlockSpec(memory_space=pltpu.SMEM)


def call(kernel, name, outs, args, in_specs=(), scratch=(), flops=0, out_spec=IN_VMEM):
    in_specs = list(in_specs)
    return pl.pallas_call(
        kernel,
        name=name,
        out_shape=[jax.ShapeDtypeStruct(shape, dtype) for shape, dtype in outs],
        in_specs=in_specs + [IN_VMEM] * (len(args) - len(in_specs)),
        out_specs=[out_spec] * len(outs),
        scratch_shapes=list(scratch),
        compiler_params=pltpu.CompilerParams(vmem_limit_bytes=VMEM_LIMIT),
        cost_estimate=pl.CostEstimate(flops=flops, bytes_accessed=2**20, transcendentals=0),
    )(*args)


def swapped(value, axis, odd):
    pitch, span = (lax.axis_size("pitch"), lax.axis_size("span"))
    pairs = []
    for i in range(pitch):
        for j in range(span):
            if axis == "pitch":
                other = ((i + (1 if i % 2 == odd else -1)) % pitch, j)
            else:
                other = (i, j + (1 if j % 2 == odd else -1))
                if not 0 <= other[1] < span:
                    other = (i ^ 1, j)
            pairs.append((i * span + j, other[0] * span + other[1]))
    return lax.ppermute(value, ("pitch", "span"), pairs)


def span_exchanged(faces):
    return swapped(faces[0], "span", 0), swapped(faces[1], "span", 1)


def pitch_exchanged(faces):
    return swapped(faces[1], "pitch", 1), swapped(faces[0], "pitch", 0)


F32 = jnp.float32
PITCH_OUTS = [((BLOCK, LANES), F32), ((BLOCK, LANES), F32), ((2 * BLOCK, LANES), F32)]
SPAN_OUTS = [((SPAN_ROWS, 2 * LANES), F32)] * 2
SMALL_OUT = ((8, LANES), F32)
NEAR_OUTS = [((4 * BLOCK, 2 * LANES), jnp.bfloat16)] * 2
FAR_OUTS = [((2 * BLOCK, 2 * LANES), jnp.bfloat16)] * 2
STATE_OUT = ((ROWS, 2 * LANES), F32)
TRACE_OUT = ((TRACES, 2 * LANES), F32)


def shards(table, links, state, wake_planes, bar_offsets):
    x = state.reshape(-1, 1, LANES)
    wake = wake_planes.transpose(0, 1, 3, 4, 2).reshape(50, 1, 5)
    faces = call(begin_span_kernel, "begin_span", SPAN_OUTS, [x], flops=10**10)
    span = span_exchanged(faces)
    *faces, inner = call(begin_pitch_kernel, "begin_pitch", PITCH_OUTS, [x, wake], flops=10**10)
    pitch = pitch_exchanged(faces)
    base, partial, traces, flags = call(
        first_kernel,
        "first",
        [STATE_OUT, STATE_OUT, TRACE_OUT, SMALL_OUT],
        [bar_offsets, x, table],
        in_specs=[IN_SMEM],
        flops=10**9,
    )
    buffers = [pltpu.VMEM(shape, dtype) for shape, dtype in [STATE_OUT] + FAR_OUTS]
    for section in range(2):
        odd, even = pitch
        near_faces, *near = call(
            functools.partial(near_kernel, section),
            "near",
            [TRACE_OUT] + NEAR_OUTS,
            [*span, even, inner, traces, links],
            flops=10**8,
        )
        next_a, next_b, inner, *faces = call(
            functools.partial(far_kernel, section),
            "far",
            PITCH_OUTS + SPAN_OUTS,
            [flags, odd, even, near_faces],
            scratch=[
                pltpu.VMEM(shape, F32)
                for shape in (
                    (TRACES, LANES),
                    (TRACES, LANES),
                    (BLOCK + 2 * FACE_PAD, LANES),
                    (BLOCK, LANES),
                )
            ],
            flops=10**8,
        )
        span = span_exchanged(faces)
        pitch = pitch_exchanged([next_a, next_b])
        args = [base, partial, *near, flags, odd, even, table, links]
        if section == 0:
            partial, traces = call(
                later_kernel, "later", [STATE_OUT, TRACE_OUT], args, scratch=buffers, flops=10**9
            )
    (rows,) = call(
        last_kernel,
        "last",
        [(x.shape, F32)],
        args,
        scratch=buffers + buffers[:1],
        flops=10**9,
    )
    odd, even = pitch
    (near,) = call(
        final_near_kernel,
        "final_near",
        [(x.shape, F32)],
        [*span, even, inner, rows],
        scratch=[pltpu.VMEM((BLOCK + 2 * FACE_PAD, 2 * LANES), F32)] * 2,
        flops=10**8,
    )
    (out,) = call(
        final_kernel,
        "final",
        [(x.shape, F32)],
        [flags, odd, even, near],
        scratch=[
            pltpu.VMEM(x.shape, F32),
            pltpu.VMEM((BLOCK + 2 * FACE_PAD, LANES), F32),
            pltpu.VMEM((BLOCK, LANES), F32),
            pltpu.SemaphoreType.DMA((5,)),
        ],
        flops=10**8,
        out_spec=pl.BlockSpec(memory_space=pl.ANY),
    )
    return out.reshape(state.shape)


def solution(mesh):
    volume, lift, trace, link = operator_tables()
    high, low = split_table(volume)
    table = np.concatenate([exact_table(trace), high, low])
    reached = [
        v * PER_VAR + r for v in range(5) for r in (*range(MAIN), *range(TAIL, PER_VAR))
    ]
    inlet = np.zeros((5 * INLET_ROWS, HALO))
    inlet[:, :BLOCK] = lift[reached, 4 * BLOCK :]
    lift[reached, 4 * BLOCK :] = 0.0
    assert not lift[:, 4 * BLOCK :].any()
    links = np.concatenate([exact_table(t) for t in (link, lift, inlet)])
    in_specs = (
        P(None, None, None, None, "pitch", "span", None),
        P(None, None, None, "pitch", "span"),
        P(),
    )
    out_specs = P(None, None, None, None, "pitch", "span", None)
    return jax.shard_map(
        functools.partial(shards, jnp.asarray(table), jnp.asarray(links)),
        mesh=mesh,
        in_specs=in_specs,
        out_specs=out_specs,
        check_vma=False,
    )
```

```python
import functools

import jax
import jax.numpy as jnp
import ml_dtypes
import numpy as np
from jax import lax
from jax.experimental import pallas as pl
from jax.experimental.pallas import tpu as pltpu
from jax.sharding import PartitionSpec as P

MEAN_FLOW = (0.5, 0.3, 0.0)
WAVE_SPEED = (1.5, 1.3, 1.0)
ELEM_SIZE = (1.0, 0.8, 1.2)
END_WEIGHT = 0.1
TIME_STEP = 0.01
KEEP = (0.0, 0.75, 1.0 / 3.0)
GAIN = (1.0, 0.25, 2.0 / 3.0)

ORDER = (1, 4, 2, 3, 0)
MAIN = 24
TAIL = 5 * MAIN
PER_VAR = 128
ROWS = 5 * PER_VAR
INLET_ROWS = 32
TILES = ((0, 0, 2), (1, 2, 4), (4, 4, 5))
BLOCK = 128
SPAN_ROWS = 104
TRACES = 4 * BLOCK
HALO = 5 * BLOCK
WAKE_ROW = 125
FACE_PAD = 16
HIGH_AT = TRACES
LOW_AT = HIGH_AT + ROWS
LIFT_AT = TRACES
INLET_AT = LIFT_AT + ROWS
LANES = 128
VMEM_LIMIT = 24 * 1024 * 1024


def derivative_table():
    points = np.array([-1.0, -np.sqrt(3.0 / 7.0), 0.0, np.sqrt(3.0 / 7.0), 1.0])
    products = np.array(
        [np.prod([points[j] - points[k] for k in range(5) if k != j]) for j in range(5)]
    )
    matrix = np.zeros((5, 5))
    for i in range(5):
        for j in range(5):
            if i != j:
                matrix[i, j] = products[i] / (products[j] * (points[i] - points[j]))
        matrix[i, i] = sum((1.0 / (points[i] - points[k]) for k in range(5) if k != i))
    return matrix


def flux_matrix(direction):
    flux = MEAN_FLOW[direction] * np.eye(5)
    flux[0, 1 + direction] += 1.0
    flux[4, 1 + direction] += 1.0
    flux[1 + direction, 4] += 1.0
    return flux


def half_flux(direction, sign):
    return 0.5 * (flux_matrix(direction) + sign * WAVE_SPEED[direction] * np.eye(5))


def lift_factor(direction):
    return TIME_STEP * 2.0 / (ELEM_SIZE[direction] * END_WEIGHT)


def half_scales():
    return (lift_factor(1) / 10.0, lift_factor(1), lift_factor(2), lift_factor(2), lift_factor(0))


def var_start(v):
    return ORDER.index(v) * PER_VAR


def node_row(v, a, p, s):
    node = p * 5 + s
    return var_start(v) + (a * MAIN + node if node < MAIN else TAIL + a)


def operator_tables():
    deriv = derivative_table()
    volume = np.zeros((ROWS, ROWS))
    lift = np.zeros((ROWS, HALO))
    trace = np.zeros((TRACES, ROWS))
    fluxes = [flux_matrix(d) for d in range(3)]
    plus = [half_flux(d, 1.0) for d in range(3)]
    minus = [half_flux(d, -1.0) for d in range(3)]
    plus_sent, minus_sent = (plus[2][:4], minus[2][:4])
    back_plus = np.vstack([np.eye(4), [[0.0, 0.0, 0.0, 1.0]]])
    back_minus = np.vstack([np.eye(4), [[0.0, 0.0, 0.0, -1.0]]])
    assert np.allclose(back_plus @ plus_sent, plus[2])
    assert np.allclose(back_minus @ minus_sent, minus[2])
    for a in range(5):
        for p in range(5):
            for s in range(5):
                here = [node_row(v, a, p, s) for v in range(5)]
                place = (a, p, s)
                for d in range(3):
                    for j in range(5):
                        there = list(place)
                        there[d] = j
                        cols = [node_row(v, *there) for v in range(5)]
                        coeff = -TIME_STEP * (2.0 / ELEM_SIZE[d]) * deriv[place[d], j]
                        volume[np.ix_(here, cols)] += coeff * fluxes[d]
                for d in (1, 2):
                    if place[d] == 4:
                        volume[np.ix_(here, here)] += lift_factor(d) * minus[d]
                    if place[d] == 0:
                        volume[np.ix_(here, here)] -= lift_factor(d) * plus[d]
                if p == 0:
                    cols = [s * 25 + v * 5 + a for v in range(5)]
                    lift[np.ix_(here, cols)] += lift_factor(1) * plus[1]
                    for v in range(5):
                        trace[BLOCK + s * 25 + v * 5 + a, here[v]] = 1.0
                if p == 4:
                    cols = [BLOCK + s * 25 + v * 5 + a for v in range(5)]
                    lift[np.ix_(here, cols)] -= lift_factor(1) * minus[1]
                    for v in range(5):
                        trace[s * 25 + v * 5 + a, here[v]] = 1.0
                if s == 0:
                    cols = [2 * BLOCK + c * 25 + a * 5 + p for c in range(4)]
                    lift[np.ix_(here, cols)] += lift_factor(2) * back_plus
                    rows = [3 * BLOCK + c * 25 + a * 5 + p for c in range(4)]
                    trace[np.ix_(rows, here)] += minus_sent
                if s == 4:
                    cols = [3 * BLOCK + c * 25 + a * 5 + p for c in range(4)]
                    lift[np.ix_(here, cols)] -= lift_factor(2) * back_minus
                    rows = [2 * BLOCK + c * 25 + a * 5 + p for c in range(4)]
                    trace[np.ix_(rows, here)] += plus_sent
                if a == 0:
                    cols = [4 * BLOCK + v * 25 + p * 5 + s for v in range(5)]
                    lift[np.ix_(here, cols)] += lift_factor(0) * plus[0]
    lift = lift / np.repeat(half_scales(), BLOCK)
    return volume, lift, trace, trace @ lift


def exact_table(table):
    exact = table.astype(ml_dtypes.bfloat16)
    assert np.allclose(exact.astype(np.float64), table, rtol=1e-12, atol=1e-12)
    return exact


def split_table(table):
    high = table.astype(ml_dtypes.bfloat16)
    low = (table - high.astype(np.float64)).astype(ml_dtypes.bfloat16)
    return high, low


def split(values):
    high = values.astype(jnp.bfloat16)
    low = (values - high.astype(jnp.float32)).astype(jnp.bfloat16)
    return high, low


def dot(left, right):
    return jnp.dot(left, right, preferred_element_type=jnp.float32)


def product(table, high, low):
    return dot(table, high) + dot(table, low)


def with_rows(values, first, extra):
    rows = lax.broadcasted_iota(jnp.int32, values.shape, 0)
    for k, row in enumerate(extra):
        values = jnp.where(rows == first + k, row, values)
    return values


def emit_pitch_faces(traces, wake, pitch_odd, pitch_a, pitch_b, inner):
    upper, lower = traces[0:BLOCK], traces[BLOCK : 2 * BLOCK]
    up = with_rows(upper[:, LANES:], WAKE_ROW, wake)
    down = lower[:, :LANES]
    pitch_a[...] = jnp.where(pitch_odd, down, up)
    pitch_b[...] = jnp.where(pitch_odd, up, down)
    inner[0:BLOCK] = upper[:, :LANES]
    inner[BLOCK:] = lower[:, LANES:]


def emit_span_faces(traces, span_odd, span_a, span_b):
    above, below = traces[0:SPAN_ROWS], traces[BLOCK : BLOCK + SPAN_ROWS]
    span_a[...] = jnp.where(span_odd, below, above)
    span_b[...] = jnp.where(span_odd, above, below)


def parities():
    return lax.axis_index("pitch") % 2 == 1, lax.axis_index("span") % 2 == 1


def combine(table, values):
    return [
        sum(float(table[i, j]) * values[j] for j in range(5) if table[i, j] != 0.0)
        for i in range(table.shape[0])
    ]


def begin_span_kernel(x, span_a, span_b):
    flat = x.reshape(x.shape[0], LANES)
    _, span_odd = parities()
    rest = jnp.zeros((SPAN_ROWS - 96, LANES), jnp.float32)
    for e in range(2):
        lanes = slice(e * LANES, (e + 1) * LANES)
        sides = []
        for s, sign in ((4, 1.0), (0, -1.0)):
            faces = [flat[pl.ds(v * 250 + 2 * s + e, 25, stride=10), :] for v in range(5)]
            sides.append(combine(half_flux(2, sign)[:4], faces))
        span_a[96:SPAN_ROWS, lanes] = rest
        span_b[96:SPAN_ROWS, lanes] = rest
        for c in range(4):
            above, below = (sides[0][c], sides[1][c])
            span_a[c * 25 : c * 25 + 25, lanes] = jnp.where(span_odd, below, above)
            span_b[c * 25 : c * 25 + 25, lanes] = jnp.where(span_odd, above, below)


def begin_pitch_kernel(x, wake, pitch_a, pitch_b, inner):
    flat = x.reshape(x.shape[0], LANES)
    pitch_odd, _ = parities()
    planes = wake.reshape(50, 5)[...]
    rows = lax.broadcasted_iota(jnp.int32, (50, LANES), 0)
    cols = lax.broadcasted_iota(jnp.int32, (50, LANES), 1)
    spread = jnp.zeros((50, LANES), jnp.float32)
    for s in range(5):
        mine = (cols - s) == 5 * (rows // 2)
        spread = jnp.where(mine, planes[:, s : s + 1], spread)
    own = [
        jnp.sum(jnp.where(rows % 2 == k, spread, 0.0), axis=0, keepdims=True) for k in range(2)
    ]
    tail = jnp.zeros((8, LANES), jnp.float32)
    up_tail = with_rows(tail, WAKE_ROW - 120, own)
    pitch_a[120:BLOCK] = jnp.where(pitch_odd, tail, up_tail)
    pitch_b[120:BLOCK] = jnp.where(pitch_odd, up_tail, tail)
    inner[120:BLOCK] = tail
    inner[BLOCK + 120 :] = tail
    for s in range(5):
        at = slice(s * 25, s * 25 + 25)
        upper, lower = (
            [flat[pl.ds(p * 10 + 2 * s + e, 25, stride=50), :] for e in range(2)] for p in (4, 0)
        )
        pitch_a[at] = jnp.where(pitch_odd, lower[0], upper[1])
        pitch_b[at] = jnp.where(pitch_odd, upper[1], lower[0])
        inner[at] = upper[0]
        inner[BLOCK + s * 25 : BLOCK + s * 25 + 25] = lower[1]


def load_state(x, state):
    flat = x.reshape(x.shape[0], LANES)
    for e in range(2):
        lanes = slice(e * LANES, (e + 1) * LANES)
        for v in range(5):
            base = var_start(v)
            first = v * 250 + e
            for a in range(5):
                at = base + a * MAIN
                state[at : at + MAIN, lanes] = flat[pl.ds(first + a * 50, MAIN, stride=2), :]
            tail = base + TAIL
            state[tail : tail + 8, lanes] = jnp.zeros((8, LANES), jnp.float32)
            state[tail : tail + 5, lanes] = flat[pl.ds(first + 2 * MAIN, 5, stride=50), :]


def add_axial_terms(gain, state, partial):
    lanes = lax.broadcasted_iota(jnp.int32, (MAIN + 8, LANES), 1)
    rows = lax.broadcasted_iota(jnp.int32, (8, LANES), 0)
    for e in range(2):
        own = slice(e * LANES, (e + 1) * LANES)
        upper_gap, lower_gap = ([], [])
        for v in range(5):
            base = var_start(v)
            lower = state[base : base + MAIN, own]
            upper = state[base + 4 * MAIN : base + TAIL, own]
            tail = state[base + TAIL : base + PER_VAR, own]
            turned = pltpu.roll(tail, 4, 0)
            join = lambda main, end: jnp.concatenate([main, end], axis=0)
            after = pltpu.roll(join(lower, turned), LANES - 1, 1)
            before = pltpu.roll(join(upper, turned), 1, 1)
            upper = join(upper, tail)
            upper_gap.append(jnp.where(lanes == LANES - 1, 0.0, upper - after))
            lower_gap.append(jnp.where(lanes == 0, 0.0, before) - join(lower, tail))
        mixed = []
        for gap, sign in ((upper_gap, -1.0), (lower_gap, 1.0)):
            mixed.append(combine(gain * lift_factor(0) * half_flux(0, sign), gap))
        for v in range(5):
            base = var_start(v)
            upper, lower = (mixed[0][v], mixed[1][v])
            partial[base : base + MAIN, own] += lower[:MAIN]
            partial[base + 4 * MAIN : base + TAIL, own] += upper[:MAIN]
            ends = jnp.where(rows == 0, lower[MAIN:], jnp.where(rows == 4, upper[MAIN:], 0.0))
            partial[base + TAIL : base + PER_VAR, own] += ends


def volume_rate(table, high, low):
    rate = [None] * 5
    for first, start, stop in TILES:
        part = slice(start * PER_VAR, stop * PER_VAR)
        table_high, table_low = (
            table[at + first * PER_VAR : at + ROWS, part] for at in (HIGH_AT, LOW_AT)
        )
        term = product(table_high, high[part], low[part]) + dot(table_low, high[part])
        for v in range(first, 5):
            block = term[(v - first) * PER_VAR : (v - first + 1) * PER_VAR]
            rate[v] = block if rate[v] is None else rate[v] + block
    return jnp.concatenate(rate, axis=0)


def phase(run):
    pl.when(lax.axis_index("span") >= 0)(run)


def advance_body(section, base, state, table, partial, faces):
    gain, keep = GAIN[section], KEEP[section]

    @phase
    def _():
        rate = volume_rate(table, *split(state[...]))
        if keep == 0.0:
            partial[...] = state[...] + rate
        else:
            partial[...] = keep * base[...] + gain * (state[...] + rate)

    @phase
    def _():
        add_axial_terms(gain, state, partial)

    if faces is not None:
        faces[...] = product(table[0:TRACES], *split(partial[...]))


def add_halo(section, before, near, far, links, state, far_high, far_low):
    gain = GAIN[section]
    gather_far(section, *far, far_high, far_low)
    side = pl.multiple_of(lax.axis_index("pitch") % 2 * BLOCK, BLOCK)
    rows = slice(LIFT_AT, LIFT_AT + ROWS)
    near_high, near_low = near
    state[...] = before[...] + gain * (
        product(links[rows, : 4 * BLOCK], near_high[...], near_low[...])
        + product(links[rows, pl.ds(side, BLOCK)], far_high[0:BLOCK], far_low[0:BLOCK])
    )
    added = gain * product(
        links[INLET_AT : INLET_AT + 5 * INLET_ROWS, 0:BLOCK], far_high[BLOCK:], far_low[BLOCK:]
    )
    for k in range(5):
        start, at = (k * PER_VAR, k * INLET_ROWS)
        state[start : start + MAIN] += added[at : at + MAIN]
        state[start + TAIL : start + PER_VAR] += added[at + MAIN : at + INLET_ROWS]


def first_kernel(offsets, x, table, base, partial, faces, flags):
    cols = lax.broadcasted_iota(jnp.int32, flags.shape, 1)
    moved = jnp.zeros(flags.shape, jnp.float32)
    for k in range(3):
        moved = jnp.where((cols == k) & (offsets[k] % 2 == 1), 1.0, moved)
    flags[...] = moved
    load_state(x, base)
    advance_body(0, None, base, table, partial, faces)


def later_kernel(
    base, before, near_high, near_low, flags, pitch_b, pitch_a, table, links, partial, faces,
    state, far_high, far_low,
):
    near, far = ((near_high, near_low), (flags, pitch_a, pitch_b))
    add_halo(0, before, near, far, links, state, far_high, far_low)
    advance_body(1, base, state, table, partial, faces)


def put_halo(halo_high, halo_low, block, first, scale, values):
    at = (slice(block * BLOCK, (block + 1) * BLOCK), slice(first, first + values.shape[1]))
    halo_high[at], halo_low[at] = split(scale * values)


def gather_near(pitch_a, span_a, span_b, inner, halo_high, halo_low):
    put = functools.partial(put_halo, halo_high, halo_low)
    scales = half_scales()
    pitch_odd, span_odd = parities()
    near = pitch_a[...]
    put(0, 0, scales[0], jnp.where(pitch_odd, near, 0.0))
    put(0, LANES, scales[0], inner[0:BLOCK])
    put(1, 0, scales[1], inner[BLOCK:])
    put(1, LANES, scales[1], jnp.where(pitch_odd, 0.0, near))
    above = jnp.where(span_odd, span_b[...], span_a[...])
    below = jnp.where(span_odd, span_a[...], span_b[...])
    place = lax.axis_index("span")
    above = jnp.where(place == lax.axis_size("span") - 1, 0.0, above)
    below = jnp.where(place == 0, 0.0, below)
    rest = jnp.zeros((BLOCK - SPAN_ROWS, 2 * LANES), jnp.float32)
    put(2, 0, scales[2], jnp.concatenate([below, rest], axis=0))
    put(3, 0, scales[3], jnp.concatenate([above, rest], axis=0))


def arrived_wake(pitch_a, pitch_b):
    pitch_odd, _ = parities()
    rows = slice(WAKE_ROW, WAKE_ROW + 2)
    return jnp.where(pitch_odd, pitch_a[rows], pitch_b[rows])


def inlet_row(section, flags, wake, e):
    moved = flags[0:1, section : section + 1] > 0.5
    return jnp.where(moved, wake[1 - e : 2 - e], wake[e : e + 1])


def gather_far(section, flags, pitch_a, pitch_b, halo_high, halo_low):
    put = functools.partial(put_halo, halo_high, halo_low)
    scales = half_scales()
    pitch_odd, _ = parities()
    far = jnp.where(pitch_odd, scales[1], scales[0]) * pitch_b[...]
    put(0, 0, 1.0, jnp.where(pitch_odd, 0.0, far))
    put(0, LANES, 1.0, jnp.where(pitch_odd, far, 0.0))
    wake = arrived_wake(pitch_a, pitch_b)
    rows = lax.broadcasted_iota(jnp.int32, (BLOCK, LANES), 0)
    cols = lax.broadcasted_iota(jnp.int32, (BLOCK, LANES), 1)
    for e in range(2):
        row = inlet_row(section, flags, wake, e)
        column = jnp.sum(jnp.where(rows == cols, row, 0.0), axis=1, keepdims=True)
        put(1, e * LANES, scales[4], jnp.where(cols == 0, column, 0.0))


def near_kernel(
    section, span_a, span_b, pitch_a, inner, faces, links, near_faces, halo_high, halo_low
):
    gather_near(pitch_a, span_a, span_b, inner, halo_high, halo_low)
    for half in range(2):
        at = slice(half * 2 * BLOCK, (half + 1) * 2 * BLOCK)
        near_faces[at] = faces[at] + GAIN[section] * dot(
            links[at, : 4 * BLOCK], halo_high[...]
        )


def far_lift(gain, pitch_b, faces):
    pitch_odd, _ = parities()
    faces[FACE_PAD : FACE_PAD + BLOCK] = pitch_b[...]
    plus, minus = (half_flux(1, 1.0), half_flux(1, -1.0))
    scale = gain * lift_factor(1)
    assert np.allclose(plus - np.diag(np.diag(plus)), minus - np.diag(np.diag(minus)))
    factor = lambda i, j: jnp.where(
        pitch_odd, -scale * float(minus[i, j]), scale * float(plus[i, j])
    )
    rows = lax.broadcasted_iota(jnp.int32, (BLOCK, LANES), 0)
    place = rows - 25 * sum((rows >= 25 * s).astype(jnp.int32) for s in range(1, 5))
    total = factor(0, 0) * pitch_b[...]
    for i in range(5):
        for j in range(5):
            if i != j and plus[i, j] != 0.0:
                at = FACE_PAD + 5 * (j - i)
                here = (place >= 5 * i) & (place < 5 * i + 5)
                total = total + jnp.where(here, factor(i, j) * faces[at : at + BLOCK], 0.0)
    return jnp.where(rows < WAKE_ROW, total, 0.0)


def far_kernel(
    section, flags, pitch_b, pitch_a, near_faces,
    next_pitch_a, next_pitch_b, next_inner, next_span_a, next_span_b, *refs
):
    *buffers, faces, lifted = refs
    traces, inlets = (buffers[:2], buffers[2:])
    pitch_odd, span_odd = parities()
    gain = GAIN[section]
    for e in range(2):
        traces[e][...] = near_faces[:, e * LANES : (e + 1) * LANES]
        inlets[e][...] = jnp.zeros((TRACES, LANES), jnp.float32)

    def add(start, count, stride, e, values):
        at = pl.ds(start, count, stride=stride) if stride > 1 else pl.ds(start, count)
        traces[e][at, :] = traces[e][at, :] + values

    total = far_lift(gain, pitch_b, faces)
    lifted[...] = total
    add(0, BLOCK, 1, 1, jnp.where(pitch_odd, total, 0.0))
    add(BLOCK, BLOCK, 1, 0, jnp.where(pitch_odd, 0.0, total))
    for block, s, sign in ((2, 4, 1.0), (3, 0, -1.0)):
        edge = [lifted[s * 25 + 5 * v : s * 25 + 5 * v + 5] for v in range(5)]
        for c, values in enumerate(combine(half_flux(2, sign)[:4], edge)):
            start = block * BLOCK + c * 25
            add(start + 4, 5, 5, 1, jnp.where(pitch_odd, values, 0.0))
            add(start, 5, 5, 0, jnp.where(pitch_odd, 0.0, values))

    wake = arrived_wake(pitch_a, pitch_b)
    rows = lax.broadcasted_iota(jnp.int32, (25, LANES), 0)
    cols = lax.broadcasted_iota(jnp.int32, (25, LANES), 1)
    node = sum((rows >= 5 * k).astype(jnp.int32) for k in range(1, 5))
    variable = rows - 5 * node
    scale = gain * lift_factor(0)
    inflow = half_flux(0, 1.0)

    def weights(table, choice, lane):
        total = jnp.zeros(choice.shape, jnp.float32)
        for v in range(5):
            values = [float(scale * table[i, v]) for i in range(table.shape[0])]
            if any(values):
                factor = sum(
                    jnp.where(choice == i, value, 0.0) for i, value in enumerate(values) if value
                )
                total = total + jnp.where(cols[: choice.shape[0]] == 25 * v + lane, factor, 0.0)
        return total

    def column(part, row):
        total = jnp.sum(part * row, axis=1, keepdims=True)
        return jnp.where(cols[: part.shape[0]] == 0, total, 0.0)

    pitch_parts = [
        (block, weights(inflow, variable, 5 * p + node)) for block, p in ((0, 4), (1, 0))
    ]
    span_parts = []
    for block, s, sign in ((2, 4, 1.0), (3, 0, -1.0)):
        sent = half_flux(2, sign)[:4] @ inflow
        for c in range(4):
            part = weights(sent[c : c + 1], rows[:5] * 0, 5 * rows[:5] + s)
            span_parts.append((block * BLOCK + c * 25, part))
    for e in range(2):
        row = inlet_row(section, flags, wake, e)
        for block, part in pitch_parts:
            inlets[e][pl.ds(block * BLOCK, 25, stride=5), :] = column(part, row)
        for start, part in span_parts:
            inlets[e][start : start + 5] = column(part, row)

    both = jnp.concatenate([traces[e][...] + inlets[e][...] for e in range(2)], axis=1)
    emit_span_faces(both[2 * BLOCK :], span_odd, next_span_a, next_span_b)
    emit_pitch_faces(
        both[: 2 * BLOCK], [wake[0:1], wake[1:2]], pitch_odd, next_pitch_a, next_pitch_b,
        next_inner,
    )


def last_kernel(
    base, before, near_high, near_low, flags, pitch_b, pitch_a, table, links, rows,
    state, far_high, far_low, partial,
):
    near, far = ((near_high, near_low), (flags, pitch_a, pitch_b))
    add_halo(1, before, near, far, links, state, far_high, far_low)
    advance_body(2, base, state, table, partial, None)
    flat = rows.reshape(rows.shape[0], LANES)
    for e in range(2):
        lanes = slice(e * LANES, (e + 1) * LANES)
        for v in range(5):
            start = var_start(v)
            first = v * 250 + e
            for a in range(5):
                at = start + a * MAIN
                flat[pl.ds(first + a * 50, MAIN, stride=2), :] = partial[at : at + MAIN, lanes]
            tail = start + TAIL
            flat[pl.ds(first + 2 * MAIN, 5, stride=50), :] = partial[tail : tail + 5, lanes]


def mixed_faces(faces, s, lanes, direction, sign):
    table = half_flux(direction, sign)
    at = FACE_PAD + s * 25
    rows = lax.broadcasted_iota(jnp.int32, (25, LANES), 0)
    own = faces[at : at + 25, lanes]
    total = float(table[0, 0]) * own
    for i in range(5):
        for j in range(5):
            if i != j and table[i, j] != 0.0:
                moved = faces[at + 5 * (j - i) : at + 5 * (j - i) + 25, lanes]
                here = (rows >= 5 * i) & (rows < 5 * i + 5)
                total = total + jnp.where(here, float(table[i, j]) * moved, 0.0)
    return total


def final_near_kernel(
    span_a, span_b, pitch_a, inner, before, result, after_faces, before_faces
):
    flat = result.reshape(result.shape[0], LANES)
    flat[...] = before.reshape(before.shape[0], LANES)[...]
    pitch_odd, span_odd = parities()
    gain = GAIN[2]

    def add(start, stride, values):
        at = pl.ds(start, values.shape[0], stride=stride)
        flat[at, :] = flat[at, :] + values

    place = lax.axis_index("span")
    scale = gain * lift_factor(2)
    up_scale = jnp.where(place == lax.axis_size("span") - 1, 0.0, -scale)
    down_scale = jnp.where(place == 0, 0.0, scale)
    for e in range(2):
        lanes = slice(e * LANES, (e + 1) * LANES)
        for c in range(4):
            at = slice(c * 25, c * 25 + 25)
            first, second = (span_a[at, lanes], span_b[at, lanes])
            above = up_scale * jnp.where(span_odd, second, first)
            below = down_scale * jnp.where(span_odd, first, second)
            add(c * 250 + 8 + e, 10, above)
            add(c * 250 + e, 10, below)
            if c == 3:
                add(4 * 250 + 8 + e, 10, -above)
                add(4 * 250 + e, 10, below)

    at = slice(FACE_PAD, FACE_PAD + BLOCK)
    near = pitch_a[...]
    before_faces[at, :LANES] = jnp.where(pitch_odd, near, 0.0)
    before_faces[at, LANES:] = inner[0:BLOCK]
    after_faces[at, :LANES] = inner[BLOCK:]
    after_faces[at, LANES:] = jnp.where(pitch_odd, 0.0, near)
    scale = gain * lift_factor(1)
    for e in range(2):
        lanes = slice(e * LANES, (e + 1) * LANES)
        for s in range(5):
            add(40 + 2 * s + e, 50, -scale * mixed_faces(after_faces, s, lanes, 1, -1.0))
            add(2 * s + e, 50, scale * mixed_faces(before_faces, s, lanes, 1, 1.0))


def final_kernel(flags, pitch_b, pitch_a, near, out, result, faces, lifted, done):
    flat = result.reshape(result.shape[0], LANES)
    flat[...] = near.reshape(near.shape[0], LANES)[...]
    pitch_odd, _ = parities()
    gain = GAIN[2]

    def add(start, stride, values):
        at = pl.ds(start, values.shape[0], stride=stride)
        flat[at, :] = flat[at, :] + values

    lifted[...] = far_lift(gain, pitch_b, faces)
    for s in range(5):
        values = lifted[s * 25 : s * 25 + 25]
        add(40 + 2 * s + 1, 50, jnp.where(pitch_odd, values, 0.0))
        add(2 * s, 50, jnp.where(pitch_odd, 0.0, values))

    wake = arrived_wake(pitch_a, pitch_b)
    rows = lax.broadcasted_iota(jnp.int32, (25, LANES), 0)
    cols = lax.broadcasted_iota(jnp.int32, (25, LANES), 1)
    for e in range(2):
        row = inlet_row(2, flags, wake, e)
        columns = [
            jnp.sum(jnp.where(cols == rows + 25 * v, row, 0.0), axis=1, keepdims=True)
            for v in range(5)
        ]
        inlet = combine(gain * lift_factor(0) * half_flux(0, 1.0), columns)
        for v in range(5):
            add(v * 250 + e, 2, jnp.where(cols == 0, inlet[v], 0.0))

    copies = []
    for v in range(5):
        part = pl.ds(v * 250, 250)
        copies.append(pltpu.make_async_copy(result.at[part], out.at[part], done.at[v]))
        copies[-1].start()
    for copy in copies:
        copy.wait()


IN_VMEM = pl.BlockSpec(memory_space=pltpu.VMEM)
IN_SMEM = pl.BlockSpec(memory_space=pltpu.SMEM)


def call(kernel, name, outs, args, in_specs=(), scratch=(), flops=0, out_spec=IN_VMEM):
    in_specs = list(in_specs)
    return pl.pallas_call(
        kernel,
        name=name,
        out_shape=[jax.ShapeDtypeStruct(shape, dtype) for shape, dtype in outs],
        in_specs=in_specs + [IN_VMEM] * (len(args) - len(in_specs)),
        out_specs=[out_spec] * len(outs),
        scratch_shapes=list(scratch),
        compiler_params=pltpu.CompilerParams(vmem_limit_bytes=VMEM_LIMIT),
        cost_estimate=pl.CostEstimate(flops=flops, bytes_accessed=2**20, transcendentals=0),
    )(*args)


def swapped(value, axis, odd):
    pitch, span = (lax.axis_size("pitch"), lax.axis_size("span"))
    pairs = []
    for i in range(pitch):
        for j in range(span):
            if axis == "pitch":
                other = ((i + (1 if i % 2 == odd else -1)) % pitch, j)
            else:
                other = (i, j + (1 if j % 2 == odd else -1))
                if not 0 <= other[1] < span:
                    other = (i ^ 1, j)
            pairs.append((i * span + j, other[0] * span + other[1]))
    return lax.ppermute(value, ("pitch", "span"), pairs)


def span_exchanged(faces):
    return swapped(faces[0], "span", 0), swapped(faces[1], "span", 1)


def pitch_exchanged(faces):
    return swapped(faces[1], "pitch", 1), swapped(faces[0], "pitch", 0)


F32 = jnp.float32
PITCH_OUTS = [((BLOCK, LANES), F32), ((BLOCK, LANES), F32), ((2 * BLOCK, LANES), F32)]
SPAN_OUTS = [((SPAN_ROWS, 2 * LANES), F32)] * 2
SMALL_OUT = ((8, LANES), F32)
NEAR_OUTS = [((4 * BLOCK, 2 * LANES), jnp.bfloat16)] * 2
FAR_OUTS = [((2 * BLOCK, 2 * LANES), jnp.bfloat16)] * 2
STATE_OUT = ((ROWS, 2 * LANES), F32)
TRACE_OUT = ((TRACES, 2 * LANES), F32)


def shards(table, links, state, wake_planes, bar_offsets):
    x = state.reshape(-1, 1, LANES)
    wake = wake_planes.transpose(0, 1, 3, 4, 2).reshape(50, 1, 5)
    faces = call(begin_span_kernel, "begin_span", SPAN_OUTS, [x], flops=10**10)
    span = span_exchanged(faces)
    *faces, inner = call(begin_pitch_kernel, "begin_pitch", PITCH_OUTS, [x, wake], flops=10**10)
    pitch = pitch_exchanged(faces)
    base, partial, traces, flags = call(
        first_kernel,
        "first",
        [STATE_OUT, STATE_OUT, TRACE_OUT, SMALL_OUT],
        [bar_offsets, x, table],
        in_specs=[IN_SMEM],
        flops=10**9,
    )
    buffers = [pltpu.VMEM(shape, dtype) for shape, dtype in [STATE_OUT] + FAR_OUTS]
    for section in range(2):
        odd, even = pitch
        near_faces, *near = call(
            functools.partial(near_kernel, section),
            "near",
            [TRACE_OUT] + NEAR_OUTS,
            [*span, even, inner, traces, links],
            flops=10**8,
        )
        next_a, next_b, inner, *faces = call(
            functools.partial(far_kernel, section),
            "far",
            PITCH_OUTS + SPAN_OUTS,
            [flags, odd, even, near_faces],
            scratch=[
                pltpu.VMEM(shape, F32)
                for shape in (
                    *[(TRACES, LANES)] * 4,
                    (BLOCK + 2 * FACE_PAD, LANES),
                    (BLOCK, LANES),
                )
            ],
            flops=10**8,
        )
        span = span_exchanged(faces)
        pitch = pitch_exchanged([next_a, next_b])
        args = [base, partial, *near, flags, odd, even, table, links]
        if section == 0:
            partial, traces = call(
                later_kernel, "later", [STATE_OUT, TRACE_OUT], args, scratch=buffers, flops=10**9
            )
    (rows,) = call(
        last_kernel,
        "last",
        [(x.shape, F32)],
        args,
        scratch=buffers + buffers[:1],
        flops=10**9,
    )
    odd, even = pitch
    (near,) = call(
        final_near_kernel,
        "final_near",
        [(x.shape, F32)],
        [*span, even, inner, rows],
        scratch=[pltpu.VMEM((BLOCK + 2 * FACE_PAD, 2 * LANES), F32)] * 2,
        flops=10**8,
    )
    (out,) = call(
        final_kernel,
        "final",
        [(x.shape, F32)],
        [flags, odd, even, near],
        scratch=[
            pltpu.VMEM(x.shape, F32),
            pltpu.VMEM((BLOCK + 2 * FACE_PAD, LANES), F32),
            pltpu.VMEM((BLOCK, LANES), F32),
            pltpu.SemaphoreType.DMA((5,)),
        ],
        flops=10**8,
        out_spec=pl.BlockSpec(memory_space=pl.ANY),
    )
    return out.reshape(state.shape)


def solution(mesh):
    volume, lift, trace, link = operator_tables()
    high, low = split_table(volume)
    table = np.concatenate([exact_table(trace), high, low])
    reached = [
        v * PER_VAR + r for v in range(5) for r in (*range(MAIN), *range(TAIL, PER_VAR))
    ]
    inlet = np.zeros((5 * INLET_ROWS, HALO))
    inlet[:, :BLOCK] = lift[reached, 4 * BLOCK :]
    lift[reached, 4 * BLOCK :] = 0.0
    assert not lift[:, 4 * BLOCK :].any()
    links = np.concatenate([exact_table(t) for t in (link, lift, inlet)])
    in_specs = (
        P(None, None, None, None, "pitch", "span", None),
        P(None, None, None, "pitch", "span"),
        P(),
    )
    out_specs = P(None, None, None, None, "pitch", "span", None)
    return jax.shard_map(
        functools.partial(shards, jnp.asarray(table), jnp.asarray(links)),
        mesh=mesh,
        in_specs=in_specs,
        out_specs=out_specs,
        check_vma=False,
    )
```

```python
import functools

import jax
import jax.numpy as jnp
import ml_dtypes
import numpy as np
from jax import lax
from jax.experimental import pallas as pl
from jax.experimental.pallas import tpu as pltpu
from jax.sharding import PartitionSpec as P

MEAN_FLOW = (0.5, 0.3, 0.0)
WAVE_SPEED = (1.5, 1.3, 1.0)
ELEM_SIZE = (1.0, 0.8, 1.2)
END_WEIGHT = 0.1
TIME_STEP = 0.01
KEEP = (0.0, 0.75, 1.0 / 3.0)
GAIN = (1.0, 0.25, 2.0 / 3.0)

ORDER = (1, 4, 2, 3, 0)
MAIN = 24
TAIL = 5 * MAIN
PER_VAR = 128
ROWS = 5 * PER_VAR
INLET_ROWS = 32
TILES = ((0, 0, 2), (1, 2, 4), (4, 4, 5))
BLOCK = 128
SPAN_ROWS = 104
TRACES = 4 * BLOCK
HALO = 5 * BLOCK
WAKE_ROW = 125
FACE_PAD = 16
HIGH_AT = TRACES
LOW_AT = HIGH_AT + ROWS
LIFT_AT = TRACES
INLET_AT = LIFT_AT + ROWS
LANES = 128
VMEM_LIMIT = 24 * 1024 * 1024


def derivative_table():
    points = np.array([-1.0, -np.sqrt(3.0 / 7.0), 0.0, np.sqrt(3.0 / 7.0), 1.0])
    products = np.array(
        [np.prod([points[j] - points[k] for k in range(5) if k != j]) for j in range(5)]
    )
    matrix = np.zeros((5, 5))
    for i in range(5):
        for j in range(5):
            if i != j:
                matrix[i, j] = products[i] / (products[j] * (points[i] - points[j]))
        matrix[i, i] = sum((1.0 / (points[i] - points[k]) for k in range(5) if k != i))
    return matrix


def flux_matrix(direction):
    flux = MEAN_FLOW[direction] * np.eye(5)
    flux[0, 1 + direction] += 1.0
    flux[4, 1 + direction] += 1.0
    flux[1 + direction, 4] += 1.0
    return flux


def half_flux(direction, sign):
    return 0.5 * (flux_matrix(direction) + sign * WAVE_SPEED[direction] * np.eye(5))


def lift_factor(direction):
    return TIME_STEP * 2.0 / (ELEM_SIZE[direction] * END_WEIGHT)


def half_scales():
    return (lift_factor(1) / 10.0, lift_factor(1), lift_factor(2), lift_factor(2), lift_factor(0))


def var_start(v):
    return ORDER.index(v) * PER_VAR


def node_row(v, a, p, s):
    node = p * 5 + s
    return var_start(v) + (a * MAIN + node if node < MAIN else TAIL + a)


def operator_tables():
    deriv = derivative_table()
    volume = np.zeros((ROWS, ROWS))
    lift = np.zeros((ROWS, HALO))
    trace = np.zeros((TRACES, ROWS))
    fluxes = [flux_matrix(d) for d in range(3)]
    plus = [half_flux(d, 1.0) for d in range(3)]
    minus = [half_flux(d, -1.0) for d in range(3)]
    plus_sent, minus_sent = (plus[2][:4], minus[2][:4])
    back_plus = np.vstack([np.eye(4), [[0.0, 0.0, 0.0, 1.0]]])
    back_minus = np.vstack([np.eye(4), [[0.0, 0.0, 0.0, -1.0]]])
    assert np.allclose(back_plus @ plus_sent, plus[2])
    assert np.allclose(back_minus @ minus_sent, minus[2])
    for a in range(5):
        for p in range(5):
            for s in range(5):
                here = [node_row(v, a, p, s) for v in range(5)]
                place = (a, p, s)
                for d in range(3):
                    for j in range(5):
                        there = list(place)
                        there[d] = j
                        cols = [node_row(v, *there) for v in range(5)]
                        coeff = -TIME_STEP * (2.0 / ELEM_SIZE[d]) * deriv[place[d], j]
                        volume[np.ix_(here, cols)] += coeff * fluxes[d]
                for d in (1, 2):
                    if place[d] == 4:
                        volume[np.ix_(here, here)] += lift_factor(d) * minus[d]
                    if place[d] == 0:
                        volume[np.ix_(here, here)] -= lift_factor(d) * plus[d]
                if p == 0:
                    cols = [s * 25 + v * 5 + a for v in range(5)]
                    lift[np.ix_(here, cols)] += lift_factor(1) * plus[1]
                    for v in range(5):
                        trace[BLOCK + s * 25 + v * 5 + a, here[v]] = 1.0
                if p == 4:
                    cols = [BLOCK + s * 25 + v * 5 + a for v in range(5)]
                    lift[np.ix_(here, cols)] -= lift_factor(1) * minus[1]
                    for v in range(5):
                        trace[s * 25 + v * 5 + a, here[v]] = 1.0
                if s == 0:
                    cols = [2 * BLOCK + c * 25 + a * 5 + p for c in range(4)]
                    lift[np.ix_(here, cols)] += lift_factor(2) * back_plus
                    rows = [3 * BLOCK + c * 25 + a * 5 + p for c in range(4)]
                    trace[np.ix_(rows, here)] += minus_sent
                if s == 4:
                    cols = [3 * BLOCK + c * 25 + a * 5 + p for c in range(4)]
                    lift[np.ix_(here, cols)] -= lift_factor(2) * back_minus
                    rows = [2 * BLOCK + c * 25 + a * 5 + p for c in range(4)]
                    trace[np.ix_(rows, here)] += plus_sent
                if a == 0:
                    cols = [4 * BLOCK + v * 25 + p * 5 + s for v in range(5)]
                    lift[np.ix_(here, cols)] += lift_factor(0) * plus[0]
    lift = lift / np.repeat(half_scales(), BLOCK)
    return volume, lift, trace, trace @ lift


def exact_table(table):
    exact = table.astype(ml_dtypes.bfloat16)
    assert np.allclose(exact.astype(np.float64), table, rtol=1e-12, atol=1e-12)
    return exact


def split_table(table):
    high = table.astype(ml_dtypes.bfloat16)
    low = (table - high.astype(np.float64)).astype(ml_dtypes.bfloat16)
    return high, low


def split(values):
    high = values.astype(jnp.bfloat16)
    low = (values - high.astype(jnp.float32)).astype(jnp.bfloat16)
    return high, low


def dot(left, right):
    return jnp.dot(left, right, preferred_element_type=jnp.float32)


def product(table, high, low):
    return dot(table, high) + dot(table, low)


def with_rows(values, first, extra):
    rows = lax.broadcasted_iota(jnp.int32, values.shape, 0)
    for k, row in enumerate(extra):
        values = jnp.where(rows == first + k, row, values)
    return values


def emit_pitch_faces(traces, wake, pitch_odd, pitch_a, pitch_b, inner):
    upper, lower = traces[0:BLOCK], traces[BLOCK : 2 * BLOCK]
    up = with_rows(upper[:, LANES:], WAKE_ROW, wake)
    down = lower[:, :LANES]
    pitch_a[...] = jnp.where(pitch_odd, down, up)
    pitch_b[...] = jnp.where(pitch_odd, up, down)
    inner[0:BLOCK] = upper[:, :LANES]
    inner[BLOCK:] = lower[:, LANES:]


def emit_span_faces(traces, span_odd, span_a, span_b):
    above, below = traces[0:SPAN_ROWS], traces[BLOCK : BLOCK + SPAN_ROWS]
    span_a[...] = jnp.where(span_odd, below, above)
    span_b[...] = jnp.where(span_odd, above, below)


def parities():
    return lax.axis_index("pitch") % 2 == 1, lax.axis_index("span") % 2 == 1


def combine(table, values):
    return [
        sum(float(table[i, j]) * values[j] for j in range(5) if table[i, j] != 0.0)
        for i in range(table.shape[0])
    ]


def begin_span_kernel(x, span_a, span_b):
    flat = x.reshape(x.shape[0], LANES)
    _, span_odd = parities()
    rest = jnp.zeros((SPAN_ROWS - 96, LANES), jnp.float32)
    for e in range(2):
        lanes = slice(e * LANES, (e + 1) * LANES)
        sides = []
        for s, sign in ((4, 1.0), (0, -1.0)):
            faces = [flat[pl.ds(v * 250 + 2 * s + e, 25, stride=10), :] for v in range(5)]
            sides.append(combine(half_flux(2, sign)[:4], faces))
        span_a[96:SPAN_ROWS, lanes] = rest
        span_b[96:SPAN_ROWS, lanes] = rest
        for c in range(4):
            above, below = (sides[0][c], sides[1][c])
            span_a[c * 25 : c * 25 + 25, lanes] = jnp.where(span_odd, below, above)
            span_b[c * 25 : c * 25 + 25, lanes] = jnp.where(span_odd, above, below)


def begin_pitch_kernel(x, wake, pitch_a, pitch_b, inner):
    flat = x.reshape(x.shape[0], LANES)
    pitch_odd, _ = parities()
    planes = wake.reshape(50, 5)[...]
    rows = lax.broadcasted_iota(jnp.int32, (50, LANES), 0)
    cols = lax.broadcasted_iota(jnp.int32, (50, LANES), 1)
    spread = jnp.zeros((50, LANES), jnp.float32)
    for s in range(5):
        mine = (cols - s) == 5 * (rows // 2)
        spread = jnp.where(mine, planes[:, s : s + 1], spread)
    own = [
        jnp.sum(jnp.where(rows % 2 == k, spread, 0.0), axis=0, keepdims=True) for k in range(2)
    ]
    tail = jnp.zeros((8, LANES), jnp.float32)
    up_tail = with_rows(tail, WAKE_ROW - 120, own)
    pitch_a[120:BLOCK] = jnp.where(pitch_odd, tail, up_tail)
    pitch_b[120:BLOCK] = jnp.where(pitch_odd, up_tail, tail)
    inner[120:BLOCK] = tail
    inner[BLOCK + 120 :] = tail
    for s in range(5):
        at = slice(s * 25, s * 25 + 25)
        upper, lower = (
            [flat[pl.ds(p * 10 + 2 * s + e, 25, stride=50), :] for e in range(2)] for p in (4, 0)
        )
        pitch_a[at] = jnp.where(pitch_odd, lower[0], upper[1])
        pitch_b[at] = jnp.where(pitch_odd, upper[1], lower[0])
        inner[at] = upper[0]
        inner[BLOCK + s * 25 : BLOCK + s * 25 + 25] = lower[1]


def load_state(x, state):
    flat = x.reshape(x.shape[0], LANES)
    for e in range(2):
        lanes = slice(e * LANES, (e + 1) * LANES)
        for v in range(5):
            base = var_start(v)
            first = v * 250 + e
            for a in range(5):
                at = base + a * MAIN
                state[at : at + MAIN, lanes] = flat[pl.ds(first + a * 50, MAIN, stride=2), :]
            tail = base + TAIL
            state[tail : tail + 8, lanes] = jnp.zeros((8, LANES), jnp.float32)
            state[tail : tail + 5, lanes] = flat[pl.ds(first + 2 * MAIN, 5, stride=50), :]


def add_axial_terms(gain, state, partial):
    lanes = lax.broadcasted_iota(jnp.int32, (MAIN + 8, LANES), 1)
    rows = lax.broadcasted_iota(jnp.int32, (8, LANES), 0)
    for e in range(2):
        own = slice(e * LANES, (e + 1) * LANES)
        upper_gap, lower_gap = ([], [])
        for v in range(5):
            base = var_start(v)
            lower = state[base : base + MAIN, own]
            upper = state[base + 4 * MAIN : base + TAIL, own]
            tail = state[base + TAIL : base + PER_VAR, own]
            turned = pltpu.roll(tail, 4, 0)
            join = lambda main, end: jnp.concatenate([main, end], axis=0)
            after = pltpu.roll(join(lower, turned), LANES - 1, 1)
            before = pltpu.roll(join(upper, turned), 1, 1)
            upper = join(upper, tail)
            upper_gap.append(jnp.where(lanes == LANES - 1, 0.0, upper - after))
            lower_gap.append(jnp.where(lanes == 0, 0.0, before) - join(lower, tail))
        mixed = []
        for gap, sign in ((upper_gap, -1.0), (lower_gap, 1.0)):
            mixed.append(combine(gain * lift_factor(0) * half_flux(0, sign), gap))
        for v in range(5):
            base = var_start(v)
            upper, lower = (mixed[0][v], mixed[1][v])
            partial[base : base + MAIN, own] += lower[:MAIN]
            partial[base + 4 * MAIN : base + TAIL, own] += upper[:MAIN]
            ends = jnp.where(rows == 0, lower[MAIN:], jnp.where(rows == 4, upper[MAIN:], 0.0))
            partial[base + TAIL : base + PER_VAR, own] += ends


def volume_rate(table, high, low):
    rate = [None] * 5
    for first, start, stop in TILES:
        part = slice(start * PER_VAR, stop * PER_VAR)
        table_high, table_low = (
            table[at + first * PER_VAR : at + ROWS, part] for at in (HIGH_AT, LOW_AT)
        )
        term = product(table_high, high[part], low[part]) + dot(table_low, high[part])
        for v in range(first, 5):
            block = term[(v - first) * PER_VAR : (v - first + 1) * PER_VAR]
            rate[v] = block if rate[v] is None else rate[v] + block
    return jnp.concatenate(rate, axis=0)


def phase(run):
    pl.when(lax.axis_index("span") >= 0)(run)


def advance_body(section, base, state, table, partial, faces):
    gain, keep = GAIN[section], KEEP[section]

    @phase
    def _():
        rate = volume_rate(table, *split(state[...]))
        if keep == 0.0:
            partial[...] = state[...] + rate
        else:
            partial[...] = keep * base[...] + gain * (state[...] + rate)

    @phase
    def _():
        add_axial_terms(gain, state, partial)

    if faces is not None:
        faces[...] = product(table[0:TRACES], *split(partial[...]))


def add_halo(section, before, near, far, links, state, far_high, far_low):
    gain = GAIN[section]
    gather_far(section, *far, far_high, far_low)
    side = pl.multiple_of(lax.axis_index("pitch") % 2 * BLOCK, BLOCK)
    rows = slice(LIFT_AT, LIFT_AT + ROWS)
    near_high, near_low = near
    state[...] = before[...] + gain * (
        product(links[rows, : 4 * BLOCK], near_high[...], near_low[...])
        + product(links[rows, pl.ds(side, BLOCK)], far_high[0:BLOCK], far_low[0:BLOCK])
    )
    added = gain * product(
        links[INLET_AT : INLET_AT + 5 * INLET_ROWS, 0:BLOCK], far_high[BLOCK:], far_low[BLOCK:]
    )
    for k in range(5):
        start, at = (k * PER_VAR, k * INLET_ROWS)
        state[start : start + MAIN] += added[at : at + MAIN]
        state[start + TAIL : start + PER_VAR] += added[at + MAIN : at + INLET_ROWS]


def first_kernel(offsets, x, table, base, partial, faces, flags):
    cols = lax.broadcasted_iota(jnp.int32, flags.shape, 1)
    moved = jnp.zeros(flags.shape, jnp.float32)
    for k in range(3):
        moved = jnp.where((cols == k) & (offsets[k] % 2 == 1), 1.0, moved)
    flags[...] = moved
    load_state(x, base)
    advance_body(0, None, base, table, partial, faces)


def later_kernel(
    base, before, near_high, near_low, flags, pitch_b, pitch_a, table, links, partial, faces,
    state, far_high, far_low,
):
    near, far = ((near_high, near_low), (flags, pitch_a, pitch_b))
    add_halo(0, before, near, far, links, state, far_high, far_low)
    advance_body(1, base, state, table, partial, faces)


def put_halo(halo_high, halo_low, block, first, scale, values):
    at = (slice(block * BLOCK, (block + 1) * BLOCK), slice(first, first + values.shape[1]))
    halo_high[at], halo_low[at] = split(scale * values)


def gather_near(pitch_a, span_a, span_b, inner, halo_high, halo_low):
    put = functools.partial(put_halo, halo_high, halo_low)
    scales = half_scales()
    pitch_odd, span_odd = parities()
    near = pitch_a[...]
    put(0, 0, scales[0], jnp.where(pitch_odd, near, 0.0))
    put(0, LANES, scales[0], inner[0:BLOCK])
    put(1, 0, scales[1], inner[BLOCK:])
    put(1, LANES, scales[1], jnp.where(pitch_odd, 0.0, near))
    above = jnp.where(span_odd, span_b[...], span_a[...])
    below = jnp.where(span_odd, span_a[...], span_b[...])
    place = lax.axis_index("span")
    above = jnp.where(place == lax.axis_size("span") - 1, 0.0, above)
    below = jnp.where(place == 0, 0.0, below)
    rest = jnp.zeros((BLOCK - SPAN_ROWS, 2 * LANES), jnp.float32)
    put(2, 0, scales[2], jnp.concatenate([below, rest], axis=0))
    put(3, 0, scales[3], jnp.concatenate([above, rest], axis=0))


def arrived_wake(pitch_a, pitch_b):
    pitch_odd, _ = parities()
    rows = slice(WAKE_ROW, WAKE_ROW + 2)
    return jnp.where(pitch_odd, pitch_a[rows], pitch_b[rows])


def inlet_row(section, flags, wake, e):
    moved = flags[0:1, section : section + 1] > 0.5
    return jnp.where(moved, wake[1 - e : 2 - e], wake[e : e + 1])


def gather_far(section, flags, pitch_a, pitch_b, halo_high, halo_low):
    put = functools.partial(put_halo, halo_high, halo_low)
    scales = half_scales()
    pitch_odd, _ = parities()
    far = jnp.where(pitch_odd, scales[1], scales[0]) * pitch_b[...]
    put(0, 0, 1.0, jnp.where(pitch_odd, 0.0, far))
    put(0, LANES, 1.0, jnp.where(pitch_odd, far, 0.0))
    wake = arrived_wake(pitch_a, pitch_b)
    rows = lax.broadcasted_iota(jnp.int32, (BLOCK, LANES), 0)
    cols = lax.broadcasted_iota(jnp.int32, (BLOCK, LANES), 1)
    for e in range(2):
        row = inlet_row(section, flags, wake, e)
        column = jnp.sum(jnp.where(rows == cols, row, 0.0), axis=1, keepdims=True)
        put(1, e * LANES, scales[4], jnp.where(cols == 0, column, 0.0))


def near_kernel(
    section, span_a, span_b, pitch_a, inner, faces, links, near_faces, halo_high, halo_low
):
    gather_near(pitch_a, span_a, span_b, inner, halo_high, halo_low)
    for half in range(2):
        at = slice(half * 2 * BLOCK, (half + 1) * 2 * BLOCK)
        near_faces[at] = faces[at] + GAIN[section] * dot(
            links[at, : 4 * BLOCK], halo_high[...]
        )


def far_lift(gain, pitch_b, faces):
    pitch_odd, _ = parities()
    faces[FACE_PAD : FACE_PAD + BLOCK] = pitch_b[...]
    plus, minus = (half_flux(1, 1.0), half_flux(1, -1.0))
    scale = gain * lift_factor(1)
    assert np.allclose(plus - np.diag(np.diag(plus)), minus - np.diag(np.diag(minus)))
    factor = lambda i, j: jnp.where(
        pitch_odd, -scale * float(minus[i, j]), scale * float(plus[i, j])
    )
    rows = lax.broadcasted_iota(jnp.int32, (BLOCK, LANES), 0)
    place = rows - 25 * sum((rows >= 25 * s).astype(jnp.int32) for s in range(1, 5))
    total = factor(0, 0) * pitch_b[...]
    for i in range(5):
        for j in range(5):
            if i != j and plus[i, j] != 0.0:
                at = FACE_PAD + 5 * (j - i)
                here = (place >= 5 * i) & (place < 5 * i + 5)
                total = total + jnp.where(here, factor(i, j) * faces[at : at + BLOCK], 0.0)
    return jnp.where(rows < WAKE_ROW, total, 0.0)


def far_kernel(
    section, flags, pitch_b, pitch_a, near_faces,
    next_pitch_a, next_pitch_b, next_inner, next_span_a, next_span_b, *refs
):
    *buffers, faces, lifted = refs
    traces, inlets = (buffers[:2], buffers[2:])
    pitch_odd, span_odd = parities()
    gain = GAIN[section]
    for e in range(2):
        traces[e][...] = near_faces[:, e * LANES : (e + 1) * LANES]
        inlets[e][...] = jnp.zeros((TRACES, LANES), jnp.float32)

    def add(start, count, stride, e, values):
        at = pl.ds(start, count, stride=stride) if stride > 1 else pl.ds(start, count)
        traces[e][at, :] = traces[e][at, :] + values

    total = far_lift(gain, pitch_b, faces)
    lifted[...] = total
    add(0, BLOCK, 1, 1, jnp.where(pitch_odd, total, 0.0))
    add(BLOCK, BLOCK, 1, 0, jnp.where(pitch_odd, 0.0, total))
    for block, s, sign in ((2, 4, 1.0), (3, 0, -1.0)):
        edge = [lifted[s * 25 + 5 * v : s * 25 + 5 * v + 5] for v in range(5)]
        for c, values in enumerate(combine(half_flux(2, sign)[:4], edge)):
            start = block * BLOCK + c * 25
            add(start + 4, 5, 5, 1, jnp.where(pitch_odd, values, 0.0))
            add(start, 5, 5, 0, jnp.where(pitch_odd, 0.0, values))

    wake = arrived_wake(pitch_a, pitch_b)
    rows = lax.broadcasted_iota(jnp.int32, (25, LANES), 0)
    cols = lax.broadcasted_iota(jnp.int32, (25, LANES), 1)
    node = sum((rows >= 5 * k).astype(jnp.int32) for k in range(1, 5))
    variable = rows - 5 * node
    scale = gain * lift_factor(0)
    inflow = half_flux(0, 1.0)

    def weights(table, choice, lane):
        total = jnp.zeros(choice.shape, jnp.float32)
        for v in range(5):
            values = [float(scale * table[i, v]) for i in range(table.shape[0])]
            if any(values):
                factor = sum(
                    jnp.where(choice == i, value, 0.0) for i, value in enumerate(values) if value
                )
                total = total + jnp.where(cols[: choice.shape[0]] == 25 * v + lane, factor, 0.0)
        return total

    def column(part, row):
        total = jnp.sum(part * row, axis=1, keepdims=True)
        return jnp.where(cols[: part.shape[0]] == 0, total, 0.0)

    pitch_parts = [
        (block, weights(inflow, variable, 5 * p + node)) for block, p in ((0, 4), (1, 0))
    ]
    span_parts = []
    for block, s, sign in ((2, 4, 1.0), (3, 0, -1.0)):
        sent = half_flux(2, sign)[:4] @ inflow
        for c in range(4):
            part = weights(sent[c : c + 1], rows[:5] * 0, 5 * rows[:5] + s)
            span_parts.append((block * BLOCK + c * 25, part))
    for e in range(2):
        row = inlet_row(section, flags, wake, e)
        for block, part in pitch_parts:
            inlets[e][pl.ds(block * BLOCK, 25, stride=5), :] = column(part, row)
        for start, part in span_parts:
            inlets[e][start : start + 5] = column(part, row)

    both = jnp.concatenate([traces[e][...] + inlets[e][...] for e in range(2)], axis=1)
    emit_span_faces(both[2 * BLOCK :], span_odd, next_span_a, next_span_b)
    emit_pitch_faces(
        both[: 2 * BLOCK], [wake[0:1], wake[1:2]], pitch_odd, next_pitch_a, next_pitch_b,
        next_inner,
    )


def last_kernel(
    base, before, near_high, near_low, flags, pitch_b, pitch_a, table, links, rows,
    state, far_high, far_low, partial,
):
    near, far = ((near_high, near_low), (flags, pitch_a, pitch_b))
    add_halo(1, before, near, far, links, state, far_high, far_low)
    advance_body(2, base, state, table, partial, None)
    flat = rows.reshape(rows.shape[0], LANES)
    for e in range(2):
        lanes = slice(e * LANES, (e + 1) * LANES)
        for v in range(5):
            start = var_start(v)
            first = v * 250 + e
            for a in range(5):
                at = start + a * MAIN
                flat[pl.ds(first + a * 50, MAIN, stride=2), :] = partial[at : at + MAIN, lanes]
            tail = start + TAIL
            flat[pl.ds(first + 2 * MAIN, 5, stride=50), :] = partial[tail : tail + 5, lanes]


def mixed_faces(faces, s, lanes, direction, sign):
    table = half_flux(direction, sign)
    at = FACE_PAD + s * 25
    rows = lax.broadcasted_iota(jnp.int32, (25, LANES), 0)
    own = faces[at : at + 25, lanes]
    total = float(table[0, 0]) * own
    for i in range(5):
        for j in range(5):
            if i != j and table[i, j] != 0.0:
                moved = faces[at + 5 * (j - i) : at + 5 * (j - i) + 25, lanes]
                here = (rows >= 5 * i) & (rows < 5 * i + 5)
                total = total + jnp.where(here, float(table[i, j]) * moved, 0.0)
    return total


def final_near_kernel(
    span_a, span_b, pitch_a, inner, before, result, after_faces, before_faces
):
    flat = result.reshape(result.shape[0], LANES)
    flat[...] = before.reshape(before.shape[0], LANES)[...]
    pitch_odd, span_odd = parities()
    gain = GAIN[2]

    def add(start, stride, values):
        at = pl.ds(start, values.shape[0], stride=stride)
        flat[at, :] = flat[at, :] + values

    place = lax.axis_index("span")
    scale = gain * lift_factor(2)
    up_scale = jnp.where(place == lax.axis_size("span") - 1, 0.0, -scale)
    down_scale = jnp.where(place == 0, 0.0, scale)
    for e in range(2):
        lanes = slice(e * LANES, (e + 1) * LANES)
        for c in range(4):
            at = slice(c * 25, c * 25 + 25)
            first, second = (span_a[at, lanes], span_b[at, lanes])
            above = up_scale * jnp.where(span_odd, second, first)
            below = down_scale * jnp.where(span_odd, first, second)
            add(c * 250 + 8 + e, 10, above)
            add(c * 250 + e, 10, below)
            if c == 3:
                add(4 * 250 + 8 + e, 10, -above)
                add(4 * 250 + e, 10, below)

    at = slice(FACE_PAD, FACE_PAD + BLOCK)
    near = pitch_a[...]
    before_faces[at, :LANES] = jnp.where(pitch_odd, near, 0.0)
    before_faces[at, LANES:] = inner[0:BLOCK]
    after_faces[at, :LANES] = inner[BLOCK:]
    after_faces[at, LANES:] = jnp.where(pitch_odd, 0.0, near)
    scale = gain * lift_factor(1)
    for e in range(2):
        lanes = slice(e * LANES, (e + 1) * LANES)
        for s in range(5):
            add(40 + 2 * s + e, 50, -scale * mixed_faces(after_faces, s, lanes, 1, -1.0))
            add(2 * s + e, 50, scale * mixed_faces(before_faces, s, lanes, 1, 1.0))


def final_kernel(flags, pitch_b, pitch_a, near, out, result, faces, lifted, done):
    copies = []

    def send(origin, part):
        grouped = (5, 5, 50, 1, LANES)
        copy = pltpu.make_async_copy(
            origin.reshape(*grouped).at[part], out.reshape(*grouped).at[part], done.at[len(copies)]
        )
        copy.start()
        copies.append(copy)

    odd = lax.axis_index("pitch") % 2
    every, behind = (pl.ds(0, 5), pl.ds(1, 4))
    send(near, (every, behind, pl.ds(10 - 10 * odd, 40)))
    flat = result.reshape(result.shape[0], LANES)
    flat[...] = near.reshape(near.shape[0], LANES)[...]
    pitch_odd, _ = parities()
    gain = GAIN[2]

    def add(start, stride, values):
        at = pl.ds(start, values.shape[0], stride=stride)
        flat[at, :] = flat[at, :] + values

    lifted[...] = far_lift(gain, pitch_b, faces)
    for s in range(5):
        values = lifted[s * 25 : s * 25 + 25]
        add(40 + 2 * s + 1, 50, jnp.where(pitch_odd, values, 0.0))
        add(2 * s, 50, jnp.where(pitch_odd, 0.0, values))

    wake = arrived_wake(pitch_a, pitch_b)
    rows = lax.broadcasted_iota(jnp.int32, (25, LANES), 0)
    cols = lax.broadcasted_iota(jnp.int32, (25, LANES), 1)
    for e in range(2):
        row = inlet_row(2, flags, wake, e)
        columns = [
            jnp.sum(jnp.where(cols == rows + 25 * v, row, 0.0), axis=1, keepdims=True)
            for v in range(5)
        ]
        inlet = combine(gain * lift_factor(0) * half_flux(0, 1.0), columns)
        for v in range(5):
            add(v * 250 + e, 2, jnp.where(cols == 0, inlet[v], 0.0))

    send(result, (every, pl.ds(0, 1), pl.ds(0, 50)))
    send(result, (every, behind, pl.ds(40 * odd, 10)))
    for copy in copies:
        copy.wait()


IN_VMEM = pl.BlockSpec(memory_space=pltpu.VMEM)
IN_SMEM = pl.BlockSpec(memory_space=pltpu.SMEM)


def call(kernel, name, outs, args, in_specs=(), scratch=(), flops=0, out_spec=IN_VMEM):
    in_specs = list(in_specs)
    return pl.pallas_call(
        kernel,
        name=name,
        out_shape=[jax.ShapeDtypeStruct(shape, dtype) for shape, dtype in outs],
        in_specs=in_specs + [IN_VMEM] * (len(args) - len(in_specs)),
        out_specs=[out_spec] * len(outs),
        scratch_shapes=list(scratch),
        compiler_params=pltpu.CompilerParams(vmem_limit_bytes=VMEM_LIMIT),
        cost_estimate=pl.CostEstimate(flops=flops, bytes_accessed=2**20, transcendentals=0),
    )(*args)


def swapped(value, axis, odd):
    pitch, span = (lax.axis_size("pitch"), lax.axis_size("span"))
    pairs = []
    for i in range(pitch):
        for j in range(span):
            if axis == "pitch":
                other = ((i + (1 if i % 2 == odd else -1)) % pitch, j)
            else:
                other = (i, j + (1 if j % 2 == odd else -1))
                if not 0 <= other[1] < span:
                    other = (i ^ 1, j)
            pairs.append((i * span + j, other[0] * span + other[1]))
    return lax.ppermute(value, ("pitch", "span"), pairs)


def span_exchanged(faces):
    return swapped(faces[0], "span", 0), swapped(faces[1], "span", 1)


def pitch_exchanged(faces):
    return swapped(faces[1], "pitch", 1), swapped(faces[0], "pitch", 0)


F32 = jnp.float32
PITCH_OUTS = [((BLOCK, LANES), F32), ((BLOCK, LANES), F32), ((2 * BLOCK, LANES), F32)]
SPAN_OUTS = [((SPAN_ROWS, 2 * LANES), F32)] * 2
SMALL_OUT = ((8, LANES), F32)
NEAR_OUTS = [((4 * BLOCK, 2 * LANES), jnp.bfloat16)] * 2
FAR_OUTS = [((2 * BLOCK, 2 * LANES), jnp.bfloat16)] * 2
STATE_OUT = ((ROWS, 2 * LANES), F32)
TRACE_OUT = ((TRACES, 2 * LANES), F32)


def shards(table, links, state, wake_planes, bar_offsets):
    x = state.reshape(-1, 1, LANES)
    wake = wake_planes.transpose(0, 1, 3, 4, 2).reshape(50, 1, 5)
    faces = call(begin_span_kernel, "begin_span", SPAN_OUTS, [x], flops=10**10)
    span = span_exchanged(faces)
    *faces, inner = call(begin_pitch_kernel, "begin_pitch", PITCH_OUTS, [x, wake], flops=10**10)
    pitch = pitch_exchanged(faces)
    base, partial, traces, flags = call(
        first_kernel,
        "first",
        [STATE_OUT, STATE_OUT, TRACE_OUT, SMALL_OUT],
        [bar_offsets, x, table],
        in_specs=[IN_SMEM],
        flops=10**9,
    )
    buffers = [pltpu.VMEM(shape, dtype) for shape, dtype in [STATE_OUT] + FAR_OUTS]
    for section in range(2):
        odd, even = pitch
        near_faces, *near = call(
            functools.partial(near_kernel, section),
            "near",
            [TRACE_OUT] + NEAR_OUTS,
            [*span, even, inner, traces, links],
            flops=10**8,
        )
        next_a, next_b, inner, *faces = call(
            functools.partial(far_kernel, section),
            "far",
            PITCH_OUTS + SPAN_OUTS,
            [flags, odd, even, near_faces],
            scratch=[
                pltpu.VMEM(shape, F32)
                for shape in (
                    *[(TRACES, LANES)] * 4,
                    (BLOCK + 2 * FACE_PAD, LANES),
                    (BLOCK, LANES),
                )
            ],
            flops=10**8,
        )
        span = span_exchanged(faces)
        pitch = pitch_exchanged([next_a, next_b])
        args = [base, partial, *near, flags, odd, even, table, links]
        if section == 0:
            partial, traces = call(
                later_kernel, "later", [STATE_OUT, TRACE_OUT], args, scratch=buffers, flops=10**9
            )
    (rows,) = call(
        last_kernel,
        "last",
        [(x.shape, F32)],
        args,
        scratch=buffers + buffers[:1],
        flops=10**9,
    )
    odd, even = pitch
    (near,) = call(
        final_near_kernel,
        "final_near",
        [(x.shape, F32)],
        [*span, even, inner, rows],
        scratch=[pltpu.VMEM((BLOCK + 2 * FACE_PAD, 2 * LANES), F32)] * 2,
        flops=10**8,
    )
    (out,) = call(
        final_kernel,
        "final",
        [(x.shape, F32)],
        [flags, odd, even, near],
        scratch=[
            pltpu.VMEM(x.shape, F32),
            pltpu.VMEM((BLOCK + 2 * FACE_PAD, LANES), F32),
            pltpu.VMEM((BLOCK, LANES), F32),
            pltpu.SemaphoreType.DMA((3,)),
        ],
        flops=10**8,
        out_spec=pl.BlockSpec(memory_space=pl.ANY),
    )
    return out.reshape(state.shape)


def solution(mesh):
    volume, lift, trace, link = operator_tables()
    high, low = split_table(volume)
    table = np.concatenate([exact_table(trace), high, low])
    reached = [
        v * PER_VAR + r for v in range(5) for r in (*range(MAIN), *range(TAIL, PER_VAR))
    ]
    inlet = np.zeros((5 * INLET_ROWS, HALO))
    inlet[:, :BLOCK] = lift[reached, 4 * BLOCK :]
    lift[reached, 4 * BLOCK :] = 0.0
    assert not lift[:, 4 * BLOCK :].any()
    links = np.concatenate([exact_table(t) for t in (link, lift, inlet)])
    in_specs = (
        P(None, None, None, None, "pitch", "span", None),
        P(None, None, None, "pitch", "span"),
        P(),
    )
    out_specs = P(None, None, None, None, "pitch", "span", None)
    return jax.shard_map(
        functools.partial(shards, jnp.asarray(table), jnp.asarray(links)),
        mesh=mesh,
        in_specs=in_specs,
        out_specs=out_specs,
        check_vma=False,
    )
```

```python
import functools

import jax
import jax.numpy as jnp
import ml_dtypes
import numpy as np
from jax import lax
from jax.experimental import pallas as pl
from jax.experimental.pallas import tpu as pltpu
from jax.sharding import PartitionSpec as P

MEAN_FLOW = (0.5, 0.3, 0.0)
WAVE_SPEED = (1.5, 1.3, 1.0)
ELEM_SIZE = (1.0, 0.8, 1.2)
END_WEIGHT = 0.1
TIME_STEP = 0.01
KEEP = (0.0, 0.75, 1.0 / 3.0)
GAIN = (1.0, 0.25, 2.0 / 3.0)

ORDER = (1, 4, 2, 3, 0)
MAIN = 24
TAIL = 5 * MAIN
PER_VAR = 128
ROWS = 5 * PER_VAR
INLET_ROWS = 32
TILES = ((0, 0, 2), (1, 2, 4), (4, 4, 5))
BLOCK = 128
SPAN_ROWS = 104
TRACES = 4 * BLOCK
HALO = 5 * BLOCK
WAKE_ROW = 125
FACE_PAD = 16
HIGH_AT = TRACES
LOW_AT = HIGH_AT + ROWS
LIFT_AT = TRACES
INLET_AT = LIFT_AT + ROWS
LANES = 128
VMEM_LIMIT = 24 * 1024 * 1024


def derivative_table():
    points = np.array([-1.0, -np.sqrt(3.0 / 7.0), 0.0, np.sqrt(3.0 / 7.0), 1.0])
    products = np.array(
        [np.prod([points[j] - points[k] for k in range(5) if k != j]) for j in range(5)]
    )
    matrix = np.zeros((5, 5))
    for i in range(5):
        for j in range(5):
            if i != j:
                matrix[i, j] = products[i] / (products[j] * (points[i] - points[j]))
        matrix[i, i] = sum((1.0 / (points[i] - points[k]) for k in range(5) if k != i))
    return matrix


def flux_matrix(direction):
    flux = MEAN_FLOW[direction] * np.eye(5)
    flux[0, 1 + direction] += 1.0
    flux[4, 1 + direction] += 1.0
    flux[1 + direction, 4] += 1.0
    return flux


def half_flux(direction, sign):
    return 0.5 * (flux_matrix(direction) + sign * WAVE_SPEED[direction] * np.eye(5))


def lift_factor(direction):
    return TIME_STEP * 2.0 / (ELEM_SIZE[direction] * END_WEIGHT)


def half_scales():
    return (lift_factor(1) / 10.0, lift_factor(1), lift_factor(2), lift_factor(2), lift_factor(0))


def var_start(v):
    return ORDER.index(v) * PER_VAR


def node_row(v, a, p, s):
    node = p * 5 + s
    return var_start(v) + (a * MAIN + node if node < MAIN else TAIL + a)


def operator_tables():
    deriv = derivative_table()
    volume = np.zeros((ROWS, ROWS))
    lift = np.zeros((ROWS, HALO))
    trace = np.zeros((TRACES, ROWS))
    fluxes = [flux_matrix(d) for d in range(3)]
    plus = [half_flux(d, 1.0) for d in range(3)]
    minus = [half_flux(d, -1.0) for d in range(3)]
    plus_sent, minus_sent = (plus[2][:4], minus[2][:4])
    back_plus = np.vstack([np.eye(4), [[0.0, 0.0, 0.0, 1.0]]])
    back_minus = np.vstack([np.eye(4), [[0.0, 0.0, 0.0, -1.0]]])
    assert np.allclose(back_plus @ plus_sent, plus[2])
    assert np.allclose(back_minus @ minus_sent, minus[2])
    for a in range(5):
        for p in range(5):
            for s in range(5):
                here = [node_row(v, a, p, s) for v in range(5)]
                place = (a, p, s)
                for d in range(3):
                    for j in range(5):
                        there = list(place)
                        there[d] = j
                        cols = [node_row(v, *there) for v in range(5)]
                        coeff = -TIME_STEP * (2.0 / ELEM_SIZE[d]) * deriv[place[d], j]
                        volume[np.ix_(here, cols)] += coeff * fluxes[d]
                for d in (1, 2):
                    if place[d] == 4:
                        volume[np.ix_(here, here)] += lift_factor(d) * minus[d]
                    if place[d] == 0:
                        volume[np.ix_(here, here)] -= lift_factor(d) * plus[d]
                if p == 0:
                    cols = [s * 25 + v * 5 + a for v in range(5)]
                    lift[np.ix_(here, cols)] += lift_factor(1) * plus[1]
                    for v in range(5):
                        trace[BLOCK + s * 25 + v * 5 + a, here[v]] = 1.0
                if p == 4:
                    cols = [BLOCK + s * 25 + v * 5 + a for v in range(5)]
                    lift[np.ix_(here, cols)] -= lift_factor(1) * minus[1]
                    for v in range(5):
                        trace[s * 25 + v * 5 + a, here[v]] = 1.0
                if s == 0:
                    cols = [2 * BLOCK + c * 25 + a * 5 + p for c in range(4)]
                    lift[np.ix_(here, cols)] += lift_factor(2) * back_plus
                    rows = [3 * BLOCK + c * 25 + a * 5 + p for c in range(4)]
                    trace[np.ix_(rows, here)] += minus_sent
                if s == 4:
                    cols = [3 * BLOCK + c * 25 + a * 5 + p for c in range(4)]
                    lift[np.ix_(here, cols)] -= lift_factor(2) * back_minus
                    rows = [2 * BLOCK + c * 25 + a * 5 + p for c in range(4)]
                    trace[np.ix_(rows, here)] += plus_sent
                if a == 0:
                    cols = [4 * BLOCK + v * 25 + p * 5 + s for v in range(5)]
                    lift[np.ix_(here, cols)] += lift_factor(0) * plus[0]
    lift = lift / np.repeat(half_scales(), BLOCK)
    return volume, lift, trace, trace @ lift


def exact_table(table):
    exact = table.astype(ml_dtypes.bfloat16)
    assert np.allclose(exact.astype(np.float64), table, rtol=1e-12, atol=1e-12)
    return exact


def split_table(table):
    high = table.astype(ml_dtypes.bfloat16)
    low = (table - high.astype(np.float64)).astype(ml_dtypes.bfloat16)
    return high, low


def split(values):
    high = values.astype(jnp.bfloat16)
    low = (values - high.astype(jnp.float32)).astype(jnp.bfloat16)
    return high, low


def dot(left, right):
    return jnp.dot(left, right, preferred_element_type=jnp.float32)


def product(table, high, low):
    return dot(table, high) + dot(table, low)


def with_rows(values, first, extra):
    rows = lax.broadcasted_iota(jnp.int32, values.shape, 0)
    for k, row in enumerate(extra):
        values = jnp.where(rows == first + k, row, values)
    return values


def emit_pitch_faces(traces, wake, pitch_odd, pitch_a, pitch_b, inner):
    upper, lower = traces[0:BLOCK], traces[BLOCK : 2 * BLOCK]
    up = with_rows(upper[:, LANES:], WAKE_ROW, wake)
    down = lower[:, :LANES]
    pitch_a[...] = jnp.where(pitch_odd, down, up)
    pitch_b[...] = jnp.where(pitch_odd, up, down)
    inner[0:BLOCK] = upper[:, :LANES]
    inner[BLOCK:] = lower[:, LANES:]


def emit_span_faces(traces, span_odd, span_a, span_b):
    above, below = traces[0:SPAN_ROWS], traces[BLOCK : BLOCK + SPAN_ROWS]
    span_a[...] = jnp.where(span_odd, below, above)
    span_b[...] = jnp.where(span_odd, above, below)


def parities():
    return lax.axis_index("pitch") % 2 == 1, lax.axis_index("span") % 2 == 1


def combine(table, values):
    return [
        sum(float(table[i, j]) * values[j] for j in range(5) if table[i, j] != 0.0)
        for i in range(table.shape[0])
    ]


def begin_span_kernel(x, span_a, span_b):
    flat = x.reshape(x.shape[0], LANES)
    _, span_odd = parities()
    rest = jnp.zeros((SPAN_ROWS - 96, LANES), jnp.float32)
    for e in range(2):
        lanes = slice(e * LANES, (e + 1) * LANES)
        sides = []
        for s, sign in ((4, 1.0), (0, -1.0)):
            faces = [flat[pl.ds(v * 250 + 2 * s + e, 25, stride=10), :] for v in range(5)]
            sides.append(combine(half_flux(2, sign)[:4], faces))
        span_a[96:SPAN_ROWS, lanes] = rest
        span_b[96:SPAN_ROWS, lanes] = rest
        for c in range(4):
            above, below = (sides[0][c], sides[1][c])
            span_a[c * 25 : c * 25 + 25, lanes] = jnp.where(span_odd, below, above)
            span_b[c * 25 : c * 25 + 25, lanes] = jnp.where(span_odd, above, below)


def begin_pitch_kernel(x, wake, pitch_a, pitch_b, inner):
    flat = x.reshape(x.shape[0], LANES)
    pitch_odd, _ = parities()
    planes = wake.reshape(50, 5)[...]
    rows = lax.broadcasted_iota(jnp.int32, (50, LANES), 0)
    cols = lax.broadcasted_iota(jnp.int32, (50, LANES), 1)
    spread = jnp.zeros((50, LANES), jnp.float32)
    for s in range(5):
        mine = (cols - s) == 5 * (rows // 2)
        spread = jnp.where(mine, planes[:, s : s + 1], spread)
    own = [
        jnp.sum(jnp.where(rows % 2 == k, spread, 0.0), axis=0, keepdims=True) for k in range(2)
    ]
    tail = jnp.zeros((8, LANES), jnp.float32)
    up_tail = with_rows(tail, WAKE_ROW - 120, own)
    pitch_a[120:BLOCK] = jnp.where(pitch_odd, tail, up_tail)
    pitch_b[120:BLOCK] = jnp.where(pitch_odd, up_tail, tail)
    inner[120:BLOCK] = tail
    inner[BLOCK + 120 :] = tail
    for s in range(5):
        at = slice(s * 25, s * 25 + 25)
        upper, lower = (
            [flat[pl.ds(p * 10 + 2 * s + e, 25, stride=50), :] for e in range(2)] for p in (4, 0)
        )
        pitch_a[at] = jnp.where(pitch_odd, lower[0], upper[1])
        pitch_b[at] = jnp.where(pitch_odd, upper[1], lower[0])
        inner[at] = upper[0]
        inner[BLOCK + s * 25 : BLOCK + s * 25 + 25] = lower[1]


def load_state(x, state):
    flat = x.reshape(x.shape[0], LANES)
    for e in range(2):
        lanes = slice(e * LANES, (e + 1) * LANES)
        for v in range(5):
            base = var_start(v)
            first = v * 250 + e
            for a in range(5):
                at = base + a * MAIN
                state[at : at + MAIN, lanes] = flat[pl.ds(first + a * 50, MAIN, stride=2), :]
            tail = base + TAIL
            state[tail : tail + 8, lanes] = jnp.zeros((8, LANES), jnp.float32)
            state[tail : tail + 5, lanes] = flat[pl.ds(first + 2 * MAIN, 5, stride=50), :]


def add_axial_terms(gain, state, partial):
    lanes = lax.broadcasted_iota(jnp.int32, (MAIN + 8, LANES), 1)
    rows = lax.broadcasted_iota(jnp.int32, (8, LANES), 0)
    for e in range(2):
        own = slice(e * LANES, (e + 1) * LANES)
        upper_gap, lower_gap = ([], [])
        for v in range(5):
            base = var_start(v)
            lower = state[base : base + MAIN, own]
            upper = state[base + 4 * MAIN : base + TAIL, own]
            tail = state[base + TAIL : base + PER_VAR, own]
            turned = pltpu.roll(tail, 4, 0)
            join = lambda main, end: jnp.concatenate([main, end], axis=0)
            after = pltpu.roll(join(lower, turned), LANES - 1, 1)
            before = pltpu.roll(join(upper, turned), 1, 1)
            upper = join(upper, tail)
            upper_gap.append(jnp.where(lanes == LANES - 1, 0.0, upper - after))
            lower_gap.append(jnp.where(lanes == 0, 0.0, before) - join(lower, tail))
        mixed = []
        for gap, sign in ((upper_gap, -1.0), (lower_gap, 1.0)):
            mixed.append(combine(gain * lift_factor(0) * half_flux(0, sign), gap))
        for v in range(5):
            base = var_start(v)
            upper, lower = (mixed[0][v], mixed[1][v])
            partial[base : base + MAIN, own] += lower[:MAIN]
            partial[base + 4 * MAIN : base + TAIL, own] += upper[:MAIN]
            ends = jnp.where(rows == 0, lower[MAIN:], jnp.where(rows == 4, upper[MAIN:], 0.0))
            partial[base + TAIL : base + PER_VAR, own] += ends


def volume_rate(table, high, low):
    rate = [None] * 5
    for first, start, stop in TILES:
        part = slice(start * PER_VAR, stop * PER_VAR)
        table_high, table_low = (
            table[at + first * PER_VAR : at + ROWS, part] for at in (HIGH_AT, LOW_AT)
        )
        term = product(table_high, high[part], low[part]) + dot(table_low, high[part])
        for v in range(first, 5):
            block = term[(v - first) * PER_VAR : (v - first + 1) * PER_VAR]
            rate[v] = block if rate[v] is None else rate[v] + block
    return jnp.concatenate(rate, axis=0)


def phase(run):
    pl.when(lax.axis_index("span") >= 0)(run)


def advance_body(section, base, state, table, partial, faces):
    gain, keep = GAIN[section], KEEP[section]

    @phase
    def _():
        rate = volume_rate(table, *split(state[...]))
        if keep == 0.0:
            partial[...] = state[...] + rate
        else:
            partial[...] = keep * base[...] + gain * (state[...] + rate)

    @phase
    def _():
        add_axial_terms(gain, state, partial)

    if faces is not None:
        faces[...] = product(table[0:TRACES], *split(partial[...]))


def add_halo(section, before, near, far, links, state, far_high, far_low):
    gain = GAIN[section]
    gather_far(section, *far, far_high, far_low)
    side = pl.multiple_of(lax.axis_index("pitch") % 2 * BLOCK, BLOCK)
    rows = slice(LIFT_AT, LIFT_AT + ROWS)
    near_high, near_low = near
    state[...] = before[...] + gain * (
        product(links[rows, : 4 * BLOCK], near_high[...], near_low[...])
        + product(links[rows, pl.ds(side, BLOCK)], far_high[0:BLOCK], far_low[0:BLOCK])
    )
    added = gain * product(
        links[INLET_AT : INLET_AT + 5 * INLET_ROWS, 0:BLOCK], far_high[BLOCK:], far_low[BLOCK:]
    )
    for k in range(5):
        start, at = (k * PER_VAR, k * INLET_ROWS)
        state[start : start + MAIN] += added[at : at + MAIN]
        state[start + TAIL : start + PER_VAR] += added[at + MAIN : at + INLET_ROWS]


def first_kernel(offsets, x, table, base, partial, faces, flags):
    cols = lax.broadcasted_iota(jnp.int32, flags.shape, 1)
    moved = jnp.zeros(flags.shape, jnp.float32)
    for k in range(3):
        moved = jnp.where((cols == k) & (offsets[k] % 2 == 1), 1.0, moved)
    flags[...] = moved
    load_state(x, base)
    advance_body(0, None, base, table, partial, faces)


def later_kernel(
    base, before, near_high, near_low, flags, pitch_b, pitch_a, table, links, partial, faces,
    state, far_high, far_low,
):
    near, far = ((near_high, near_low), (flags, pitch_a, pitch_b))
    add_halo(0, before, near, far, links, state, far_high, far_low)
    advance_body(1, base, state, table, partial, faces)


def put_halo(halo_high, halo_low, block, first, scale, values):
    at = (slice(block * BLOCK, (block + 1) * BLOCK), slice(first, first + values.shape[1]))
    halo_high[at], halo_low[at] = split(scale * values)


def gather_near(pitch_a, span_a, span_b, inner, halo_high, halo_low):
    put = functools.partial(put_halo, halo_high, halo_low)
    scales = half_scales()
    pitch_odd, span_odd = parities()
    near = pitch_a[...]
    put(0, 0, scales[0], jnp.where(pitch_odd, near, 0.0))
    put(0, LANES, scales[0], inner[0:BLOCK])
    put(1, 0, scales[1], inner[BLOCK:])
    put(1, LANES, scales[1], jnp.where(pitch_odd, 0.0, near))
    above = jnp.where(span_odd, span_b[...], span_a[...])
    below = jnp.where(span_odd, span_a[...], span_b[...])
    place = lax.axis_index("span")
    above = jnp.where(place == lax.axis_size("span") - 1, 0.0, above)
    below = jnp.where(place == 0, 0.0, below)
    rest = jnp.zeros((BLOCK - SPAN_ROWS, 2 * LANES), jnp.float32)
    put(2, 0, scales[2], jnp.concatenate([below, rest], axis=0))
    put(3, 0, scales[3], jnp.concatenate([above, rest], axis=0))


def arrived_wake(pitch_a, pitch_b):
    pitch_odd, _ = parities()
    rows = slice(WAKE_ROW, WAKE_ROW + 2)
    return jnp.where(pitch_odd, pitch_a[rows], pitch_b[rows])


def inlet_row(section, flags, wake, e):
    moved = flags[0:1, section : section + 1] > 0.5
    return jnp.where(moved, wake[1 - e : 2 - e], wake[e : e + 1])


def gather_far(section, flags, pitch_a, pitch_b, halo_high, halo_low):
    put = functools.partial(put_halo, halo_high, halo_low)
    scales = half_scales()
    pitch_odd, _ = parities()
    far = jnp.where(pitch_odd, scales[1], scales[0]) * pitch_b[...]
    put(0, 0, 1.0, jnp.where(pitch_odd, 0.0, far))
    put(0, LANES, 1.0, jnp.where(pitch_odd, far, 0.0))
    wake = arrived_wake(pitch_a, pitch_b)
    rows = lax.broadcasted_iota(jnp.int32, (BLOCK, LANES), 0)
    cols = lax.broadcasted_iota(jnp.int32, (BLOCK, LANES), 1)
    for e in range(2):
        row = inlet_row(section, flags, wake, e)
        column = jnp.sum(jnp.where(rows == cols, row, 0.0), axis=1, keepdims=True)
        put(1, e * LANES, scales[4], jnp.where(cols == 0, column, 0.0))


def near_kernel(
    section, span_a, span_b, pitch_a, inner, faces, links, near_faces, halo_high, halo_low
):
    gather_near(pitch_a, span_a, span_b, inner, halo_high, halo_low)
    for half in range(2):
        at = slice(half * 2 * BLOCK, (half + 1) * 2 * BLOCK)
        near_faces[at] = faces[at] + GAIN[section] * dot(
            links[at, : 4 * BLOCK], halo_high[...]
        )


def weights(table, choice, cols, lane):
    total = jnp.zeros(choice.shape, jnp.float32)
    for v in range(5):
        values = [float(table[i, v]) for i in range(table.shape[0])]
        if any(values):
            factor = sum(
                jnp.where(choice == i, value, 0.0) for i, value in enumerate(values) if value
            )
            total = total + jnp.where(cols == 25 * v + lane, factor, 0.0)
    return total


def inlet_column(part, row):
    cols = lax.broadcasted_iota(jnp.int32, part.shape, 1)
    return jnp.where(cols == 0, jnp.sum(part * row, axis=1, keepdims=True), 0.0)


def far_lift(gain, pitch_b, faces):
    pitch_odd, _ = parities()
    faces[FACE_PAD : FACE_PAD + BLOCK] = pitch_b[...]
    plus, minus = (half_flux(1, 1.0), half_flux(1, -1.0))
    scale = gain * lift_factor(1)
    assert np.allclose(plus - np.diag(np.diag(plus)), minus - np.diag(np.diag(minus)))
    factor = lambda i, j: jnp.where(
        pitch_odd, -scale * float(minus[i, j]), scale * float(plus[i, j])
    )
    rows = lax.broadcasted_iota(jnp.int32, (BLOCK, LANES), 0)
    place = rows - 25 * sum((rows >= 25 * s).astype(jnp.int32) for s in range(1, 5))
    total = factor(0, 0) * pitch_b[...]
    for i in range(5):
        for j in range(5):
            if i != j and plus[i, j] != 0.0:
                at = FACE_PAD + 5 * (j - i)
                here = (place >= 5 * i) & (place < 5 * i + 5)
                total = total + jnp.where(here, factor(i, j) * faces[at : at + BLOCK], 0.0)
    return jnp.where(rows < WAKE_ROW, total, 0.0)


def far_kernel(
    section, flags, pitch_b, pitch_a, near_faces,
    next_pitch_a, next_pitch_b, next_inner, next_span_a, next_span_b, *refs
):
    *buffers, faces, lifted = refs
    traces, inlets = (buffers[:2], buffers[2:])
    pitch_odd, span_odd = parities()
    gain = GAIN[section]
    for e in range(2):
        traces[e][...] = near_faces[:, e * LANES : (e + 1) * LANES]
        inlets[e][...] = jnp.zeros((TRACES, LANES), jnp.float32)

    def add(start, count, stride, e, values):
        at = pl.ds(start, count, stride=stride) if stride > 1 else pl.ds(start, count)
        traces[e][at, :] = traces[e][at, :] + values

    total = far_lift(gain, pitch_b, faces)
    lifted[...] = total
    add(0, BLOCK, 1, 1, jnp.where(pitch_odd, total, 0.0))
    add(BLOCK, BLOCK, 1, 0, jnp.where(pitch_odd, 0.0, total))
    for block, s, sign in ((2, 4, 1.0), (3, 0, -1.0)):
        edge = [lifted[s * 25 + 5 * v : s * 25 + 5 * v + 5] for v in range(5)]
        for c, values in enumerate(combine(half_flux(2, sign)[:4], edge)):
            start = block * BLOCK + c * 25
            add(start + 4, 5, 5, 1, jnp.where(pitch_odd, values, 0.0))
            add(start, 5, 5, 0, jnp.where(pitch_odd, 0.0, values))

    wake = arrived_wake(pitch_a, pitch_b)
    rows = lax.broadcasted_iota(jnp.int32, (25, LANES), 0)
    cols = lax.broadcasted_iota(jnp.int32, (25, LANES), 1)
    node = sum((rows >= 5 * k).astype(jnp.int32) for k in range(1, 5))
    variable = rows - 5 * node
    inflow = gain * lift_factor(0) * half_flux(0, 1.0)

    pitch_parts = [
        (block, weights(inflow, variable, cols, 5 * p + node)) for block, p in ((0, 4), (1, 0))
    ]
    span_parts = []
    for block, s, sign in ((2, 4, 1.0), (3, 0, -1.0)):
        sent = half_flux(2, sign)[:4] @ inflow
        for c in range(4):
            part = weights(sent[c : c + 1], rows[:5] * 0, cols[:5], 5 * rows[:5] + s)
            span_parts.append((block * BLOCK + c * 25, part))
    for e in range(2):
        row = inlet_row(section, flags, wake, e)
        for block, part in pitch_parts:
            inlets[e][pl.ds(block * BLOCK, 25, stride=5), :] = inlet_column(part, row)
        for start, part in span_parts:
            inlets[e][start : start + 5] = inlet_column(part, row)

    both = jnp.concatenate([traces[e][...] + inlets[e][...] for e in range(2)], axis=1)
    emit_span_faces(both[2 * BLOCK :], span_odd, next_span_a, next_span_b)
    emit_pitch_faces(
        both[: 2 * BLOCK], [wake[0:1], wake[1:2]], pitch_odd, next_pitch_a, next_pitch_b,
        next_inner,
    )


def last_kernel(
    base, before, near_high, near_low, flags, pitch_b, pitch_a, table, links, rows,
    state, far_high, far_low, partial,
):
    near, far = ((near_high, near_low), (flags, pitch_a, pitch_b))
    add_halo(1, before, near, far, links, state, far_high, far_low)
    advance_body(2, base, state, table, partial, None)
    flat = rows.reshape(rows.shape[0], LANES)
    for e in range(2):
        lanes = slice(e * LANES, (e + 1) * LANES)
        for v in range(5):
            start = var_start(v)
            first = v * 250 + e
            for a in range(5):
                at = start + a * MAIN
                flat[pl.ds(first + a * 50, MAIN, stride=2), :] = partial[at : at + MAIN, lanes]
            tail = start + TAIL
            flat[pl.ds(first + 2 * MAIN, 5, stride=50), :] = partial[tail : tail + 5, lanes]


def mixed_faces(faces, s, lanes, direction, sign):
    table = half_flux(direction, sign)
    at = FACE_PAD + s * 25
    rows = lax.broadcasted_iota(jnp.int32, (25, LANES), 0)
    own = faces[at : at + 25, lanes]
    total = float(table[0, 0]) * own
    for i in range(5):
        for j in range(5):
            if i != j and table[i, j] != 0.0:
                moved = faces[at + 5 * (j - i) : at + 5 * (j - i) + 25, lanes]
                here = (rows >= 5 * i) & (rows < 5 * i + 5)
                total = total + jnp.where(here, float(table[i, j]) * moved, 0.0)
    return total


def final_near_kernel(
    span_a, span_b, pitch_a, inner, before, result, after_faces, before_faces
):
    flat = result.reshape(result.shape[0], LANES)
    flat[...] = before.reshape(before.shape[0], LANES)[...]
    pitch_odd, span_odd = parities()
    gain = GAIN[2]

    def add(start, stride, values):
        at = pl.ds(start, values.shape[0], stride=stride)
        flat[at, :] = flat[at, :] + values

    place = lax.axis_index("span")
    scale = gain * lift_factor(2)
    up_scale = jnp.where(place == lax.axis_size("span") - 1, 0.0, -scale)
    down_scale = jnp.where(place == 0, 0.0, scale)
    for e in range(2):
        lanes = slice(e * LANES, (e + 1) * LANES)
        for c in range(4):
            at = slice(c * 25, c * 25 + 25)
            first, second = (span_a[at, lanes], span_b[at, lanes])
            above = up_scale * jnp.where(span_odd, second, first)
            below = down_scale * jnp.where(span_odd, first, second)
            add(c * 250 + 8 + e, 10, above)
            add(c * 250 + e, 10, below)
            if c == 3:
                add(4 * 250 + 8 + e, 10, -above)
                add(4 * 250 + e, 10, below)

    at = slice(FACE_PAD, FACE_PAD + BLOCK)
    near = pitch_a[...]
    before_faces[at, :LANES] = jnp.where(pitch_odd, near, 0.0)
    before_faces[at, LANES:] = inner[0:BLOCK]
    after_faces[at, :LANES] = inner[BLOCK:]
    after_faces[at, LANES:] = jnp.where(pitch_odd, 0.0, near)
    scale = gain * lift_factor(1)
    for e in range(2):
        lanes = slice(e * LANES, (e + 1) * LANES)
        for s in range(5):
            add(40 + 2 * s + e, 50, -scale * mixed_faces(after_faces, s, lanes, 1, -1.0))
            add(2 * s + e, 50, scale * mixed_faces(before_faces, s, lanes, 1, 1.0))


def final_kernel(flags, pitch_b, pitch_a, near, out, result, faces, lifted, done):
    copies = []

    def send(origin, part):
        grouped = (5, 5, 50, 1, LANES)
        copy = pltpu.make_async_copy(
            origin.reshape(*grouped).at[part], out.reshape(*grouped).at[part], done.at[len(copies)]
        )
        copy.start()
        copies.append(copy)

    odd = lax.axis_index("pitch") % 2
    every, behind = (pl.ds(0, 5), pl.ds(1, 4))
    send(near, (every, behind, pl.ds(10 - 10 * odd, 40)))
    source = near.reshape(near.shape[0], LANES)
    flat = result.reshape(result.shape[0], LANES)
    flat[...] = source[...]
    pitch_odd, _ = parities()
    gain = GAIN[2]

    lifted[...] = far_lift(gain, pitch_b, faces)
    for s in range(5):
        values = lifted[s * 25 : s * 25 + 25]
        for start, own in ((40 + 2 * s + 1, True), (2 * s, False)):
            at = pl.ds(start, 25, stride=50)
            added = jnp.where(pitch_odd, values, 0.0) if own else jnp.where(pitch_odd, 0.0, values)
            flat[at, :] = source[at, :] + added

    wake = arrived_wake(pitch_a, pitch_b)
    rows = lax.broadcasted_iota(jnp.int32, (25, LANES), 0)
    cols = lax.broadcasted_iota(jnp.int32, (25, LANES), 1)
    inflow = gain * lift_factor(0) * half_flux(0, 1.0)
    parts = [weights(inflow[v : v + 1], rows * 0, cols, rows) for v in range(5)]
    for e in range(2):
        row = inlet_row(2, flags, wake, e)
        for v in range(5):
            at = pl.ds(v * 250 + e, 25, stride=2)
            flat[at, :] = flat[at, :] + inlet_column(parts[v], row)

    send(result, (every, pl.ds(0, 1), pl.ds(0, 50)))
    send(result, (every, behind, pl.ds(40 * odd, 10)))
    for copy in copies:
        copy.wait()


IN_VMEM = pl.BlockSpec(memory_space=pltpu.VMEM)
IN_SMEM = pl.BlockSpec(memory_space=pltpu.SMEM)


def call(kernel, name, outs, args, in_specs=(), scratch=(), flops=0, out_spec=IN_VMEM):
    in_specs = list(in_specs)
    return pl.pallas_call(
        kernel,
        name=name,
        out_shape=[jax.ShapeDtypeStruct(shape, dtype) for shape, dtype in outs],
        in_specs=in_specs + [IN_VMEM] * (len(args) - len(in_specs)),
        out_specs=[out_spec] * len(outs),
        scratch_shapes=list(scratch),
        compiler_params=pltpu.CompilerParams(vmem_limit_bytes=VMEM_LIMIT),
        cost_estimate=pl.CostEstimate(flops=flops, bytes_accessed=2**20, transcendentals=0),
    )(*args)


def swapped(value, axis, odd):
    pitch, span = (lax.axis_size("pitch"), lax.axis_size("span"))
    pairs = []
    for i in range(pitch):
        for j in range(span):
            if axis == "pitch":
                other = ((i + (1 if i % 2 == odd else -1)) % pitch, j)
            else:
                other = (i, j + (1 if j % 2 == odd else -1))
                if not 0 <= other[1] < span:
                    other = (i ^ 1, j)
            pairs.append((i * span + j, other[0] * span + other[1]))
    return lax.ppermute(value, ("pitch", "span"), pairs)


def span_exchanged(faces):
    return swapped(faces[0], "span", 0), swapped(faces[1], "span", 1)


def pitch_exchanged(faces):
    return swapped(faces[1], "pitch", 1), swapped(faces[0], "pitch", 0)


F32 = jnp.float32
PITCH_OUTS = [((BLOCK, LANES), F32), ((BLOCK, LANES), F32), ((2 * BLOCK, LANES), F32)]
SPAN_OUTS = [((SPAN_ROWS, 2 * LANES), F32)] * 2
SMALL_OUT = ((8, LANES), F32)
NEAR_OUTS = [((4 * BLOCK, 2 * LANES), jnp.bfloat16)] * 2
FAR_OUTS = [((2 * BLOCK, 2 * LANES), jnp.bfloat16)] * 2
STATE_OUT = ((ROWS, 2 * LANES), F32)
TRACE_OUT = ((TRACES, 2 * LANES), F32)


def shards(table, links, state, wake_planes, bar_offsets):
    x = state.reshape(-1, 1, LANES)
    wake = wake_planes.transpose(0, 1, 3, 4, 2).reshape(50, 1, 5)
    faces = call(begin_span_kernel, "begin_span", SPAN_OUTS, [x], flops=10**10)
    span = span_exchanged(faces)
    *faces, inner = call(begin_pitch_kernel, "begin_pitch", PITCH_OUTS, [x, wake], flops=10**10)
    pitch = pitch_exchanged(faces)
    base, partial, traces, flags = call(
        first_kernel,
        "first",
        [STATE_OUT, STATE_OUT, TRACE_OUT, SMALL_OUT],
        [bar_offsets, x, table],
        in_specs=[IN_SMEM],
        flops=10**9,
    )
    buffers = [pltpu.VMEM(shape, dtype) for shape, dtype in [STATE_OUT] + FAR_OUTS]
    for section in range(2):
        odd, even = pitch
        near_faces, *near = call(
            functools.partial(near_kernel, section),
            "near",
            [TRACE_OUT] + NEAR_OUTS,
            [*span, even, inner, traces, links],
            flops=10**8,
        )
        next_a, next_b, inner, *faces = call(
            functools.partial(far_kernel, section),
            "far",
            PITCH_OUTS + SPAN_OUTS,
            [flags, odd, even, near_faces],
            scratch=[
                pltpu.VMEM(shape, F32)
                for shape in (
                    *[(TRACES, LANES)] * 4,
                    (BLOCK + 2 * FACE_PAD, LANES),
                    (BLOCK, LANES),
                )
            ],
            flops=10**8,
        )
        span = span_exchanged(faces)
        pitch = pitch_exchanged([next_a, next_b])
        args = [base, partial, *near, flags, odd, even, table, links]
        if section == 0:
            partial, traces = call(
                later_kernel, "later", [STATE_OUT, TRACE_OUT], args, scratch=buffers, flops=10**9
            )
    (rows,) = call(
        last_kernel,
        "last",
        [(x.shape, F32)],
        args,
        scratch=buffers + buffers[:1],
        flops=10**9,
    )
    odd, even = pitch
    (near,) = call(
        final_near_kernel,
        "final_near",
        [(x.shape, F32)],
        [*span, even, inner, rows],
        scratch=[pltpu.VMEM((BLOCK + 2 * FACE_PAD, 2 * LANES), F32)] * 2,
        flops=10**8,
    )
    (out,) = call(
        final_kernel,
        "final",
        [(x.shape, F32)],
        [flags, odd, even, near],
        scratch=[
            pltpu.VMEM(x.shape, F32),
            pltpu.VMEM((BLOCK + 2 * FACE_PAD, LANES), F32),
            pltpu.VMEM((BLOCK, LANES), F32),
            pltpu.SemaphoreType.DMA((3,)),
        ],
        flops=10**8,
        out_spec=pl.BlockSpec(memory_space=pl.ANY),
    )
    return out.reshape(state.shape)


def solution(mesh):
    volume, lift, trace, link = operator_tables()
    high, low = split_table(volume)
    table = np.concatenate([exact_table(trace), high, low])
    reached = [
        v * PER_VAR + r for v in range(5) for r in (*range(MAIN), *range(TAIL, PER_VAR))
    ]
    inlet = np.zeros((5 * INLET_ROWS, HALO))
    inlet[:, :BLOCK] = lift[reached, 4 * BLOCK :]
    lift[reached, 4 * BLOCK :] = 0.0
    assert not lift[:, 4 * BLOCK :].any()
    links = np.concatenate([exact_table(t) for t in (link, lift, inlet)])
    in_specs = (
        P(None, None, None, None, "pitch", "span", None),
        P(None, None, None, "pitch", "span"),
        P(),
    )
    out_specs = P(None, None, None, None, "pitch", "span", None)
    return jax.shard_map(
        functools.partial(shards, jnp.asarray(table), jnp.asarray(links)),
        mesh=mesh,
        in_specs=in_specs,
        out_specs=out_specs,
        check_vma=False,
    )
```

```python
import functools

import jax
import jax.numpy as jnp
import ml_dtypes
import numpy as np
from jax import lax
from jax.experimental import pallas as pl
from jax.experimental.pallas import tpu as pltpu
from jax.sharding import PartitionSpec as P

MEAN_FLOW = (0.5, 0.3, 0.0)
WAVE_SPEED = (1.5, 1.3, 1.0)
ELEM_SIZE = (1.0, 0.8, 1.2)
END_WEIGHT = 0.1
TIME_STEP = 0.01
KEEP = (0.0, 0.75, 1.0 / 3.0)
GAIN = (1.0, 0.25, 2.0 / 3.0)

ORDER = (1, 4, 2, 3, 0)
MAIN = 24
TAIL = 5 * MAIN
PER_VAR = 128
ROWS = 5 * PER_VAR
INLET_ROWS = 32
TILES = ((0, 0, 2), (1, 2, 4), (4, 4, 5))
BLOCK = 128
SPAN_ROWS = 104
TRACES = 4 * BLOCK
HALO = 5 * BLOCK
WAKE_ROW = 125
FACE_PAD = 16
HIGH_AT = TRACES
LOW_AT = HIGH_AT + ROWS
LIFT_AT = TRACES
INLET_AT = LIFT_AT + ROWS
LANES = 128
VMEM_LIMIT = 8 * 1024 * 1024


def derivative_table():
    points = np.array([-1.0, -np.sqrt(3.0 / 7.0), 0.0, np.sqrt(3.0 / 7.0), 1.0])
    products = np.array(
        [np.prod([points[j] - points[k] for k in range(5) if k != j]) for j in range(5)]
    )
    matrix = np.zeros((5, 5))
    for i in range(5):
        for j in range(5):
            if i != j:
                matrix[i, j] = products[i] / (products[j] * (points[i] - points[j]))
        matrix[i, i] = sum((1.0 / (points[i] - points[k]) for k in range(5) if k != i))
    return matrix


def flux_matrix(direction):
    flux = MEAN_FLOW[direction] * np.eye(5)
    flux[0, 1 + direction] += 1.0
    flux[4, 1 + direction] += 1.0
    flux[1 + direction, 4] += 1.0
    return flux


def half_flux(direction, sign):
    return 0.5 * (flux_matrix(direction) + sign * WAVE_SPEED[direction] * np.eye(5))


def lift_factor(direction):
    return TIME_STEP * 2.0 / (ELEM_SIZE[direction] * END_WEIGHT)


def half_scales():
    return (lift_factor(1) / 10.0, lift_factor(1), lift_factor(2), lift_factor(2), lift_factor(0))


def var_start(v):
    return ORDER.index(v) * PER_VAR


def node_row(v, a, p, s):
    node = p * 5 + s
    return var_start(v) + (a * MAIN + node if node < MAIN else TAIL + a)


def operator_tables():
    deriv = derivative_table()
    volume = np.zeros((ROWS, ROWS))
    lift = np.zeros((ROWS, HALO))
    trace = np.zeros((TRACES, ROWS))
    fluxes = [flux_matrix(d) for d in range(3)]
    plus = [half_flux(d, 1.0) for d in range(3)]
    minus = [half_flux(d, -1.0) for d in range(3)]
    plus_sent, minus_sent = (plus[2][:4], minus[2][:4])
    back_plus = np.vstack([np.eye(4), [[0.0, 0.0, 0.0, 1.0]]])
    back_minus = np.vstack([np.eye(4), [[0.0, 0.0, 0.0, -1.0]]])
    assert np.allclose(back_plus @ plus_sent, plus[2])
    assert np.allclose(back_minus @ minus_sent, minus[2])
    for a in range(5):
        for p in range(5):
            for s in range(5):
                here = [node_row(v, a, p, s) for v in range(5)]
                place = (a, p, s)
                for d in range(3):
                    for j in range(5):
                        there = list(place)
                        there[d] = j
                        cols = [node_row(v, *there) for v in range(5)]
                        coeff = -TIME_STEP * (2.0 / ELEM_SIZE[d]) * deriv[place[d], j]
                        volume[np.ix_(here, cols)] += coeff * fluxes[d]
                for d in (1, 2):
                    if place[d] == 4:
                        volume[np.ix_(here, here)] += lift_factor(d) * minus[d]
                    if place[d] == 0:
                        volume[np.ix_(here, here)] -= lift_factor(d) * plus[d]
                if p == 0:
                    cols = [s * 25 + v * 5 + a for v in range(5)]
                    lift[np.ix_(here, cols)] += lift_factor(1) * plus[1]
                    for v in range(5):
                        trace[BLOCK + s * 25 + v * 5 + a, here[v]] = 1.0
                if p == 4:
                    cols = [BLOCK + s * 25 + v * 5 + a for v in range(5)]
                    lift[np.ix_(here, cols)] -= lift_factor(1) * minus[1]
                    for v in range(5):
                        trace[s * 25 + v * 5 + a, here[v]] = 1.0
                if s == 0:
                    cols = [2 * BLOCK + c * 25 + a * 5 + p for c in range(4)]
                    lift[np.ix_(here, cols)] += lift_factor(2) * back_plus
                    rows = [3 * BLOCK + c * 25 + a * 5 + p for c in range(4)]
                    trace[np.ix_(rows, here)] += minus_sent
                if s == 4:
                    cols = [3 * BLOCK + c * 25 + a * 5 + p for c in range(4)]
                    lift[np.ix_(here, cols)] -= lift_factor(2) * back_minus
                    rows = [2 * BLOCK + c * 25 + a * 5 + p for c in range(4)]
                    trace[np.ix_(rows, here)] += plus_sent
                if a == 0:
                    cols = [4 * BLOCK + v * 25 + p * 5 + s for v in range(5)]
                    lift[np.ix_(here, cols)] += lift_factor(0) * plus[0]
    lift = lift / np.repeat(half_scales(), BLOCK)
    return volume, lift, trace, trace @ lift


def exact_table(table):
    exact = table.astype(ml_dtypes.bfloat16)
    assert np.allclose(exact.astype(np.float64), table, rtol=1e-12, atol=1e-12)
    return exact


def split_table(table):
    high = table.astype(ml_dtypes.bfloat16)
    low = (table - high.astype(np.float64)).astype(ml_dtypes.bfloat16)
    return high, low


def split(values):
    high = values.astype(jnp.bfloat16)
    low = (values - high.astype(jnp.float32)).astype(jnp.bfloat16)
    return high, low


def dot(left, right):
    return jnp.dot(left, right, preferred_element_type=jnp.float32)


def product(table, high, low):
    return dot(table, high) + dot(table, low)


def with_rows(values, first, extra):
    rows = lax.broadcasted_iota(jnp.int32, values.shape, 0)
    for k, row in enumerate(extra):
        values = jnp.where(rows == first + k, row, values)
    return values


def emit_pitch_faces(traces, wake, pitch_odd, pitch_a, pitch_b, inner):
    upper, lower = traces[0:BLOCK], traces[BLOCK : 2 * BLOCK]
    up = with_rows(upper[:, LANES:], WAKE_ROW, wake)
    down = lower[:, :LANES]
    pitch_a[...] = jnp.where(pitch_odd, down, up)
    pitch_b[...] = jnp.where(pitch_odd, up, down)
    inner[0:BLOCK] = upper[:, :LANES]
    inner[BLOCK:] = lower[:, LANES:]


def emit_span_faces(traces, span_odd, span_a, span_b):
    above, below = traces[0:SPAN_ROWS], traces[BLOCK : BLOCK + SPAN_ROWS]
    span_a[...] = jnp.where(span_odd, below, above)
    span_b[...] = jnp.where(span_odd, above, below)


def parities():
    return lax.axis_index("pitch") % 2 == 1, lax.axis_index("span") % 2 == 1


def combine(table, values):
    return [
        sum(float(table[i, j]) * values[j] for j in range(5) if table[i, j] != 0.0)
        for i in range(table.shape[0])
    ]


def begin_span_kernel(x, span_a, span_b):
    flat = x.reshape(x.shape[0], LANES)
    _, span_odd = parities()
    rest = jnp.zeros((SPAN_ROWS - 96, LANES), jnp.float32)
    for e in range(2):
        lanes = slice(e * LANES, (e + 1) * LANES)
        sides = []
        for s, sign in ((4, 1.0), (0, -1.0)):
            faces = [flat[pl.ds(v * 250 + 2 * s + e, 25, stride=10), :] for v in range(5)]
            sides.append(combine(half_flux(2, sign)[:4], faces))
        span_a[96:SPAN_ROWS, lanes] = rest
        span_b[96:SPAN_ROWS, lanes] = rest
        for c in range(4):
            above, below = (sides[0][c], sides[1][c])
            span_a[c * 25 : c * 25 + 25, lanes] = jnp.where(span_odd, below, above)
            span_b[c * 25 : c * 25 + 25, lanes] = jnp.where(span_odd, above, below)


def begin_pitch_kernel(x, wake, pitch_a, pitch_b, inner):
    flat = x.reshape(x.shape[0], LANES)
    pitch_odd, _ = parities()
    planes = wake.reshape(50, 5)[...]
    rows = lax.broadcasted_iota(jnp.int32, (50, LANES), 0)
    cols = lax.broadcasted_iota(jnp.int32, (50, LANES), 1)
    spread = jnp.zeros((50, LANES), jnp.float32)
    for s in range(5):
        mine = (cols - s) == 5 * (rows // 2)
        spread = jnp.where(mine, planes[:, s : s + 1], spread)
    own = [
        jnp.sum(jnp.where(rows % 2 == k, spread, 0.0), axis=0, keepdims=True) for k in range(2)
    ]
    tail = jnp.zeros((8, LANES), jnp.float32)
    up_tail = with_rows(tail, WAKE_ROW - 120, own)
    pitch_a[120:BLOCK] = jnp.where(pitch_odd, tail, up_tail)
    pitch_b[120:BLOCK] = jnp.where(pitch_odd, up_tail, tail)
    inner[120:BLOCK] = tail
    inner[BLOCK + 120 :] = tail
    for s in range(5):
        at = slice(s * 25, s * 25 + 25)
        upper, lower = (
            [flat[pl.ds(p * 10 + 2 * s + e, 25, stride=50), :] for e in range(2)] for p in (4, 0)
        )
        pitch_a[at] = jnp.where(pitch_odd, lower[0], upper[1])
        pitch_b[at] = jnp.where(pitch_odd, upper[1], lower[0])
        inner[at] = upper[0]
        inner[BLOCK + s * 25 : BLOCK + s * 25 + 25] = lower[1]


def load_state(x, state):
    flat = x.reshape(x.shape[0], LANES)
    for e in range(2):
        lanes = slice(e * LANES, (e + 1) * LANES)
        for v in range(5):
            base = var_start(v)
            first = v * 250 + e
            for a in range(5):
                at = base + a * MAIN
                state[at : at + MAIN, lanes] = flat[pl.ds(first + a * 50, MAIN, stride=2), :]
            tail = base + TAIL
            state[tail : tail + 8, lanes] = jnp.zeros((8, LANES), jnp.float32)
            state[tail : tail + 5, lanes] = flat[pl.ds(first + 2 * MAIN, 5, stride=50), :]


def add_axial_terms(gain, state, partial):
    lanes = lax.broadcasted_iota(jnp.int32, (MAIN + 8, LANES), 1)
    rows = lax.broadcasted_iota(jnp.int32, (8, LANES), 0)
    for e in range(2):
        own = slice(e * LANES, (e + 1) * LANES)
        upper_gap, lower_gap = ([], [])
        for v in range(5):
            base = var_start(v)
            lower = state[base : base + MAIN, own]
            upper = state[base + 4 * MAIN : base + TAIL, own]
            tail = state[base + TAIL : base + PER_VAR, own]
            turned = pltpu.roll(tail, 4, 0)
            join = lambda main, end: jnp.concatenate([main, end], axis=0)
            after = pltpu.roll(join(lower, turned), LANES - 1, 1)
            before = pltpu.roll(join(upper, turned), 1, 1)
            upper = join(upper, tail)
            upper_gap.append(jnp.where(lanes == LANES - 1, 0.0, upper - after))
            lower_gap.append(jnp.where(lanes == 0, 0.0, before) - join(lower, tail))
        mixed = []
        for gap, sign in ((upper_gap, -1.0), (lower_gap, 1.0)):
            mixed.append(combine(gain * lift_factor(0) * half_flux(0, sign), gap))
        for v in range(5):
            base = var_start(v)
            upper, lower = (mixed[0][v], mixed[1][v])
            partial[base : base + MAIN, own] += lower[:MAIN]
            partial[base + 4 * MAIN : base + TAIL, own] += upper[:MAIN]
            ends = jnp.where(rows == 0, lower[MAIN:], jnp.where(rows == 4, upper[MAIN:], 0.0))
            partial[base + TAIL : base + PER_VAR, own] += ends


def volume_rate(table, high, low):
    rate = [None] * 5
    for first, start, stop in TILES:
        part = slice(start * PER_VAR, stop * PER_VAR)
        table_high, table_low = (
            table[at + first * PER_VAR : at + ROWS, part] for at in (HIGH_AT, LOW_AT)
        )
        term = product(table_high, high[part], low[part]) + dot(table_low, high[part])
        for v in range(first, 5):
            block = term[(v - first) * PER_VAR : (v - first + 1) * PER_VAR]
            rate[v] = block if rate[v] is None else rate[v] + block
    return jnp.concatenate(rate, axis=0)


def phase(run):
    pl.when(lax.axis_index("span") >= 0)(run)


def advance_body(section, base, state, table, partial, faces):
    gain, keep = GAIN[section], KEEP[section]

    @phase
    def _():
        rate = volume_rate(table, *split(state[...]))
        if keep == 0.0:
            partial[...] = state[...] + rate
        else:
            partial[...] = keep * base[...] + gain * (state[...] + rate)

    @phase
    def _():
        add_axial_terms(gain, state, partial)

    if faces is not None:
        faces[...] = product(table[0:TRACES], *split(partial[...]))


def add_halo(section, before, near, far, links, state, far_high, far_low):
    gain = GAIN[section]
    gather_far(section, *far, far_high, far_low)
    side = pl.multiple_of(lax.axis_index("pitch") % 2 * BLOCK, BLOCK)
    rows = slice(LIFT_AT, LIFT_AT + ROWS)
    near_high, near_low = near
    state[...] = before[...] + gain * (
        product(links[rows, : 4 * BLOCK], near_high[...], near_low[...])
        + product(links[rows, pl.ds(side, BLOCK)], far_high[0:BLOCK], far_low[0:BLOCK])
    )
    added = gain * product(
        links[INLET_AT : INLET_AT + 5 * INLET_ROWS, 0:BLOCK], far_high[BLOCK:], far_low[BLOCK:]
    )
    for k in range(5):
        start, at = (k * PER_VAR, k * INLET_ROWS)
        state[start : start + MAIN] += added[at : at + MAIN]
        state[start + TAIL : start + PER_VAR] += added[at + MAIN : at + INLET_ROWS]


def first_kernel(offsets, x, table, base, partial, faces, flags):
    cols = lax.broadcasted_iota(jnp.int32, flags.shape, 1)
    moved = jnp.zeros(flags.shape, jnp.float32)
    for k in range(3):
        moved = jnp.where((cols == k) & (offsets[k] % 2 == 1), 1.0, moved)
    flags[...] = moved
    load_state(x, base)
    advance_body(0, None, base, table, partial, faces)


def later_kernel(
    base, before, near_high, near_low, flags, pitch_b, pitch_a, table, links, partial, faces,
    state, far_high, far_low,
):
    near, far = ((near_high, near_low), (flags, pitch_a, pitch_b))
    add_halo(0, before, near, far, links, state, far_high, far_low)
    advance_body(1, base, state, table, partial, faces)


def put_halo(halo_high, halo_low, block, first, scale, values):
    at = (slice(block * BLOCK, (block + 1) * BLOCK), slice(first, first + values.shape[1]))
    halo_high[at], halo_low[at] = split(scale * values)


def gather_near(pitch_a, span_a, span_b, inner, halo_high, halo_low):
    put = functools.partial(put_halo, halo_high, halo_low)
    scales = half_scales()
    pitch_odd, span_odd = parities()
    near = pitch_a[...]
    put(0, 0, scales[0], jnp.where(pitch_odd, near, 0.0))
    put(0, LANES, scales[0], inner[0:BLOCK])
    put(1, 0, scales[1], inner[BLOCK:])
    put(1, LANES, scales[1], jnp.where(pitch_odd, 0.0, near))
    above = jnp.where(span_odd, span_b[...], span_a[...])
    below = jnp.where(span_odd, span_a[...], span_b[...])
    place = lax.axis_index("span")
    above = jnp.where(place == lax.axis_size("span") - 1, 0.0, above)
    below = jnp.where(place == 0, 0.0, below)
    rest = jnp.zeros((BLOCK - SPAN_ROWS, 2 * LANES), jnp.float32)
    put(2, 0, scales[2], jnp.concatenate([below, rest], axis=0))
    put(3, 0, scales[3], jnp.concatenate([above, rest], axis=0))


def arrived_wake(pitch_a, pitch_b):
    pitch_odd, _ = parities()
    rows = slice(WAKE_ROW, WAKE_ROW + 2)
    return jnp.where(pitch_odd, pitch_a[rows], pitch_b[rows])


def inlet_row(section, flags, wake, e):
    moved = flags[0:1, section : section + 1] > 0.5
    return jnp.where(moved, wake[1 - e : 2 - e], wake[e : e + 1])


def gather_far(section, flags, pitch_a, pitch_b, halo_high, halo_low):
    put = functools.partial(put_halo, halo_high, halo_low)
    scales = half_scales()
    pitch_odd, _ = parities()
    far = jnp.where(pitch_odd, scales[1], scales[0]) * pitch_b[...]
    put(0, 0, 1.0, jnp.where(pitch_odd, 0.0, far))
    put(0, LANES, 1.0, jnp.where(pitch_odd, far, 0.0))
    wake = arrived_wake(pitch_a, pitch_b)
    rows = lax.broadcasted_iota(jnp.int32, (BLOCK, LANES), 0)
    cols = lax.broadcasted_iota(jnp.int32, (BLOCK, LANES), 1)
    for e in range(2):
        row = inlet_row(section, flags, wake, e)
        column = jnp.sum(jnp.where(rows == cols, row, 0.0), axis=1, keepdims=True)
        put(1, e * LANES, scales[4], jnp.where(cols == 0, column, 0.0))


def near_kernel(
    section, span_a, span_b, pitch_a, inner, faces, links, near_faces, halo_high, halo_low
):
    gather_near(pitch_a, span_a, span_b, inner, halo_high, halo_low)
    for half in range(2):
        at = slice(half * 2 * BLOCK, (half + 1) * 2 * BLOCK)
        near_faces[at] = faces[at] + GAIN[section] * dot(
            links[at, : 4 * BLOCK], halo_high[...]
        )


def weights(table, choice, cols, lane):
    total = jnp.zeros(choice.shape, jnp.float32)
    for v in range(5):
        values = [float(table[i, v]) for i in range(table.shape[0])]
        if any(values):
            factor = sum(
                jnp.where(choice == i, value, 0.0) for i, value in enumerate(values) if value
            )
            total = total + jnp.where(cols == 25 * v + lane, factor, 0.0)
    return total


def inlet_column(part, row):
    cols = lax.broadcasted_iota(jnp.int32, part.shape, 1)
    return jnp.where(cols == 0, jnp.sum(part * row, axis=1, keepdims=True), 0.0)


def far_lift(gain, pitch_b, faces):
    pitch_odd, _ = parities()
    faces[FACE_PAD : FACE_PAD + BLOCK] = pitch_b[...]
    plus, minus = (half_flux(1, 1.0), half_flux(1, -1.0))
    scale = gain * lift_factor(1)
    assert np.allclose(plus - np.diag(np.diag(plus)), minus - np.diag(np.diag(minus)))
    factor = lambda i, j: jnp.where(
        pitch_odd, -scale * float(minus[i, j]), scale * float(plus[i, j])
    )
    rows = lax.broadcasted_iota(jnp.int32, (BLOCK, LANES), 0)
    place = rows - 25 * sum((rows >= 25 * s).astype(jnp.int32) for s in range(1, 5))
    total = factor(0, 0) * pitch_b[...]
    for i in range(5):
        for j in range(5):
            if i != j and plus[i, j] != 0.0:
                at = FACE_PAD + 5 * (j - i)
                here = (place >= 5 * i) & (place < 5 * i + 5)
                total = total + jnp.where(here, factor(i, j) * faces[at : at + BLOCK], 0.0)
    return jnp.where(rows < WAKE_ROW, total, 0.0)


def far_kernel(
    section, flags, pitch_b, pitch_a, near_faces,
    next_pitch_a, next_pitch_b, next_inner, next_span_a, next_span_b, *refs
):
    *buffers, faces, lifted = refs
    traces, inlets = (buffers[:2], buffers[2:])
    pitch_odd, span_odd = parities()
    gain = GAIN[section]
    for e in range(2):
        traces[e][...] = near_faces[:, e * LANES : (e + 1) * LANES]
        inlets[e][...] = jnp.zeros((TRACES, LANES), jnp.float32)

    def add(start, count, stride, e, values):
        at = pl.ds(start, count, stride=stride) if stride > 1 else pl.ds(start, count)
        traces[e][at, :] = traces[e][at, :] + values

    total = far_lift(gain, pitch_b, faces)
    lifted[...] = total
    add(0, BLOCK, 1, 1, jnp.where(pitch_odd, total, 0.0))
    add(BLOCK, BLOCK, 1, 0, jnp.where(pitch_odd, 0.0, total))
    for block, s, sign in ((2, 4, 1.0), (3, 0, -1.0)):
        edge = [lifted[s * 25 + 5 * v : s * 25 + 5 * v + 5] for v in range(5)]
        for c, values in enumerate(combine(half_flux(2, sign)[:4], edge)):
            start = block * BLOCK + c * 25
            add(start + 4, 5, 5, 1, jnp.where(pitch_odd, values, 0.0))
            add(start, 5, 5, 0, jnp.where(pitch_odd, 0.0, values))

    wake = arrived_wake(pitch_a, pitch_b)
    rows = lax.broadcasted_iota(jnp.int32, (25, LANES), 0)
    cols = lax.broadcasted_iota(jnp.int32, (25, LANES), 1)
    node = sum((rows >= 5 * k).astype(jnp.int32) for k in range(1, 5))
    variable = rows - 5 * node
    inflow = gain * lift_factor(0) * half_flux(0, 1.0)

    pitch_parts = [
        (block, weights(inflow, variable, cols, 5 * p + node)) for block, p in ((0, 4), (1, 0))
    ]
    span_parts = []
    for block, s, sign in ((2, 4, 1.0), (3, 0, -1.0)):
        sent = half_flux(2, sign)[:4] @ inflow
        for c in range(4):
            part = weights(sent[c : c + 1], rows[:5] * 0, cols[:5], 5 * rows[:5] + s)
            span_parts.append((block * BLOCK + c * 25, part))
    for e in range(2):
        row = inlet_row(section, flags, wake, e)
        for block, part in pitch_parts:
            inlets[e][pl.ds(block * BLOCK, 25, stride=5), :] = inlet_column(part, row)
        for start, part in span_parts:
            inlets[e][start : start + 5] = inlet_column(part, row)

    both = jnp.concatenate([traces[e][...] + inlets[e][...] for e in range(2)], axis=1)
    emit_span_faces(both[2 * BLOCK :], span_odd, next_span_a, next_span_b)
    emit_pitch_faces(
        both[: 2 * BLOCK], [wake[0:1], wake[1:2]], pitch_odd, next_pitch_a, next_pitch_b,
        next_inner,
    )


def last_kernel(
    base, before, near_high, near_low, flags, pitch_b, pitch_a, table, links, rows,
    state, far_high, far_low, partial,
):
    near, far = ((near_high, near_low), (flags, pitch_a, pitch_b))
    add_halo(1, before, near, far, links, state, far_high, far_low)
    advance_body(2, base, state, table, partial, None)
    flat = rows.reshape(rows.shape[0], LANES)
    for e in range(2):
        lanes = slice(e * LANES, (e + 1) * LANES)
        for v in range(5):
            start = var_start(v)
            first = v * 250 + e
            for a in range(5):
                at = start + a * MAIN
                flat[pl.ds(first + a * 50, MAIN, stride=2), :] = partial[at : at + MAIN, lanes]
            tail = start + TAIL
            flat[pl.ds(first + 2 * MAIN, 5, stride=50), :] = partial[tail : tail + 5, lanes]


def mixed_faces(faces, s, lanes, direction, sign):
    table = half_flux(direction, sign)
    at = FACE_PAD + s * 25
    rows = lax.broadcasted_iota(jnp.int32, (25, LANES), 0)
    own = faces[at : at + 25, lanes]
    total = float(table[0, 0]) * own
    for i in range(5):
        for j in range(5):
            if i != j and table[i, j] != 0.0:
                moved = faces[at + 5 * (j - i) : at + 5 * (j - i) + 25, lanes]
                here = (rows >= 5 * i) & (rows < 5 * i + 5)
                total = total + jnp.where(here, float(table[i, j]) * moved, 0.0)
    return total


def final_near_kernel(
    span_a, span_b, pitch_a, inner, before, result, after_faces, before_faces
):
    flat = result.reshape(result.shape[0], LANES)
    flat[...] = before.reshape(before.shape[0], LANES)[...]
    pitch_odd, span_odd = parities()
    gain = GAIN[2]

    def add(start, stride, values):
        at = pl.ds(start, values.shape[0], stride=stride)
        flat[at, :] = flat[at, :] + values

    place = lax.axis_index("span")
    scale = gain * lift_factor(2)
    up_scale = jnp.where(place == lax.axis_size("span") - 1, 0.0, -scale)
    down_scale = jnp.where(place == 0, 0.0, scale)
    for e in range(2):
        lanes = slice(e * LANES, (e + 1) * LANES)
        for c in range(4):
            at = slice(c * 25, c * 25 + 25)
            first, second = (span_a[at, lanes], span_b[at, lanes])
            above = up_scale * jnp.where(span_odd, second, first)
            below = down_scale * jnp.where(span_odd, first, second)
            add(c * 250 + 8 + e, 10, above)
            add(c * 250 + e, 10, below)
            if c == 3:
                add(4 * 250 + 8 + e, 10, -above)
                add(4 * 250 + e, 10, below)

    at = slice(FACE_PAD, FACE_PAD + BLOCK)
    near = pitch_a[...]
    before_faces[at, :LANES] = jnp.where(pitch_odd, near, 0.0)
    before_faces[at, LANES:] = inner[0:BLOCK]
    after_faces[at, :LANES] = inner[BLOCK:]
    after_faces[at, LANES:] = jnp.where(pitch_odd, 0.0, near)
    scale = gain * lift_factor(1)
    for e in range(2):
        lanes = slice(e * LANES, (e + 1) * LANES)
        for s in range(5):
            add(40 + 2 * s + e, 50, -scale * mixed_faces(after_faces, s, lanes, 1, -1.0))
            add(2 * s + e, 50, scale * mixed_faces(before_faces, s, lanes, 1, 1.0))


def final_kernel(flags, pitch_b, pitch_a, near, out, result, faces, lifted, done):
    copies = []

    def send(origin, part):
        grouped = (5, 5, 50, 1, LANES)
        copy = pltpu.make_async_copy(
            origin.reshape(*grouped).at[part], out.reshape(*grouped).at[part], done.at[len(copies)]
        )
        copy.start()
        copies.append(copy)

    odd = lax.axis_index("pitch") % 2
    every, behind = (pl.ds(0, 5), pl.ds(1, 4))
    send(near, (every, behind, pl.ds(10 - 10 * odd, 40)))
    source = near.reshape(near.shape[0], LANES)
    flat = result.reshape(result.shape[0], LANES)
    flat[...] = source[...]
    pitch_odd, _ = parities()
    gain = GAIN[2]

    lifted[...] = far_lift(gain, pitch_b, faces)
    for s in range(5):
        values = lifted[s * 25 : s * 25 + 25]
        for start, own in ((40 + 2 * s + 1, True), (2 * s, False)):
            at = pl.ds(start, 25, stride=50)
            added = jnp.where(pitch_odd, values, 0.0) if own else jnp.where(pitch_odd, 0.0, values)
            flat[at, :] = source[at, :] + added

    wake = arrived_wake(pitch_a, pitch_b)
    rows = lax.broadcasted_iota(jnp.int32, (25, LANES), 0)
    cols = lax.broadcasted_iota(jnp.int32, (25, LANES), 1)
    inflow = gain * lift_factor(0) * half_flux(0, 1.0)
    parts = [weights(inflow[v : v + 1], rows * 0, cols, rows) for v in range(5)]
    for e in range(2):
        row = inlet_row(2, flags, wake, e)
        for v in range(5):
            at = pl.ds(v * 250 + e, 25, stride=2)
            flat[at, :] = flat[at, :] + inlet_column(parts[v], row)

    send(result, (every, pl.ds(0, 1), pl.ds(0, 50)))
    send(result, (every, behind, pl.ds(40 * odd, 10)))
    for copy in copies:
        copy.wait()


IN_VMEM = pl.BlockSpec(memory_space=pltpu.VMEM)
IN_SMEM = pl.BlockSpec(memory_space=pltpu.SMEM)


def call(kernel, name, outs, args, in_specs=(), scratch=(), flops=0, out_spec=IN_VMEM):
    in_specs = list(in_specs)
    return pl.pallas_call(
        kernel,
        name=name,
        out_shape=[jax.ShapeDtypeStruct(shape, dtype) for shape, dtype in outs],
        in_specs=in_specs + [IN_VMEM] * (len(args) - len(in_specs)),
        out_specs=[out_spec] * len(outs),
        scratch_shapes=list(scratch),
        compiler_params=pltpu.CompilerParams(vmem_limit_bytes=VMEM_LIMIT),
        cost_estimate=pl.CostEstimate(flops=flops, bytes_accessed=2**20, transcendentals=0),
    )(*args)


def swapped(value, axis, odd):
    pitch, span = (lax.axis_size("pitch"), lax.axis_size("span"))
    pairs = []
    for i in range(pitch):
        for j in range(span):
            if axis == "pitch":
                other = ((i + (1 if i % 2 == odd else -1)) % pitch, j)
            else:
                other = (i, j + (1 if j % 2 == odd else -1))
                if not 0 <= other[1] < span:
                    other = (i ^ 1, j)
            pairs.append((i * span + j, other[0] * span + other[1]))
    return lax.ppermute(value, ("pitch", "span"), pairs)


def span_exchanged(faces):
    return swapped(faces[0], "span", 0), swapped(faces[1], "span", 1)


def pitch_exchanged(faces):
    return swapped(faces[1], "pitch", 1), swapped(faces[0], "pitch", 0)


F32 = jnp.float32
PITCH_OUTS = [((BLOCK, LANES), F32), ((BLOCK, LANES), F32), ((2 * BLOCK, LANES), F32)]
SPAN_OUTS = [((SPAN_ROWS, 2 * LANES), F32)] * 2
SMALL_OUT = ((8, LANES), F32)
NEAR_OUTS = [((4 * BLOCK, 2 * LANES), jnp.bfloat16)] * 2
FAR_OUTS = [((2 * BLOCK, 2 * LANES), jnp.bfloat16)] * 2
STATE_OUT = ((ROWS, 2 * LANES), F32)
TRACE_OUT = ((TRACES, 2 * LANES), F32)


def shards(table, links, state, wake_planes, bar_offsets):
    x = state.reshape(-1, 1, LANES)
    wake = wake_planes.transpose(0, 1, 3, 4, 2).reshape(50, 1, 5)
    faces = call(begin_span_kernel, "begin_span", SPAN_OUTS, [x], flops=10**10)
    span = span_exchanged(faces)
    *faces, inner = call(begin_pitch_kernel, "begin_pitch", PITCH_OUTS, [x, wake], flops=10**10)
    pitch = pitch_exchanged(faces)
    base, partial, traces, flags = call(
        first_kernel,
        "first",
        [STATE_OUT, STATE_OUT, TRACE_OUT, SMALL_OUT],
        [bar_offsets, x, table],
        in_specs=[IN_SMEM],
        flops=10**9,
    )
    buffers = [pltpu.VMEM(shape, dtype) for shape, dtype in [STATE_OUT] + FAR_OUTS]
    for section in range(2):
        odd, even = pitch
        near_faces, *near = call(
            functools.partial(near_kernel, section),
            "near",
            [TRACE_OUT] + NEAR_OUTS,
            [*span, even, inner, traces, links],
            flops=10**8,
        )
        next_a, next_b, inner, *faces = call(
            functools.partial(far_kernel, section),
            "far",
            PITCH_OUTS + SPAN_OUTS,
            [flags, odd, even, near_faces],
            scratch=[
                pltpu.VMEM(shape, F32)
                for shape in (
                    *[(TRACES, LANES)] * 4,
                    (BLOCK + 2 * FACE_PAD, LANES),
                    (BLOCK, LANES),
                )
            ],
            flops=10**8,
        )
        span = span_exchanged(faces)
        pitch = pitch_exchanged([next_a, next_b])
        args = [base, partial, *near, flags, odd, even, table, links]
        if section == 0:
            partial, traces = call(
                later_kernel, "later", [STATE_OUT, TRACE_OUT], args, scratch=buffers, flops=10**9
            )
    (rows,) = call(
        last_kernel,
        "last",
        [(x.shape, F32)],
        args,
        scratch=buffers + buffers[:1],
        flops=10**9,
    )
    odd, even = pitch
    (near,) = call(
        final_near_kernel,
        "final_near",
        [(x.shape, F32)],
        [*span, even, inner, rows],
        scratch=[pltpu.VMEM((BLOCK + 2 * FACE_PAD, 2 * LANES), F32)] * 2,
        flops=10**8,
    )
    (out,) = call(
        final_kernel,
        "final",
        [(x.shape, F32)],
        [flags, odd, even, near],
        scratch=[
            pltpu.VMEM(x.shape, F32),
            pltpu.VMEM((BLOCK + 2 * FACE_PAD, LANES), F32),
            pltpu.VMEM((BLOCK, LANES), F32),
            pltpu.SemaphoreType.DMA((3,)),
        ],
        flops=10**8,
        out_spec=pl.BlockSpec(memory_space=pl.ANY),
    )
    return out.reshape(state.shape)


def solution(mesh):
    volume, lift, trace, link = operator_tables()
    high, low = split_table(volume)
    table = np.concatenate([exact_table(trace), high, low])
    reached = [
        v * PER_VAR + r for v in range(5) for r in (*range(MAIN), *range(TAIL, PER_VAR))
    ]
    inlet = np.zeros((5 * INLET_ROWS, HALO))
    inlet[:, :BLOCK] = lift[reached, 4 * BLOCK :]
    lift[reached, 4 * BLOCK :] = 0.0
    assert not lift[:, 4 * BLOCK :].any()
    links = np.concatenate([exact_table(t) for t in (link, lift, inlet)])
    in_specs = (
        P(None, None, None, None, "pitch", "span", None),
        P(None, None, None, "pitch", "span"),
        P(),
    )
    out_specs = P(None, None, None, None, "pitch", "span", None)
    return jax.shard_map(
        functools.partial(shards, jnp.asarray(table), jnp.asarray(links)),
        mesh=mesh,
        in_specs=in_specs,
        out_specs=out_specs,
        check_vma=False,
    )
```
